32 devices in a mesh: gx: 8 (over z, y), gy: 4 (over x, core).
Axes of the slice: x: 2, y: 2, z: 4, core: 2. Of those that a mesh axis runs over, the one named last changes fastest.
Arguments:
- features: bfloat16 [48, 16, 64, 512], P('gy', 'gx'), may hold values from -6 to 6
- conv1_weight: bfloat16 [4608, 512], P(('gx', 'gy')), may hold values from -0.09375 to 0.09375
- conv2_weight: bfloat16 [4608, 512], P(('gx', 'gy')), may hold values from -0.09375 to 0.09375
- norm_gain: bfloat16 [512, 2], P(('gx', 'gy')), may hold values from 0.25 to 1.75
- norm_bias: bfloat16 [512, 2], P(('gx', 'gy')), may hold values from -3 to 3
- head_weight: bfloat16 [512, 40], P(('gx', 'gy')), may hold values from -0.75 to 0.75
- head_bias: bfloat16 [40], replicated, may hold values from -4 to 4
- labels: int32 [48, 40], P('gy'), may hold values 0 or 1
- heights: int32 [48], replicated, may hold values from 8 to 16, as said below
- widths: int32 [48], replicated, may hold values from 32 to 64, as said below
- picks: int32 [20], replicated, may hold values from 0 to 39
Outputs:
- pooled: float32 [48, 512], P('gy')
- features_grad: float32 [48, 16, 64, 512], P('gy', 'gx')
- conv1_grad: float32 [4608, 512], P(('gx', 'gy'))
- conv2_grad: float32 [4608, 512], P(('gx', 'gy'))
- gain_grad: float32 [512, 2], P(('gx', 'gy'))
- bias_grad: float32 [512, 2], P(('gx', 'gy'))
- head_grad: float32 [512, 40], P(('gx', 'gy'))
- head_bias_grad: float32 [40], replicated
The draws below stay inside these ranges and needn't reach their ends.
Inputs may be any that keep to these rules, and one draw needn't show every extreme that they name: `heights`: some image has 16 valid rows. `widths`: some image has 64 valid columns.
All inputs are finite; a program needn't handle non-finite values. No bound on the sum of `labels` on one device may be relied on, other than what follows from the above.
Results may differ from the reference program's by a relative error of at most 0.0085.
Values may be sent and summed in bfloat16 or wider, within the bound.
A program may use at most 192 MiB of HBM per device.

```python
from functools import partial
import jax
import jax.numpy as jnp
from jax import lax

CHANNELS = 512
TASKS = 40
COLUMNS = 64
IMG_DEV = 6
MICRO = 2
STEPS = 20
HEIGHT = 16
IMAGES = 48
N_GY = 4


def draw_heights(key, part):
    key = jax.random.fold_in(key, 11)
    key_vals, key_full = jax.random.split(key)
    values = jax.random.randint(key_vals, (IMAGES,), HEIGHT // 2, HEIGHT + 1)
    chosen = jax.random.randint(key_full, (), 0, IMAGES)
    return jnp.where(jnp.arange(IMAGES) == chosen, HEIGHT, values).astype(jnp.int32)


def draw_widths(key, part):
    key = jax.random.fold_in(key, 23)
    key_vals, key_full = jax.random.split(key)
    values = jax.random.randint(key_vals, (IMAGES,), COLUMNS // 2, COLUMNS + 1)
    chosen = jax.random.randint(key_full, (), 0, IMAGES)
    return jnp.where(jnp.arange(IMAGES) == chosen, COLUMNS, values).astype(jnp.int32)


def touch_ends(values, rng, low, high):
    spot = [jax.random.randint(jax.random.fold_in(rng, axis), (), 0, length) for axis, length in enumerate(values.shape)]
    main_axis = values.shape.index(max(values.shape))
    beside = spot[:main_axis] + [(spot[main_axis] + 1) % values.shape[main_axis]] + spot[main_axis + 1:]
    return values.at[tuple(spot)].set(low).at[tuple(beside)].set(high)


def shard_levels(stream_key, dims, cuts, low, largest):
    gain = 1.0
    for axis_at, blocks in cuts:
        steps = jax.random.uniform(jax.random.fold_in(jax.random.fold_in(stream_key, 6), axis_at), (blocks,), jnp.float32, low / len(cuts), largest / len(cuts))
        gain = gain * jnp.repeat(jnp.exp(steps), dims[axis_at] // blocks).reshape((-1,) + (1,) * (len(dims) - 1 - axis_at))
    return gain


def bell_draw(stream_key, dims, spread, reach, cuts=(), kind=jnp.bfloat16):
    level = shard_levels(stream_key, dims, cuts, -0.22, 0.18) if cuts else 1.0
    values = jax.random.normal(stream_key, dims, jnp.float32) * spread * level
    return jnp.minimum(jnp.maximum(values, -reach), reach).astype(kind)


def setup_inputs(seed: int = 0) -> dict:
    key_list = jax.random.split(jax.random.key(seed), 12)
    return {
        "features": bell_draw(key_list[0], (IMAGES, HEIGHT, COLUMNS, CHANNELS), 1.0, 6.0, ((0, 4), (1, 8))),
        "conv1_weight": bell_draw(key_list[1], (9 * CHANNELS, CHANNELS), (9 * CHANNELS) ** -0.5, 0.09375, ((0, 32),)),
        "conv2_weight": bell_draw(key_list[2], (9 * CHANNELS, CHANNELS), (9 * CHANNELS) ** -0.5, 0.09375, ((0, 32),)),
        "norm_gain": jnp.clip(1.0 + 0.15 * jax.random.normal(key_list[3], (CHANNELS, 2), jnp.float32), 0.25, 1.75).astype(jnp.bfloat16),
        "norm_bias": bell_draw(key_list[4], (CHANNELS, 2), 0.5, 3.0, ((0, 32),)),
        "head_weight": bell_draw(key_list[5], (CHANNELS, TASKS), (CHANNELS // 8) ** -0.5, 0.75, ((0, 32),)),
        "head_bias": bell_draw(key_list[6], (TASKS,), 1.0, 4.0),
        "labels": touch_ends((jax.random.randint(key_list[7], (IMAGES, TASKS), 0, 2) < 1).astype(jnp.int32), jax.random.fold_in(key_list[7], 1), 0, 1),
        "heights": draw_heights(jax.random.fold_in(key_list[11], 71), 0),
        "widths": draw_widths(jax.random.fold_in(key_list[11], 71), 0),
        "picks": touch_ends(jax.random.randint(key_list[10], (STEPS,), 0, TASKS), jax.random.fold_in(key_list[10], 1), 0, TASKS - 1).astype(jnp.int32),
    }


norm_eps = 1e-05

@jax.custom_vjp
def low(v):
    return lax.optimization_barrier(v.astype(jnp.bfloat16)).astype(jnp.float32)

@jax.custom_vjp
def low_back(v):
    return v

def low_keep(v):
    return (low(v), None)

def low_pass(kept, output_gradient):
    return (output_gradient,)

def back_keep(v):
    return (v, None)

def back_low(kept, output_gradient):
    return (low(output_gradient),)
low.defvjp(low_keep, low_pass)
low_back.defvjp(back_keep, back_low)

def conv_full(act, weight):
    padded = jnp.pad(act, ((0, 0), (1, 1), (1, 1), (0, 0)))
    height = act.shape[1]
    width = act.shape[2]
    channels = act.shape[3]
    summed = jnp.zeros(act.shape[:3] + (weight.shape[1],), jnp.float32)
    for row_off in range(3):
        for col_off in range(3):
            tap_index = 3 * row_off + col_off
            summed = summed + jnp.dot(padded[:, row_off:row_off + height, col_off:col_off + width, :], weight[tap_index * channels:(tap_index + 1) * channels], precision=lax.Precision.HIGHEST)
    return summed

def normalize(values, valid, pixel_total, norm_scale_factor, bias):
    center_val = lax.optimization_barrier(jnp.sum(values * valid, axis=(0, 1, 2))) / pixel_total
    centered = values - center_val
    spread_sq = lax.optimization_barrier(jnp.sum(valid * centered * centered, axis=(0, 1, 2))) / pixel_total
    return norm_scale_factor * (centered * lax.rsqrt(spread_sq + norm_eps)) + bias

def valid_mask(heights, widths):
    row_ids = jnp.arange(HEIGHT)
    col_ids = jnp.arange(COLUMNS)
    inner_result = (row_ids[None, :, None] < heights[:, None, None]) & (col_ids[None, None, :] < widths[:, None, None])
    return inner_result.astype(jnp.float32)[..., None]

def block_forward(feats, conv_one, conv_two, scale_factors, bias_values, valid, pixel_count):
    pixel_total = jnp.sum(pixel_count)
    base = feats * valid
    first_convolution = low_back(conv_full(base, conv_one))
    hidden = low(jax.nn.silu(normalize(first_convolution, valid, pixel_total, scale_factors[:, 0], bias_values[:, 0])) * valid)
    second_convolution = low_back(conv_full(hidden, conv_two))
    final_act = jax.nn.silu(normalize(second_convolution, valid, pixel_total, scale_factors[:, 1], bias_values[:, 1]) + base) * valid
    return lax.optimization_barrier(jnp.sum(final_act, axis=(1, 2))) / pixel_count[:, None]

def frank_wolfe(gram, picks):
    task_ids = jnp.arange(TASKS)

    def fw_step(index, task_mix):
        onehot = (task_ids == picks[index]).astype(jnp.float32)
        mixed_vec = jnp.dot(gram, task_mix, precision=lax.Precision.HIGHEST)
        self_dot = jnp.sum(task_mix * mixed_vec)
        cross_dot = jnp.sum(onehot * mixed_vec)
        vertex_dot = jnp.sum(onehot * jnp.dot(gram, onehot, precision=lax.Precision.HIGHEST))
        distance = jnp.maximum(self_dot + vertex_dot - 2.0 * cross_dot, 0.1 * vertex_dot)
        step_size = jnp.clip((self_dot - cross_dot) / distance, 0.0, 1.0)
        return (1.0 - step_size) * task_mix + step_size * onehot
    start = jnp.full((TASKS,), 1.0 / TASKS, jnp.float32)
    return lax.fori_loop(0, STEPS, fw_step, start)

def micro_take(array, index):
    shaped = array.reshape((N_GY, MICRO, IMG_DEV) + array.shape[1:])
    return shaped[:, index].reshape((N_GY * IMG_DEV,) + array.shape[1:])

def micro_join(pieces):
    shaped = [piece.reshape((N_GY, IMG_DEV) + piece.shape[1:]) for piece in pieces]
    stacked = jnp.stack(shaped, 1)
    return stacked.reshape((IMAGES,) + pieces[0].shape[1:])

def reference(features, conv1_weight, conv2_weight, norm_gain, norm_bias, head_weight, head_bias, labels, heights, widths, picks):
    feats = features.astype(jnp.float32)
    conv_one = conv1_weight.astype(jnp.float32)
    conv_two = conv2_weight.astype(jnp.float32)
    scale_factors = norm_gain.astype(jnp.float32)
    bias_values = norm_bias.astype(jnp.float32)
    head_mat = head_weight.astype(jnp.float32)
    head_off = head_bias.astype(jnp.float32)
    valid_all = valid_mask(heights, widths)
    pixel_all = (heights * widths).astype(jnp.float32)
    z_parts = []
    for index in range(MICRO):
        z_parts.append(block_forward(micro_take(feats, index), conv_one, conv_two, scale_factors, bias_values, micro_take(valid_all, index), micro_take(pixel_all, index)))
    pooled = micro_join(z_parts)
    targets = labels.astype(jnp.float32)

    def task_losses(pooled_in, head_in, offset_in):
        logits = jnp.dot(pooled_in, head_in, precision=lax.Precision.HIGHEST) + offset_in
        return lax.optimization_barrier(jnp.mean(jax.nn.softplus(logits) - targets * logits, axis=0))
    losses, pull_back = jax.vjp(task_losses, pooled, head_mat, head_off)
    identity = jnp.eye(TASKS, dtype=jnp.float32)
    task_grads = jax.vmap(lambda row: pull_back(row)[0])(identity)
    gram = jnp.einsum('sic,tic->st', task_grads, task_grads, precision=lax.Precision.HIGHEST)
    unused, head_grad, head_bias_grad = pull_back(jnp.ones((TASKS,), jnp.float32))
    task_mix = frank_wolfe(gram, picks)
    pooled_cot = jnp.einsum('t,tic->ic', task_mix, task_grads, precision=lax.Precision.HIGHEST)
    feat_parts = []
    conv1_grad = jnp.zeros_like(conv_one)
    conv2_grad = jnp.zeros_like(conv_two)
    gain_grad = jnp.zeros_like(scale_factors)
    bias_grad = jnp.zeros_like(bias_values)
    for index in range(MICRO):
        forward_fn = partial(block_forward, valid=micro_take(valid_all, index), pixel_count=micro_take(pixel_all, index))
        unused_z, block_back = jax.vjp(forward_fn, micro_take(feats, index), conv_one, conv_two, scale_factors, bias_values)
        pieces = block_back(micro_take(pooled_cot, index))
        feat_parts.append(pieces[0])
        conv1_grad = conv1_grad + pieces[1]
        conv2_grad = conv2_grad + pieces[2]
        gain_grad = gain_grad + pieces[3]
        bias_grad = bias_grad + pieces[4]
    return (pooled, micro_join(feat_parts), conv1_grad, conv2_grad, gain_grad, bias_grad, head_grad, head_bias_grad)
```

```python
import functools

import jax
import jax.numpy as jnp
from jax import lax
from jax.experimental import pallas as pl
from jax.experimental.pallas import tpu as pltpu
from jax.sharding import PartitionSpec as P

TASKS = 40
MICRO = 2
STEPS = 20
norm_eps = 1e-05
BF = jnp.bfloat16
F32 = jnp.float32
HIGH = lax.Precision.HIGHEST
MESH = pl.DeviceIdType.MESH

C = 512
COLS = 64
PER = 6
ROWS = 4
SHARD = 144
CUT = 80


class Here:
    def __init__(self):
        gx = lax.axis_index("gx")
        gy = lax.axis_index("gy")
        self.z = lax.div(gx, 2)
        self.y = lax.rem(gx, 2)
        self.x = lax.div(gy, 2)
        self.c = lax.rem(gy, 2)
        self.gy = gy

    def _fill(self, z, y, x, c):
        return (
            self.z if z is None else z,
            self.y if y is None else y,
            self.x if x is None else x,
            self.c if c is None else c,
        )

    def dev(self, z=None, y=None, x=None, c=None):
        z, y, x, c = self._fill(z, y, x, c)
        return {"gx": z * 2 + y, "gy": x * 2 + c}

    def idx(self, z=None, y=None, x=None, c=None):
        z, y, x, c = self._fill(z, y, x, c)
        return ((z * 2 + y) * 2 + x) * 2 + c

    def near(self, j):
        z = self.z
        if j == 0:
            return z
        if j == 1:
            return z + 1 - 2 * lax.rem(z, 2)
        if j == 2:
            return 2 - lax.div(z, 2)
        return 3 - 3 * lax.div(z, 2)

    def other(self, dy, dx, dc):
        return (
            1 - self.y if dy else self.y,
            1 - self.x if dx else self.x,
            1 - self.c if dc else self.c,
        )

    def ydev(self):
        return self.dev(y=1 - self.y)

    def xdev(self):
        return self.dev(x=1 - self.x)

    def sib(self):
        return self.dev(c=1 - self.c)


def rcopy(src, dst, ss, rs, dev):
    return pltpu.make_async_remote_copy(
        src_ref=src, dst_ref=dst, send_sem=ss, recv_sem=rs, device_id=dev, device_id_type=MESH
    )


class Gather:
    def __init__(self, h, own, out, ss, rs, lsem, rows, cut, sent):
        self.h, self.own, self.out, self.ss, self.rs = h, own, out, ss, rs
        self.lsem, self.rows, self.cut, self.sent = lsem, rows, cut, sent
        self.split = cut < rows

    def at(self, i, lo=0, n=None):
        n = self.rows if n is None else n
        return self.out.at[pl.ds(pl.multiple_of(i * self.rows + lo, 16), n)]

    def send(self, k, i, dev, lo=0, n=None, src=None, rk=None):
        d = self.at(i, lo, n)
        cp = rcopy(d if src is None else src, d, self.ss.at[k], self.rs.at[k if rk is None else rk], dev)
        cp.start()
        self.sent.append(cp)

    def recv(self, k, i, lo=0, n=None):
        d = self.at(i, lo, n)
        rcopy(d, d, self.ss.at[0], self.rs.at[k], self.h.sib()).wait_recv()

    def start(self):
        h = self.h
        me = h.idx()
        self.local = pltpu.make_async_copy(self.own, self.at(me), self.lsem)
        self.local.start()
        for j in (1, 2, 3):
            self.send(j - 1, me, h.dev(z=h.near(j)), src=self.own, rk=39 + h.z)
        self.fan(0)

    def fan(self, j):
        h = self.h
        i = h.idx(z=h.near(j))
        src = self.own if j == 0 else None
        if j:
            self.recv(39 + h.near(j), i)
        self.send(3 + j, i, h.ydev(), src=src)
        self.send(7 + j, i, h.xdev(), src=src)
        self.send(11 + j, i, h.sib(), src=src)

    def second(self, j):
        h = self.h
        zz = h.near(j)
        i = h.idx(z=zz, y=1 - h.y)
        self.recv(3 + j, i)
        self.send(15 + j, i, h.xdev(), 0, self.cut)
        self.send(19 + j, i, h.sib())
        i = h.idx(z=zz, x=1 - h.x)
        self.recv(7 + j, i)
        if self.split:
            self.send(23 + j, i, h.ydev(), self.cut, self.rows - self.cut)
        self.send(27 + j, i, h.sib())

    def third(self, j):
        h = self.h
        i = h.idx(z=h.near(j), y=1 - h.y, x=1 - h.x)
        self.recv(15 + j, i, 0, self.cut)
        self.send(31 + j, i, h.sib(), 0, self.cut)
        if self.split:
            self.recv(23 + j, i, self.cut, self.rows - self.cut)
            self.send(35 + j, i, h.sib(), self.cut, self.rows - self.cut)

    def steps(self):
        f, s, t = self.fan, self.second, self.third
        order = [(f, 1), (s, 0), (f, 2), (s, 1), (t, 0), (f, 3), (s, 2), (t, 1), (s, 3), (t, 2), (t, 3)]
        return [functools.partial(fn, j) for fn, j in order]

    def finish(self):
        h = self.h
        c = 1 - h.c
        for j in range(4):
            zz = h.near(j)
            self.recv(11 + j, h.idx(z=zz, c=c))
            self.recv(19 + j, h.idx(z=zz, y=1 - h.y, c=c))
            self.recv(27 + j, h.idx(z=zz, x=1 - h.x, c=c))
            i = h.idx(z=zz, y=1 - h.y, x=1 - h.x, c=c)
            self.recv(31 + j, i, 0, self.cut)
            if self.split:
                self.recv(35 + j, i, self.cut, self.rows - self.cut)
        self.local.wait()


class Scatter:
    def __init__(self, h, dw, l1, lxa, lyb, lya, lxb, lz, ss, rs, out, sent):
        self.h, self.dw, self.l1, self.lxa, self.lyb = h, dw, l1, lxa, lyb
        self.lya, self.lxb, self.lz, self.ss, self.rs = lya, lxb, lz, ss, rs
        self.out, self.sent = out, sent

    def at(self, i, lo=0, n=SHARD):
        return self.dw.at[pl.ds(pl.multiple_of(i * SHARD + lo, 16), n)]

    def send(self, k, src, dst, dev):
        cp = rcopy(src, dst, self.ss.at[k], self.rs.at[k], dev)
        cp.start()
        self.sent.append(cp)

    def take(self, k, land, i, lo=0, n=SHARD):
        rcopy(land, land, self.ss.at[0], self.rs.at[k], self.h.sib()).wait_recv()
        d = self.at(i, lo, n)
        d[...] = (d[...].astype(F32) + land[...].astype(F32)).astype(BF)

    def s1(self, q):
        h = self.h
        for j in range(4):
            self.send(4 * q + j, self.at(h.idx(q, j // 2, j % 2, 1 - h.c)), self.l1.at[q, j], h.sib())

    def s2(self, q):
        h = self.h
        for j in range(4):
            self.take(4 * q + j, self.l1.at[q, j], h.idx(q, j // 2, j % 2))
        for j in range(2):
            self.send(16 + 2 * q + j, self.at(h.idx(q, j, 1 - h.x), 0, CUT), self.lxa.at[q, j], h.xdev())
            self.send(24 + 2 * q + j, self.at(h.idx(q, 1 - h.y, j), CUT, SHARD - CUT), self.lyb.at[q, j], h.ydev())

    def s3(self, q):
        h = self.h
        for j in range(2):
            self.take(16 + 2 * q + j, self.lxa.at[q, j], h.idx(q, j), 0, CUT)
            self.take(24 + 2 * q + j, self.lyb.at[q, j], h.idx(q, h.y, j), CUT, SHARD - CUT)
        self.send(32 + q, self.at(h.idx(q, 1 - h.y), 0, CUT), self.lya.at[q], h.ydev())
        self.send(36 + q, self.at(h.idx(q, h.y, 1 - h.x), CUT, SHARD - CUT), self.lxb.at[q], h.xdev())

    def _zcopy(self, q):
        h = self.h
        return rcopy(self.at(h.idx(q)), self.lz.at[h.z], self.ss.at[40 + q], self.rs.at[44 + h.z], h.dev(z=q))

    def s4(self, q):
        h = self.h
        i = h.idx(q)
        self.take(32 + q, self.lya.at[q], i, 0, CUT)
        self.take(36 + q, self.lxb.at[q], i, CUT, SHARD - CUT)

        @pl.when(h.z != q)
        def _():
            self._zcopy(q).start()

    def finish(self, extra):
        h = self.h
        total = self.at(h.idx())[...].astype(F32) + extra
        for j in (1, 2, 3):
            zz = h.near(j)
            land = self.lz.at[zz]
            rcopy(land, land, self.ss.at[0], self.rs.at[44 + zz], h.sib()).wait_recv()
            total = total + land[...].astype(F32)
        self.out[...] = total

    def drain(self):
        h = self.h
        for q in range(4):

            @pl.when(h.z != q)
            def _(q=q):
                self._zcopy(q).wait_send()

    def steps(self):
        p = functools.partial
        return [
            [p(self.s1, 0)],
            [p(self.s2, 0), p(self.s1, 1)],
            [p(self.s3, 0), p(self.s2, 1), p(self.s1, 2)],
            [p(self.s4, 0), p(self.s3, 1), p(self.s2, 2), p(self.s1, 3)],
            [p(self.s4, 1), p(self.s3, 2), p(self.s2, 3)],
            [p(self.s4, 2), p(self.s3, 3)],
            [p(self.s4, 3)],
        ]


class Halo:
    def __init__(self, h, edges, land, ss, rs):
        self.h, self.land, self.ss, self.rs = h, land, ss, rs
        self.up = rcopy(edges.at[0], land.at[1], ss.at[0], rs.at[0], h.dev(z=h.z - 1))
        self.down = rcopy(edges.at[1], land.at[0], ss.at[1], rs.at[1], h.dev(z=h.z + 1))

    def start(self):
        pl.when(self.h.z > 0)(self.up.start)
        pl.when(self.h.z < 3)(self.down.start)

    def wait(self):
        @pl.when(self.h.z > 0)
        def _():
            self.up.wait_send()
            self.down.wait_recv()

        @pl.when(self.h.z < 3)
        def _():
            self.down.wait_send()
            self.up.wait_recv()


class Sums:
    def __init__(self, h, buf, ss, rs, sent):
        self.h, self.buf, self.ss, self.rs, self.sent = h, buf, ss, rs, sent

    def start_plane(self, payload):
        h = self.h
        self.own = payload
        mine = self.buf.at[2, 0]
        mine[...] = payload
        for r in (1, 2, 3):
            _, x, c = h.other(0, r // 2, r % 2)
            cp = rcopy(mine, self.buf.at[0, h.gy], self.ss.at[r - 1], self.rs.at[r - 1], h.dev(x=x, c=c))
            cp.start()
            self.sent.append(cp)

    def plane(self):
        h = self.h
        for r in (1, 2, 3):
            _, x, c = h.other(0, r // 2, r % 2)
            land = self.buf.at[0, x * 2 + c]
            rcopy(land, land, self.ss.at[0], self.rs.at[r - 1], h.sib()).wait_recv()
        return [jnp.where(h.gy == g, self.own, self.buf[0, g]) for g in range(4)]

    def start_z(self, payload):
        h = self.h
        self.own = payload
        mine = self.buf.at[2, 1]
        mine[...] = payload
        for j in (1, 2, 3):
            cp = rcopy(mine, self.buf.at[1, h.z], self.ss.at[2 + j], self.rs.at[3 + h.z], h.dev(z=h.near(j)))
            cp.start()
            self.sent.append(cp)

    def along_z(self):
        h = self.h
        for j in (1, 2, 3):
            land = self.buf.at[1, h.near(j)]
            rcopy(land, land, self.ss.at[0], self.rs.at[3 + h.near(j)], h.sib()).wait_recv()
        return [jnp.where(h.z == g, self.own, self.buf[1, g]) for g in range(4)]


def fold(row):
    return [row[:, 128 * k : 128 * (k + 1)] for k in range(4)]


def pack_rows(*rows):
    rows = rows + (jnp.zeros((1, C), F32),) * (4 - len(rows))
    return jnp.concatenate([part for r in rows for part in fold(r)], axis=0)


def unpack_rows(p):
    return [jnp.concatenate([p[4 * n + k : 4 * n + k + 1] for k in range(4)], axis=1) for n in range(p.shape[0] // 4)]


def column(r):
    return jnp.broadcast_to(r, (128, C)).T


def merge(parts, counts):
    total = sum(counts)
    mass = sum(parts[g][0:4] for g in range(4))
    mean = mass / jnp.maximum(total, 1.0)
    spread = jnp.zeros_like(mass)
    for g in range(4):
        n = jnp.maximum(counts[g], 1.0)
        gap = parts[g][0:4] / n - mean
        spread = spread + parts[g][4:8] + counts[g] * gap * gap
    third = parts[0] + parts[1] + parts[2] + parts[3]
    return jnp.concatenate([mass, spread, third[8:16]], axis=0)


def nn(a, b):
    return lax.dot_general(a, b, (((1,), (0,)), ((), ())), preferred_element_type=F32)


def nt(a, b):
    return lax.dot_general(a, b, (((1,), (1,)), ((), ())), preferred_element_type=F32)


def tn(a, b):
    return lax.dot_general(a, b, (((0,), (0,)), ((), ())), preferred_element_type=F32)


def sigmoid(u):
    return 1.0 / (1.0 + jnp.exp(-u))


def body(
    feat, w1s, w2s, gain, bias, head, hbias, labels, spans, heights, widths, picks,
    pooled_out, fg_out, c1_out, c2_out, gg_out, bg_out, hg_out, hbg_out,
    w1, w2, x3, first, second, slope, dh, base, hid, dw,
    al, edges, bland, hland, sland, fland, fgs, fgl,
    e32, exts, ext, gb, stat, pacc, pz, pg, res, cot, yb, ht, gsc, mc1, mc2,
    l1, lxa, lyb, lya, lxb, lz,
    sem_g, rem_g, sem_ge, rem_ge, sem_l, sem_h, rem_h, sem_s, rem_s, sem_a, rem_a, sem_p, rem_p, sem_r, rem_r,
):
    h = Here()
    sent = []
    z, y = h.z, h.y

    barrier = pltpu.get_barrier_semaphore()
    peers = [h.dev(z=h.near(j)) for j in (1, 2, 3)]
    for r in range(1, 8):
        yy, xx, cc = h.other(r // 4, (r // 2) % 2, r % 2)
        peers.append(h.dev(y=yy, x=xx, c=cc))
    for dev in peers:
        pl.semaphore_signal(barrier, inc=1, device_id=dev, device_id_type=MESH)
    pl.semaphore_wait(barrier, len(peers))

    a2a = rcopy(feat.at[pl.ds(PER * (1 - y), PER)], al, sem_a.at[0], rem_a.at[0], h.ydev())
    a2a.start()
    g1 = Gather(h, w1s, w1, sem_g.at[0], rem_g.at[0], sem_l.at[0], SHARD, CUT, sent)
    sent2 = []
    g2 = Gather(h, w2s, w2, sem_g.at[1], rem_g.at[1], sem_l.at[1], SHARD, CUT, sent2)
    ge = Gather(h, exts, ext, sem_ge, rem_ge, sem_l.at[2], 16, 16, sent)
    g1.start()
    e32[...] = jnp.zeros_like(e32)
    e32[:, 0:2] = gain[...].astype(F32)
    e32[:, 128:130] = bias[...].astype(F32)
    e32[:, 256 : 256 + TASKS] = head[...].astype(F32)
    e32[0:12, 384 : 384 + TASKS] = labels[...].astype(F32)
    exts[...] = e32[...].astype(BF)
    ge.start()

    image = lax.broadcasted_iota(jnp.int32, (1, 8 * PER), 1)
    high, broad = spans[0:1], spans[1:2]

    def pixels(zz, lo, n):
        here = (image >= lo) & (image < lo + n)
        cells = jnp.where(here, jnp.clip(high - ROWS * zz, 0, ROWS) * broad, 0).astype(F32)
        return cells.sum(1, keepdims=True)

    n_plane = [pixels(z, 2 * PER * g + PER * y, PER) for g in range(4)]
    n_z = [sum(pixels(zz, 2 * PER * g + PER * y, PER) for g in range(4)) for zz in range(4)]
    total = sum(n_z)
    my_first = h.gy * 2 * PER + PER * y

    col = lax.broadcasted_iota(jnp.int32, (COLS, C), 0)

    def wide(i, r):
        return jnp.where(ROWS * z + r < heights[my_first + i], widths[my_first + i], 0)

    def keep(i, r, v):
        return jnp.where(col < wide(i, r), v, 0.0)

    zero8 = jnp.zeros((8, C), F32)

    def by8(v):
        return v.reshape(COLS // 8, 8, C).sum(0)

    def put3(i, row, v):
        x3[i, row, :, C : 2 * C] = v.astype(BF)
        x3[i, row, :, 0:C] = jnp.where(col == 0, 0.0, pltpu.roll(v, 1, 0)).astype(BF)
        x3[i, row, :, 2 * C : 3 * C] = jnp.where(col == COLS - 1, 0.0, pltpu.roll(v, COLS - 1, 0)).astype(BF)

    def put_halo(land):
        def one(i, _):
            @pl.when(z > 0)
            def _():
                put3(i, 0, land[0, i].astype(F32))

            @pl.when(z == 0)
            def _():
                x3[i, 0] = jnp.zeros((COLS, 3 * C), BF)

            @pl.when(z < 3)
            def _():
                put3(i, 5, land[1, i].astype(F32))

            @pl.when(z == 3)
            def _():
                x3[i, 5] = jnp.zeros((COLS, 3 * C), BF)

            return 0

        lax.fori_loop(0, PER, one, 0)

    def take_rows(src, offset, row0):
        def one(i, acc):
            for r in range(2):
                v = keep(i, row0 + r, src[offset + i, r].astype(F32))
                base[i, row0 + r] = v.astype(BF)
                put3(i, row0 + r + 1, v)
                acc = acc + by8(v)
            return acc

        return lax.fori_loop(0, PER, one, zero8)

    steps = g1.steps()

    def go(todo, n):
        for _ in range(min(n, len(todo))):
            todo.pop(0)()

    base_sum = take_rows(feat, PER * y, 2 * y)
    go(steps, 5)
    a2a.wait_recv()
    base_sum = (base_sum + take_rows(al, 0, 2 * (1 - y))).sum(0, keepdims=True)
    edges[0] = base[:, 0]
    edges[1] = base[:, ROWS - 1]
    halo = Halo(h, edges, bland, sem_h.at[0], rem_h.at[0])
    halo.start()
    go(steps, 99)
    for step in ge.steps():
        step()
    ge.finish()
    g1.finish()
    g2.start()
    steps = g2.steps()

    gb[0:2] = ext[:, 0:128].astype(F32).T[0:2]
    gb[2:4] = ext[:, 128:256].astype(F32).T[0:2]
    ht[...] = ext[:, 256:384].astype(F32)

    def conv(w, out, land, halo, todo=()):
        todo = list(todo)
        for p in range(3):
            im = pl.ds(2 * p, 2)
            mid = nn(x3[im, 1:5].reshape(8 * COLS, 3 * C), w[3 * C : 6 * C]).reshape(2, 4, COLS, C)
            lo = nn(x3[im, 1:4].reshape(6 * COLS, 3 * C), w[0 : 3 * C]).reshape(2, 3, COLS, C)
            hi = nn(x3[im, 2:5].reshape(6 * COLS, 3 * C), w[6 * C : 9 * C]).reshape(2, 3, COLS, C)
            out[im, 0] = mid[:, 0] + hi[:, 0]
            out[im, 1] = mid[:, 1] + lo[:, 0] + hi[:, 1]
            out[im, 2] = mid[:, 2] + lo[:, 1] + hi[:, 2]
            out[im, 3] = mid[:, 3] + lo[:, 2]
            if todo:
                todo.pop(0)()
        halo.wait()
        put_halo(land)
        out[:, 0] += nn(x3[:, 0].reshape(6 * COLS, 3 * C), w[0 : 3 * C]).reshape(PER, COLS, C)
        out[:, 3] += nn(x3[:, 5].reshape(6 * COLS, 3 * C), w[6 * C : 9 * C]).reshape(PER, COLS, C)

    def conv_back(w, out, land, halo, todo=()):
        todo = list(todo)

        def taps(lhs, a):
            acc = None
            for b in range(3):
                part = nt(lhs[:, (2 - b) * C : (3 - b) * C], w[(3 * a + b) * C : (3 * a + b + 1) * C])
                acc = part if acc is None else acc + part
            return acc

        for p in range(3):
            im = pl.ds(2 * p, 2)
            mid = taps(x3[im, 1:5].reshape(8 * COLS, 3 * C), 1).reshape(2, 4, COLS, C)
            lo = taps(x3[im, 1:4].reshape(6 * COLS, 3 * C), 2).reshape(2, 3, COLS, C)
            hi = taps(x3[im, 2:5].reshape(6 * COLS, 3 * C), 0).reshape(2, 3, COLS, C)
            out[im, 0] = mid[:, 0] + hi[:, 0]
            out[im, 1] = mid[:, 1] + lo[:, 0] + hi[:, 1]
            out[im, 2] = mid[:, 2] + lo[:, 1] + hi[:, 2]
            out[im, 3] = mid[:, 3] + lo[:, 2]
            if todo:
                todo.pop(0)()
        halo.wait()
        put_halo(land)
        out[:, 0] += taps(x3[:, 0].reshape(6 * COLS, 3 * C), 2).reshape(PER, COLS, C)
        out[:, 3] += taps(x3[:, 5].reshape(6 * COLS, 3 * C), 0).reshape(PER, COLS, C)

    def spread(src):
        def one(i, carry):
            n, mean, dev = carry
            widths_i = [wide(i, r) for r in range(ROWS)]
            ni = sum(widths_i).astype(F32)
            mass = jnp.zeros((8, C), F32)
            for r in range(ROWS):
                v = jnp.where(col < widths_i[r], src[i, r], 0.0)
                mass = mass + v.reshape(COLS // 8, 8, C).sum(0)
            mi = mass.sum(0, keepdims=True) / jnp.maximum(ni, 1.0)
            sq = jnp.zeros((8, C), F32)
            for r in range(ROWS):
                v = jnp.where(col < widths_i[r], src[i, r] - mi, 0.0)
                sq = sq + (v * v).reshape(COLS // 8, 8, C).sum(0)
            both = jnp.maximum(n + ni, 1.0)
            gap = mi - mean
            return (
                n + ni,
                mean + gap * (ni / both),
                dev + sq.sum(0, keepdims=True) + gap * gap * (n * ni / both),
            )

        zero = jnp.zeros((1, C), F32)
        n, mean, dev = lax.fori_loop(0, PER, one, (jnp.float32(0.0), zero, zero))
        return mean * n, dev

    def statistics(src, k, todo, inputs):
        ex = Sums(h, stat.at[k], sem_s.at[k], rem_s.at[k], sent)
        ex.start_plane(pack_rows(*spread(src), inputs))
        go(todo, 1)
        ex.start_z(merge(ex.plane(), n_plane))
        go(todo, 1)
        both = merge(ex.along_z(), n_z)
        mass, dev, inputs, _ = unpack_rows(both)
        return mass / total, lax.rsqrt(dev / total + norm_eps), inputs / total

    def start_sums(k, *rows):
        ex = Sums(h, stat.at[k], sem_s.at[k], rem_s.at[k], sent)
        ex.start_plane(pack_rows(*rows))
        return ex

    def mid_sums(ex):
        parts = ex.plane()
        ex.start_z(parts[0] + parts[1] + parts[2] + parts[3])

    def end_sums(ex):
        parts = ex.along_z()
        return parts[0] + parts[1] + parts[2] + parts[3]

    def edges_first(one, start):
        def edge(i, acc):
            for k, r in enumerate((0, ROWS - 1)):
                v = one(i, r)
                edges[k, i] = v.astype(BF)
                acc = acc + by8(v)
            return acc

        def inner(i, acc):
            for r in range(1, ROWS - 1):
                acc = acc + by8(one(i, r))
            return acc

        acc = lax.fori_loop(0, PER, edge, zero8)
        start()
        return lax.fori_loop(0, PER, inner, acc).sum(0, keepdims=True)

    conv(w1, first, bland, halo, [steps.pop(0) for _ in range(3)])
    center, rs1, base_mean = statistics(first, 0, steps, base_sum)
    go(steps, 1)
    gain1, bias1 = gb[0:1], gb[2:3]

    def hidden(i, r):
        xh = (first[i, r] - center) * rs1
        first[i, r] = xh
        u = gain1 * xh + bias1
        v = keep(i, r, u * sigmoid(u))
        hid[i, r] = v.astype(BF)
        put3(i, r + 1, v)
        return v

    halo = Halo(h, edges, hland, sem_h.at[1], rem_h.at[1])
    hid_sum = edges_first(hidden, halo.start)
    go(steps, 99)
    g2.finish()
    conv(w2, second, hland, halo)
    center, rs2, hid_mean = statistics(second, 1, [], hid_sum)
    gain2, bias2 = gb[1:2], gb[3:4]

    pacc[...] = jnp.zeros_like(pacc)

    def finals(i, _):
        acc = [jnp.zeros((8, C), F32) for _ in range(3)]
        for r in range(ROWS):
            xh = (second[i, r] - center) * rs2
            second[i, r] = xh
            pre = gain2 * xh + bias2 + base[i, r].astype(F32)
            s = sigmoid(pre)
            act = keep(i, r, pre * s)
            sl = keep(i, r, s * (1.0 + pre * (1.0 - s)))
            slope[i, r] = sl
            for k, v in enumerate((act, sl, sl * xh)):
                acc[k] = acc[k] + v.reshape(COLS // 8, 8, C).sum(0)
        for k in range(3):
            pacc[k, pl.ds(i, 1)] = acc[k].sum(0, keepdims=True)
        return 0

    lax.fori_loop(0, PER, finals, 0)

    rows8 = lax.broadcasted_iota(jnp.int32, (8, 1), 0)
    inv_pix = jnp.zeros((8, 1), F32)
    for i in range(PER):
        inv_pix = jnp.where(rows8 == i, 1.0 / (heights[my_first + i] * widths[my_first + i]).astype(F32), inv_pix)
    me_z = pz.at[z]
    me_z[...] = pacc[0]
    for j in (1, 2, 3):
        cp = rcopy(me_z, me_z, sem_p.at[j - 1], rem_p.at[z], h.dev(z=h.near(j)))
        cp.start()
        sent.append(cp)
    head_gram = lax.dot_general(ht[...], ht[...], (((0,), (0,)), ((), ())), precision=HIGH, preferred_element_type=F32)
    for j in (1, 2, 3):
        land = pz.at[h.near(j)]
        rcopy(land, land, sem_p.at[0], rem_p.at[h.near(j)], h.sib()).wait_recv()
    slot = (y * 2 + h.x) * 2 + h.c
    me_p = pg.at[slot]
    me_p[...] = (pz[0] + pz[1] + pz[2] + pz[3]) * inv_pix
    for r in range(1, 8):
        yy, xx, cc = h.other(r // 4, (r // 2) % 2, r % 2)
        cp = rcopy(me_p, me_p, sem_p.at[2 + r], rem_p.at[3 + r], h.dev(y=yy, x=xx, c=cc))
        cp.start()
        sent.append(cp)
    lane = lax.broadcasted_iota(jnp.int32, (8, 128), 1)
    row = lax.broadcasted_iota(jnp.int32, (8, 128), 0)
    real = (row < PER) & (lane < TASKS)
    wanted = []
    for s in range(8):
        yy, gy = s // 4, s % 4
        lab = ext[16 * gy : 16 * gy + 16, 384:512].astype(F32)
        lab = lab[PER * yy : PER * yy + PER]
        wanted.append(jnp.concatenate([lab, jnp.zeros((2, 128), F32)], axis=0))
    for r in range(1, 8):
        yy, xx, cc = h.other(r // 4, (r // 2) % 2, r % 2)
        land = pg.at[(yy * 2 + xx) * 2 + cc]
        rcopy(land, land, sem_p.at[0], rem_p.at[3 + r], h.sib()).wait_recv()
    pooled = pg[...].reshape(64, C)
    offset = hbias[...].astype(F32)
    logits = lax.dot_general(pooled, ht[...], (((1,), (0,)), ((), ())), precision=HIGH, preferred_element_type=F32)
    logits = logits.reshape(8, 8, 128) + offset
    images = 8 * PER
    for s in range(8):
        res[s] = jnp.where(real, (sigmoid(logits[s]) - wanted[s]) / images, 0.0)
    residual = res[...].reshape(64, 128)
    gram = head_gram * lax.dot_general(
        residual, residual, (((0,), (0,)), ((), ())), precision=HIGH, preferred_element_type=F32
    )
    gram = gram[0:TASKS]
    lane1 = lax.broadcasted_iota(jnp.int32, (1, 128), 1)
    sub = lax.broadcasted_iota(jnp.int32, (TASKS, 128), 0)

    def fw(k, carry):
        mix, q = carry
        t = picks[k]
        one = (lane1 == t).astype(F32)
        line = jnp.where(sub == t, gram, 0.0).sum(0, keepdims=True)
        self_dot = (mix * q).sum(1, keepdims=True)
        cross = (one * q).sum(1, keepdims=True)
        vertex = (one * line).sum(1, keepdims=True)
        d = jnp.maximum(self_dot + vertex - 2.0 * cross, 0.1 * vertex)
        step = jnp.clip((self_dot - cross) / d, 0.0, 1.0)
        return (1.0 - step) * mix + step * one, (1.0 - step) * q + step * line

    mix0 = jnp.where(lane1 < TASKS, 1.0 / TASKS, 0.0)
    mix, _ = lax.fori_loop(0, STEPS, fw, (mix0, gram.sum(0, keepdims=True) / TASKS))
    mine = res[slot] * mix
    cot[...] = inv_pix * lax.dot_general(
        mine, ht[...], (((1,), (1,)), ((), ())), precision=HIGH, preferred_element_type=F32
    )
    ex = start_sums(
        2, (cot[...] * pacc[1]).sum(0, keepdims=True), (cot[...] * pacc[2]).sum(0, keepdims=True)
    )

    for yy in range(2):
        pooled_out[PER * yy : PER * (yy + 1)] = pg[(yy * 2 + h.x) * 2 + h.c][0:PER]
    head_grad = lax.dot_general(
        pooled, residual, (((0,), (0,)), ((), ())), precision=HIGH, preferred_element_type=F32
    )
    mid_sums(ex)
    gsc[...] = head_grad
    hg_out[...] = gsc[pl.ds(pl.multiple_of(h.idx() * 16, 16), 16)][:, 0:TASKS]
    hbg_out[...] = residual.sum(0, keepdims=True)[:, 0:TASKS]
    sums2 = end_sums(ex)
    yb[0, 0:8] = sums2[0:8]
    mc1[0:C] = column(base_mean)
    mc1[C:] = mc1[0:256]
    mc2[0:C] = column(hid_mean)
    mc2[C:] = mc2[0:256]
    yb[0, 24:32] = pack_rows(hid_mean, base_mean)[0:8]

    sum_b, sum_g, _, _ = unpack_rows(sums2)
    mean_b, mean_g = sum_b / total, sum_g / total
    scale = gain2 * rs2

    def d_second(i, r):
        xh = second[i, r]
        dp = slope[i, r] * cot[pl.ds(i, 1)]
        v = keep(i, r, scale * (dp - mean_b - xh * mean_g))
        put3(i, r + 1, v)
        return v.astype(BF).astype(F32)

    halo = Halo(h, edges, sland, sem_h.at[2], rem_h.at[2])
    d2_sum = edges_first(d_second, halo.start)
    conv_back(w2, dh, sland, halo)

    def d_norm1(i, carry):
        a, b = carry
        for r in range(ROWS):
            xh = first[i, r]
            u = gain1 * xh + bias1
            s = sigmoid(u)
            v = keep(i, r, dh[i, r] * (s * (1.0 + u * (1.0 - s))))
            dh[i, r] = v
            a = a + v.reshape(COLS // 8, 8, C).sum(0)
            b = b + (v * xh).reshape(COLS // 8, 8, C).sum(0)
        return a, b

    a, b = lax.fori_loop(0, PER, d_norm1, (zero8, zero8))
    ex = start_sums(3, a.sum(0, keepdims=True), b.sum(0, keepdims=True), d2_sum)

    def weight_taps(x, out, mean, d_sum, lo, hi):
        for t in range(lo, hi):
            ta, tb = t // 3, t % 3
            d = x3[:, 2 - ta : 6 - ta, :, (2 - tb) * C : (3 - tb) * C].reshape(PER * ROWS * COLS, C)
            part = tn(x[...].reshape(PER * ROWS * COLS, C), d)
            off = jnp.concatenate([mean[0:C] * f for f in fold(d_sum)], axis=1)
            out[t * C : (t + 1) * C] = (part - off).astype(BF)

    def scatter(k, src, out):
        return Scatter(
            h, src, l1.at[k], lxa.at[k], lyb.at[k], lya.at[k], lxb.at[k], lz.at[k], sem_r.at[k], rem_r.at[k], out, sent
        )

    r2 = scatter(0, dw, c2_out)
    todo2 = r2.steps()

    def flush(todo, n=1):
        for _ in range(min(n, len(todo))):
            for step in todo.pop(0):
                step()

    weight_taps(hid, dw, mc2, d2_sum, 0, 3)
    flush(todo2)
    mid_sums(ex)
    weight_taps(hid, dw, mc2, d2_sum, 3, 5)
    flush(todo2)
    weight_taps(hid, dw, mc2, d2_sum, 5, 7)
    flush(todo2)
    weight_taps(hid, dw, mc2, d2_sum, 7, 9)
    flush(todo2)
    sums1 = end_sums(ex)
    yb[0, 8:20] = sums1[0:12]
    sum_b, sum_g, _, _ = unpack_rows(sums1)
    mean_b1, mean_g1 = sum_b / total, sum_g / total
    scale1 = gain1 * rs1

    def d_first(i, r):
        v = keep(i, r, scale1 * (dh[i, r] - mean_b1 - first[i, r] * mean_g1))
        put3(i, r + 1, v)
        return v.astype(BF).astype(F32)

    halo = Halo(h, edges, fland, sem_h.at[3], rem_h.at[3])
    d1_sum = edges_first(d_first, halo.start)
    ex = start_sums(4, d1_sum)
    conv_back(w1, dh, fland, halo, [functools.partial(flush, todo2) for _ in range(3)])
    mid_sums(ex)

    def result(i, r):
        return keep(i, r, dh[i, r] + slope[i, r] * cot[pl.ds(i, 1)])

    back = []
    for p in range(3):
        for i in (2 * p, 2 * p + 1):
            for r in range(2):
                fgs[i, r] = result(i, 2 * (1 - y) + r).astype(BF)
        im = pl.ds(2 * p, 2)
        cp = rcopy(fgs.at[im], fgl.at[im], sem_a.at[2 + p], rem_a.at[2 + p], h.ydev())
        cp.start()
        back.append(cp)

    def stay(i, _):
        for r in range(2):
            fg_out[PER * y + i, r] = result(i, 2 * y + r)
        return 0

    lax.fori_loop(0, PER, stay, 0)
    flush(todo2, 99)
    yb[0, 20:24] = end_sums(ex)[0:4]
    ysum = rcopy(yb.at[0], yb.at[1], sem_a.at[1], rem_a.at[1], h.ydev())
    ysum.start()

    for cp in sent2:
        cp.wait_send()
    r1 = scatter(1, w2, c1_out)
    todo1 = r1.steps()
    weight_taps(base, w2, mc1, d1_sum, 0, 3)
    flush(todo1)
    weight_taps(base, w2, mc1, d1_sum, 3, 5)
    flush(todo1)
    weight_taps(base, w2, mc1, d1_sum, 5, 7)
    flush(todo1)
    weight_taps(base, w2, mc1, d1_sum, 7, 9)
    flush(todo1)
    flush(todo1)

    ysum.wait_recv()
    sb2, sg2, sb1, sg1 = unpack_rows(yb[0, 0:16] + yb[1, 0:16])
    flat = jnp.concatenate([sg1, sg2, sb1, sb2, jnp.zeros((124, C), F32)], axis=0).T
    gsc[...] = flat
    own = gsc[pl.ds(pl.multiple_of(h.idx() * 16, 16), 16)]
    gg_out[...] = own[:, 0:2]
    bg_out[...] = own[:, 2:4]

    at = pl.ds(pl.multiple_of(lax.rem(h.idx() * SHARD, C), 16), SHARD)
    d2_all, d1_all, hid_other, base_other = unpack_rows(yb[1, 16:32])
    d2_mine, d1_mine, _, _ = unpack_rows(yb[0, 16:32])

    def taken_off(mean, other, all_mine, all_other):
        off = jnp.concatenate([mean[at] * f for f in fold(all_mine)], axis=1)
        mean[0:C] = column(other)
        mean[C:] = mean[0:256]
        return off + jnp.concatenate([mean[at] * f for f in fold(all_other)], axis=1)

    off2 = taken_off(mc2, hid_other, d2_mine, d2_all)
    off1 = taken_off(mc1, base_other, d1_mine, d1_all)
    r2.finish(off2)
    flush(todo1)
    for p in range(3):
        back[p].wait_recv()
        for i in (2 * p, 2 * p + 1):
            fg_out[PER * (1 - y) + i] = fgl[i].astype(F32)
    flush(todo1, 99)
    r1.finish(off1)

    a2a.wait_send()
    ysum.wait_send()
    for cp in back + sent:
        cp.wait_send()
    r1.drain()
    r2.drain()


def fused(features, w1s, w2s, gain, bias, head, head_bias, labels, heights, widths, picks):
    vm = pl.BlockSpec(memory_space=pltpu.VMEM)
    sm = pl.BlockSpec(memory_space=pltpu.SMEM)
    V = pltpu.VMEM
    dma = pltpu.SemaphoreType.DMA
    maps = (PER, ROWS, COLS, C)
    edge = (2, PER, COLS, C)
    half = (PER, 2, COLS, C)
    scratch = [
        V((9 * C, C), BF), V((9 * C, C), BF), V((PER, ROWS + 2, COLS, 3 * C), BF),
        V(maps, F32), V(maps, F32), V(maps, F32), V(maps, F32), V(maps, BF), V(maps, BF), V((9 * C, C), BF),
        V(half, BF), V(edge, BF), V(edge, BF), V(edge, BF), V(edge, BF), V(edge, BF), V(half, BF), V(half, BF),
        V((16, C), F32), V((16, C), BF), V((C, C), BF), V((8, C), F32),
        V((5, 3, 4, 16, 128), F32), V((3, 8, C), F32), V((4, 8, C), F32), V((8, 8, C), F32),
        V((8, 8, 128), F32), V((8, C), F32), V((2, 32, 128), F32), V((C, 128), F32), V((C, 128), F32),
        V((C + 256, 128), F32), V((C + 256, 128), F32),
        V((2, 4, 4, SHARD, C), BF), V((2, 4, 2, CUT, C), BF), V((2, 4, 2, SHARD - CUT, C), BF),
        V((2, 4, CUT, C), BF), V((2, 4, SHARD - CUT, C), BF), V((2, 4, SHARD, C), BF),
        dma((2, 43)), dma((2, 43)), dma((43,)), dma((43,)), dma((3,)), dma((4, 2)), dma((4, 2)),
        dma((5, 8)), dma((5, 8)), dma((5,)), dma((5,)), dma((12,)), dma((12,)), dma((2, 48)), dma((2, 48)),
    ]
    f = jax.ShapeDtypeStruct
    outs = pl.pallas_call(
        body,
        out_shape=[
            f((2 * PER, C), F32), f((2 * PER, 2, COLS, C), F32), f((SHARD, C), F32), f((SHARD, C), F32),
            f((16, 2), F32), f((16, 2), F32), f((16, TASKS), F32), f((1, TASKS), F32),
        ],
        in_specs=[vm] * 9 + [sm] * 3,
        out_specs=[vm] * 8,
        scratch_shapes=scratch,
        compiler_params=pltpu.CompilerParams(
            collective_id=0, has_side_effects=True, vmem_limit_bytes=63 * 2**20
        ),
        name="block",
    )(
        features, w1s, w2s, gain, bias, head,
        jnp.pad(head_bias.reshape(1, TASKS), ((0, 0), (0, 128 - TASKS))), labels,
        jnp.stack([heights, widths]), heights, widths, picks,
    )
    return tuple(outs[:7]) + (outs[7].reshape(TASKS),)


def extended(cells, sides, width):
    for axis, dim in sides:
        count = lax.axis_size(axis)
        ends = count - 1
        head = lax.slice_in_dim(cells, 0, width, axis=dim)
        tail = lax.slice_in_dim(cells, cells.shape[dim] - width, cells.shape[dim], axis=dim)
        cells = jnp.concatenate(
            [
                lax.ppermute(tail, axis, [(i, (i + 1) % count) for i in range(ends)]),
                cells,
                lax.ppermute(head, axis, [((i + 1) % count, i) for i in range(ends)]),
            ],
            axis=dim,
        )
    return cells


def make_patches(padded, row_count, col_count):
    widened = jnp.pad(padded, ((0, 0), (0, 0), (1, 1), (0, 0)))
    pieces = [
        widened[:, row_off : row_off + row_count, col_off : col_off + col_count, :]
        for row_off in range(3)
        for col_off in range(3)
    ]
    joined = jnp.concatenate(pieces, axis=-1)
    return joined.reshape(-1, joined.shape[-1])


def conv_rows(act, weight):
    padded = extended(act, (("gx", 1),), 1)
    patches = make_patches(padded, act.shape[1], act.shape[2])
    output = jnp.dot(patches, weight, preferred_element_type=jnp.float32)
    return (output.reshape(act.shape[:3] + (weight.shape[1],)), padded)


def reversed_taps(weight):
    channels = weight.shape[1]
    taps = weight.reshape(9, channels, channels)[::-1]
    return jnp.transpose(taps, (0, 2, 1)).reshape(9 * channels, channels)


def weight_term(padded, grad_bf):
    patches = make_patches(padded, grad_bf.shape[1], grad_bf.shape[2])
    flat_grad = grad_bf.reshape(-1, grad_bf.shape[-1])
    return lax.dot_general(
        patches, flat_grad, (((0,), (0,)), ((), ())), preferred_element_type=jnp.float32
    )


def batch_statistics(values, inner_result, pixel_total):
    center_val = (
        lax.psum(jnp.sum(values * inner_result, axis=(0, 1, 2)), ("gx", "gy")) / pixel_total
    )
    centered = values - center_val
    spread_sq = (
        lax.psum(jnp.sum(inner_result * centered * centered, axis=(0, 1, 2)), ("gx", "gy"))
        / pixel_total
    )
    inverse_scale = lax.rsqrt(spread_sq + norm_eps)
    return (centered * inverse_scale, inverse_scale)


def norm_backward(
    output_gradient, normalized_input, inverse_scale, norm_scale_factor, inner_result, pixel_total
):
    bias_gradient_total, scale_gradient_total = lax.psum(
        (
            jnp.sum(output_gradient, axis=(0, 1, 2)),
            jnp.sum(output_gradient * normalized_input, axis=(0, 1, 2)),
        ),
        ("gx", "gy"),
    )
    backward_result = (
        norm_scale_factor
        * inverse_scale
        * (
            output_gradient
            - bias_gradient_total / pixel_total
            - normalized_input * scale_gradient_total / pixel_total
        )
        * inner_result
    )
    return (backward_result, scale_gradient_total, bias_gradient_total)


def silu_slope(values):
    sig_val = jax.nn.sigmoid(values)
    return sig_val * (1.0 + values * (1.0 - sig_val))


def frank_wolfe(gram, picks):
    task_ids = jnp.arange(TASKS)

    def fw_step(index, task_mix):
        onehot = (task_ids == picks[index]).astype(jnp.float32)
        mixed_vec = jnp.dot(gram, task_mix, precision=lax.Precision.HIGHEST)
        self_dot = jnp.sum(task_mix * mixed_vec)
        cross_dot = jnp.sum(onehot * mixed_vec)
        vertex_dot = jnp.sum(onehot * jnp.dot(gram, onehot, precision=lax.Precision.HIGHEST))
        distance = jnp.maximum(self_dot + vertex_dot - 2.0 * cross_dot, 0.1 * vertex_dot)
        step_size = jnp.clip((self_dot - cross_dot) / distance, 0.0, 1.0)
        return (1.0 - step_size) * task_mix + step_size * onehot

    start = jnp.full((TASKS,), 1.0 / TASKS, jnp.float32)
    return lax.fori_loop(0, STEPS, fw_step, start)


def on_device(
    features,
    conv1_weight,
    conv2_weight,
    norm_gain,
    norm_bias,
    head_weight,
    head_bias,
    labels,
    heights,
    widths,
    picks,
):
    image_count, row_count, col_count, channels = features.shape
    per_micro = image_count // MICRO
    total_images = image_count * lax.axis_size("gy")
    row_ids = lax.axis_index("gx") * row_count + jnp.arange(row_count)
    my_heights = lax.dynamic_slice_in_dim(heights, lax.axis_index("gy") * image_count, image_count)
    my_widths = lax.dynamic_slice_in_dim(widths, lax.axis_index("gy") * image_count, image_count)
    inside_all = (
        (row_ids[None, :, None] < my_heights[:, None, None])
        & (jnp.arange(col_count)[None, None, :] < my_widths[:, None, None])
    ).astype(jnp.float32)[..., None]
    pixel_count = (my_heights * my_widths).astype(jnp.float32)
    micro_pixels = jnp.sum((heights * widths).reshape(-1, MICRO, per_micro), axis=(0, 2)).astype(
        jnp.float32
    )

    def weights_now():
        return (
            lax.all_gather(conv1_weight, ("gx", "gy"), axis=0, tiled=True),
            lax.all_gather(conv2_weight, ("gx", "gy"), axis=0, tiled=True),
            lax.all_gather(norm_gain, ("gx", "gy"), axis=0, tiled=True),
            lax.all_gather(norm_bias, ("gx", "gy"), axis=0, tiled=True),
            lax.all_gather(head_weight, ("gx", "gy"), axis=0, tiled=True),
        )

    saved = []
    pooled_parts = []
    head_full = None
    for index in range(MICRO):
        conv_one, conv_two, gain_full, bias_full, head_full = weights_now()
        scale_factors = gain_full.astype(jnp.float32)
        bias_values = bias_full.astype(jnp.float32)
        inner_result = inside_all[index * per_micro : (index + 1) * per_micro]
        pixel_total = micro_pixels[index]
        base_input_bfloat = features[
            index * per_micro : (index + 1) * per_micro
        ] * inner_result.astype(jnp.bfloat16)
        first_convolution, padded_input = conv_rows(base_input_bfloat, conv_one)
        first_normalized, first_scale = batch_statistics(
            first_convolution, inner_result, pixel_total
        )
        first_norm_output = scale_factors[:, 0] * first_normalized + bias_values[:, 0]
        hidden_bf = (jax.nn.silu(first_norm_output) * inner_result).astype(jnp.bfloat16)
        second_convolution, padded_hidden_state = conv_rows(hidden_bf, conv_two)
        second_normalized, second_scale = batch_statistics(
            second_convolution, inner_result, pixel_total
        )
        before_activation = (
            scale_factors[:, 1] * second_normalized
            + bias_values[:, 1]
            + base_input_bfloat.astype(jnp.float32)
        )
        final_act = jax.nn.silu(before_activation) * inner_result
        pooled_parts.append(jnp.sum(final_act, axis=(1, 2)))
        saved.append(
            (
                padded_input,
                padded_hidden_state,
                first_normalized,
                first_scale,
                first_norm_output,
                second_normalized,
                second_scale,
                before_activation,
            )
        )
    pooled = lax.psum(jnp.concatenate(pooled_parts, axis=0), "gx") / pixel_count[:, None]
    head_mat = head_full.astype(jnp.float32)
    logits = jnp.dot(pooled, head_mat, precision=lax.Precision.HIGHEST) + head_bias.astype(
        jnp.float32
    )
    residual = (jax.nn.sigmoid(logits) - labels.astype(jnp.float32)) / total_images
    gram_part = jnp.dot(residual.T, residual, precision=lax.Precision.HIGHEST)
    head_part = jnp.dot(pooled.T, residual, precision=lax.Precision.HIGHEST)
    gram_sum, head_bias_grad, head_total = (
        lax.psum(gram_part.astype(jnp.bfloat16), "gy").astype(jnp.float32),
        lax.psum(jnp.sum(residual, axis=0).astype(jnp.bfloat16), "gy").astype(jnp.float32),
        lax.psum(head_part.astype(jnp.bfloat16), "gy").astype(jnp.float32),
    )
    gram = gram_sum * jnp.dot(head_mat.T, head_mat, precision=lax.Precision.HIGHEST)
    task_mix = frank_wolfe(gram, picks)
    pooled_cot = jnp.dot(residual * task_mix, head_mat.T, precision=lax.Precision.HIGHEST)
    shard_rows = 9 * channels // lax.axis_size(("gx", "gy"))
    conv1_grad = jnp.zeros((shard_rows, channels), jnp.float32)
    conv2_grad = jnp.zeros((shard_rows, channels), jnp.float32)
    gain_total = jnp.zeros((channels, 2), jnp.float32)
    bias_total = jnp.zeros((channels, 2), jnp.float32)
    feat_parts = []
    for index in range(MICRO):
        conv_one, conv_two, gain_full, bias_full, unused_heads = weights_now()
        scale_factors = gain_full.astype(jnp.float32)
        (
            padded_input,
            padded_hidden_state,
            first_normalized,
            first_scale,
            first_norm_output,
            second_normalized,
            second_scale,
            before_activation,
        ) = saved[index]
        inner_result = inside_all[index * per_micro : (index + 1) * per_micro]
        pixel_total = micro_pixels[index]
        cot_part = (
            pooled_cot[index * per_micro : (index + 1) * per_micro]
            / pixel_count[index * per_micro : (index + 1) * per_micro, None]
        )
        gradient_before_relu = (
            cot_part[:, None, None, :] * inner_result * silu_slope(before_activation)
        )
        d_second, gain_two, bias_two = norm_backward(
            gradient_before_relu,
            second_normalized,
            second_scale,
            scale_factors[:, 1],
            inner_result,
            pixel_total,
        )
        second_bf = d_second.astype(jnp.bfloat16)
        term_two = weight_term(padded_hidden_state, second_bf)
        d_hidden, unused_pad = conv_rows(second_bf, reversed_taps(conv_two))
        gradient_norm_first = d_hidden * inner_result * silu_slope(first_norm_output)
        d_first, gain_one, bias_one = norm_backward(
            gradient_norm_first,
            first_normalized,
            first_scale,
            scale_factors[:, 0],
            inner_result,
            pixel_total,
        )
        first_bf = d_first.astype(jnp.bfloat16)
        term_one = weight_term(padded_input, first_bf)
        d_base, unused_pad_two = conv_rows(first_bf, reversed_taps(conv_one))
        feat_parts.append((d_base + gradient_before_relu) * inner_result)
        gain_total = gain_total + jnp.stack([gain_one, gain_two], axis=1)
        bias_total = bias_total + jnp.stack([bias_one, bias_two], axis=1)
        shard_one, shard_two = (
            lax.psum_scatter(term_one, ("gx", "gy"), scatter_dimension=0, tiled=True),
            lax.psum_scatter(term_two, ("gx", "gy"), scatter_dimension=0, tiled=True),
        )
        conv1_grad = conv1_grad + shard_one
        conv2_grad = conv2_grad + shard_two
    flat_index = lax.axis_index(("gx", "gy"))
    chan_rows = channels // lax.axis_size(("gx", "gy"))
    gain_grad = lax.dynamic_slice_in_dim(gain_total, flat_index * chan_rows, chan_rows, 0)
    bias_grad = lax.dynamic_slice_in_dim(bias_total, flat_index * chan_rows, chan_rows, 0)
    head_grad = lax.dynamic_slice_in_dim(head_total, flat_index * chan_rows, chan_rows, 0)
    features_grad = jnp.concatenate(feat_parts, axis=0)
    return (
        pooled,
        features_grad,
        conv1_grad,
        conv2_grad,
        gain_grad,
        bias_grad,
        head_grad,
        head_bias_grad,
    )


def solution(mesh):
    in_specs = (
        P("gy", "gx", None, None),
        P(("gx", "gy"), None),
        P(("gx", "gy"), None),
        P(("gx", "gy"), None),
        P(("gx", "gy"), None),
        P(("gx", "gy"), None),
        P(),
        P("gy", None),
        P(),
        P(),
        P(),
    )
    out_specs = (
        P("gy", None),
        P("gy", "gx", None, None),
        P(("gx", "gy"), None),
        P(("gx", "gy"), None),
        P(("gx", "gy"), None),
        P(("gx", "gy"), None),
        P(("gx", "gy"), None),
        P(),
    )
    whole = dict(mesh.shape) != {"gx": 8, "gy": 4}
    return jax.shard_map(
        on_device if whole else fused, mesh=mesh, in_specs=in_specs, out_specs=out_specs, check_vma=False
    )
```

```python
import functools

import jax
import jax.numpy as jnp
from jax import lax
from jax.experimental import pallas as pl
from jax.experimental.pallas import tpu as pltpu
from jax.sharding import PartitionSpec as P

TASKS = 40
MICRO = 2
STEPS = 20
norm_eps = 1e-05
BF = jnp.bfloat16
F32 = jnp.float32
HIGH = lax.Precision.HIGHEST
MESH = pl.DeviceIdType.MESH

C = 512
COLS = 64
PER = 6
ROWS = 4
SHARD = 144
CUT = 112
SUM_CUT = 112


class Here:
    def __init__(self):
        gx = lax.axis_index("gx")
        gy = lax.axis_index("gy")
        self.z = lax.div(gx, 2)
        self.y = lax.rem(gx, 2)
        self.x = lax.div(gy, 2)
        self.c = lax.rem(gy, 2)
        self.gy = gy
        self.middle = lax.rem(self.z + 1, 4) >= 2

    def _fill(self, z, y, x, c):
        return (
            self.z if z is None else z,
            self.y if y is None else y,
            self.x if x is None else x,
            self.c if c is None else c,
        )

    def dev(self, z=None, y=None, x=None, c=None):
        z, y, x, c = self._fill(z, y, x, c)
        return {"gx": z * 2 + y, "gy": x * 2 + c}

    def idx(self, z=None, y=None, x=None, c=None):
        z, y, x, c = self._fill(z, y, x, c)
        return ((z * 2 + y) * 2 + x) * 2 + c

    def near(self, j):
        z = self.z
        if j == 0:
            return z
        if j == 1:
            return z + 1 - 2 * lax.rem(z, 2)
        if j == 2:
            return 2 - lax.div(z, 2)
        return 3 - 3 * lax.div(z, 2)

    def other(self, dy, dx, dc):
        return (
            1 - self.y if dy else self.y,
            1 - self.x if dx else self.x,
            1 - self.c if dc else self.c,
        )

    def ydev(self):
        return self.dev(y=1 - self.y)

    def xdev(self):
        return self.dev(x=1 - self.x)

    def sib(self):
        return self.dev(c=1 - self.c)


def rcopy(src, dst, ss, rs, dev):
    return pltpu.make_async_remote_copy(
        src_ref=src, dst_ref=dst, send_sem=ss, recv_sem=rs, device_id=dev, device_id_type=MESH
    )


class Gather:
    def __init__(self, h, own, out, ss, rs, lsem, rows, cut, sent):
        self.h, self.own, self.ss, self.rs = h, own, ss, rs
        self.lsem, self.rows, self.cut, self.sent = lsem, rows, cut, sent
        self.all = out.reshape(4, 2, 2, 2, rows, C)
        self.split = cut < rows
        self.mids = []

    def head(self, z, y, x):
        return self.all.at[z, y, x, self.h.c, pl.ds(0, self.cut)]

    def tail(self, z, y, x):
        return self.all.at[z, y, x, self.h.c, pl.ds(self.cut, self.rows - self.cut)]

    def pair(self, z, x, c):
        return self.all.at[z, :, x, c, pl.ds(0, self.cut)]

    def plane(self, z, c):
        return self.all.at[z, :, :, c, pl.ds(self.cut, self.rows - self.cut)]

    def send(self, k, ref, dev, src=None):
        cp = rcopy(ref if src is None else src, ref, self.ss.at[k], self.rs.at[k], dev)
        cp.start()
        self.sent.append(cp)

    def mid_send(self, k, ref, j, rk, src=None):
        cp = rcopy(ref if src is None else src, ref, self.ss.at[k], self.rs.at[rk], self.h.dev(z=self.h.near(j)))
        pl.when(self.h.middle)(lambda: cp.start())
        self.mids.append(cp)

    def wait(self, k, ref):
        rcopy(ref, ref, self.ss.at[0], self.rs.at[k], self.h.sib()).wait_recv()

    def start(self):
        h = self.h
        self.local = pltpu.make_async_copy(self.own, self.all.at[h.z, h.y, h.x, h.c], self.lsem)
        self.local.start()
        me = self.head(h.z, h.y, h.x)
        own = self.own.at[pl.ds(0, self.cut)]
        self.send(8, me, h.xdev(), own)
        self.send(4, me, h.ydev(), own)
        self.send(0, me, h.dev(z=h.near(1)), own)
        self.mid_send(34, me, 2, 1, own)
        if self.split:
            self.send(24, self.tail(h.z, h.y, h.x), h.xdev(), self.own.at[pl.ds(self.cut, self.rows - self.cut)])

    def along_z(self, j):
        h = self.h
        part = self.head(h.near(j), h.y, h.x)
        self.wait(j - 1, part)
        if j == 1:
            self.mid_send(35, part, 2, 2)
        else:
            self.mid_send(34 + j, part, 1, j - 1)
        self.send(8 + j, part, h.xdev())
        self.send(4 + j, part, h.ydev())

    def along_y(self, j):
        h = self.h
        z = h.near(j)
        part = self.head(z, 1 - h.y, h.x)
        self.wait(4 + j, part)
        self.send(12 + j, part, h.xdev())
        self.send(16 + j, self.pair(z, h.x, h.c), h.sib())

    def along_x(self, j):
        h = self.h
        z = h.near(j)
        self.wait(8 + j, self.head(z, h.y, 1 - h.x))
        self.wait(12 + j, self.head(z, 1 - h.y, 1 - h.x))
        self.send(20 + j, self.pair(z, 1 - h.x, h.c), h.sib())

    def tail_x(self):
        h = self.h
        self.wait(24, self.tail(h.z, h.y, 1 - h.x))
        self.send(25, self.all.at[h.z, h.y, :, h.c, pl.ds(self.cut, self.rows - self.cut)], h.ydev())

    def tail_y(self):
        h = self.h
        self.wait(25, self.all.at[h.z, 1 - h.y, :, h.c, pl.ds(self.cut, self.rows - self.cut)])
        part = self.plane(h.z, h.c)
        self.send(26, part, h.dev(z=h.near(1)))
        self.mid_send(38, part, 2, 27)
        self.send(30, part, h.sib())

    def tail_z(self, j):
        h = self.h
        part = self.plane(h.near(j), h.c)
        self.wait(25 + j, part)
        if j == 1:
            self.mid_send(39, part, 2, 28)
        else:
            self.mid_send(38 + j, part, 1, 25 + j)
        self.send(30 + j, part, h.sib())

    def steps(self):
        p = functools.partial
        x, y, z = self.along_x, self.along_y, self.along_z
        tx, ty, tz = ([p(f)] if self.split else [] for f in (self.tail_x, self.tail_y, self.tail_z))
        order = [self.local.wait, p(y, 0), p(z, 1)] + tx + [p(x, 0), p(z, 2), p(y, 1)] + ty
        order += [p(z, 3), p(x, 1), p(y, 2)] + [p(f, 1) for f in tz] + [p(x, 2), p(y, 3)]
        return order + [p(f, j) for f in tz for j in (2, 3)] + [p(x, 3)]

    def finish(self):
        h = self.h
        c = 1 - h.c
        for j in range(4):
            z = h.near(j)
            self.wait(16 + j, self.pair(z, h.x, c))
            self.wait(20 + j, self.pair(z, 1 - h.x, c))
            if self.split:
                self.wait(30 + j, self.plane(z, c))

    def drain(self):
        for cp in self.mids:
            pl.when(self.h.middle)(lambda cp=cp: cp.wait_send())


class Scatter:
    def __init__(self, h, dw, l1, lxa, lya, lza, lzb, lyb, lxb, ss, rs, out, sent):
        self.h, self.dw, self.l1, self.lxa, self.lya = h, dw, l1, lxa, lya
        self.lza, self.lzb, self.lyb, self.lxb, self.ss, self.rs = lza, lzb, lyb, lxb, ss, rs
        self.out, self.sent = out, sent
        self.all = dw.reshape(4, 2, 2, 2, SHARD, C)
        self.head, self.tail = pl.ds(0, SUM_CUT), pl.ds(SUM_CUT, SHARD - SUM_CUT)

    def at(self, i, lo=0, n=SHARD):
        return self.dw.at[pl.ds(pl.multiple_of(i * SHARD + lo, 16), n)]

    def send(self, k, src, dst, dev):
        cp = rcopy(src, dst, self.ss.at[k], self.rs.at[k], dev)
        cp.start()
        self.sent.append(cp)

    def wait(self, k, land):
        rcopy(land, land, self.ss.at[0], self.rs.at[k], self.h.sib()).wait_recv()

    def add(self, i, lo, n, *parts):
        d = self.at(i, lo, n)
        total = d[...].astype(F32)
        for part in parts:
            total = total + part.astype(F32)
        d[...] = total.astype(BF)

    def s1(self, q):
        self.send(q, self.all.at[q, :, :, 1 - self.h.c], self.l1.at[q], self.h.sib())

    def _far(self, q):
        h = self.h
        return rcopy(
            self.all.at[q, :, :, h.c, self.tail], self.lzb.at[h.z], self.ss.at[16 + q], self.rs.at[20 + h.z], h.dev(z=q)
        )

    def s2(self, q):
        h = self.h
        self.wait(q, self.l1.at[q])
        for j in range(4):
            self.add(h.idx(q, j // 2, j % 2), 0, SHARD, self.l1[q, j // 2, j % 2])
        self.send(4 + q, self.all.at[q, :, 1 - h.x, h.c, self.head], self.lxa.at[q], h.xdev())
        pl.when(h.z != q)(lambda: self._far(q).start())

    def s3(self, q):
        h = self.h
        self.wait(4 + q, self.lxa.at[q])
        for j in range(2):
            self.add(h.idx(q, j), 0, SUM_CUT, self.lxa[q, j])
        self.send(8 + q, self.all.at[q, 1 - h.y, h.x, h.c, self.head], self.lya.at[q], h.ydev())

    def _near(self, q):
        h = self.h
        return rcopy(
            self.all.at[q, h.y, h.x, h.c, self.head], self.lza.at[h.z], self.ss.at[12 + q], self.rs.at[24 + h.z], h.dev(z=q)
        )

    def s4(self, q):
        h = self.h
        self.wait(8 + q, self.lya.at[q])
        self.add(h.idx(q), 0, SUM_CUT, self.lya[q])
        pl.when(h.z != q)(lambda: self._near(q).start())

    def t1(self):
        h = self.h
        for j in (1, 2, 3):
            self.wait(20 + h.near(j), self.lzb.at[h.near(j)])
        for j in range(4):
            parts = [self.lzb[h.near(k), j // 2, j % 2] for k in (1, 2, 3)]
            self.add(h.idx(None, j // 2, j % 2), SUM_CUT, SHARD - SUM_CUT, *parts)
        self.send(28, self.all.at[h.z, 1 - h.y, :, h.c, self.tail], self.lyb, h.ydev())

    def t2(self):
        h = self.h
        self.wait(28, self.lyb)
        for j in range(2):
            self.add(h.idx(None, None, j), SUM_CUT, SHARD - SUM_CUT, self.lyb[j])
        self.send(29, self.all.at[h.z, h.y, 1 - h.x, h.c, self.tail], self.lxb, h.xdev())

    def finish(self, extra):
        h = self.h
        self.wait(29, self.lxb)
        self.out[SUM_CUT:] = (
            self.at(h.idx(), SUM_CUT, SHARD - SUM_CUT)[...].astype(F32) + self.lxb[...].astype(F32) + extra[SUM_CUT:]
        )
        total = self.at(h.idx(), 0, SUM_CUT)[...].astype(F32) + extra[:SUM_CUT]
        for j in (1, 2, 3):
            self.wait(24 + h.near(j), self.lza.at[h.near(j)])
            total = total + self.lza[h.near(j)].astype(F32)
        self.out[:SUM_CUT] = total

    def drain(self):
        for q in range(4):

            @pl.when(self.h.z != q)
            def _(q=q):
                self._near(q).wait_send()
                self._far(q).wait_send()


class Halo:
    def __init__(self, h, edges, land, ss, rs):
        self.h, self.edges, self.land, self.ss, self.rs = h, edges, land, ss, rs
        self.up = rcopy(edges.at[0], land.at[1], ss.at[0], rs.at[0], h.dev(z=h.z - 1))
        self.down = rcopy(edges.at[1], land.at[0], ss.at[1], rs.at[1], h.dev(z=h.z + 1))

    def start_one(self, k):
        to = self.h.z + 2 * k - 1
        cp = rcopy(self.edges.at[k], self.land.at[1 - k], self.ss.at[k], self.rs.at[k], self.h.dev(z=to))
        pl.when((to >= 0) & (to <= 3))(lambda: cp.start())

    def start(self):
        pl.when(self.h.z > 0)(lambda: self.up.start())
        pl.when(self.h.z < 3)(lambda: self.down.start())

    def wait(self):
        @pl.when(self.h.z > 0)
        def _():
            self.up.wait_send()
            self.down.wait_recv()

        @pl.when(self.h.z < 3)
        def _():
            self.down.wait_send()
            self.up.wait_recv()


class Sums:
    def __init__(self, h, buf, ss, rs, sent):
        self.h, self.buf, self.ss, self.rs, self.sent = h, buf, ss, rs, sent

    def start_plane(self, payload):
        h = self.h
        self.own = payload
        mine = self.buf.at[2, 0]
        mine[...] = payload
        for r in (1, 2, 3):
            _, x, c = h.other(0, r // 2, r % 2)
            cp = rcopy(mine, self.buf.at[0, h.gy], self.ss.at[r - 1], self.rs.at[r - 1], h.dev(x=x, c=c))
            cp.start()
            self.sent.append(cp)

    def plane(self):
        h = self.h
        for r in (1, 2, 3):
            _, x, c = h.other(0, r // 2, r % 2)
            land = self.buf.at[0, x * 2 + c]
            rcopy(land, land, self.ss.at[0], self.rs.at[r - 1], h.sib()).wait_recv()
        return [jnp.where(h.gy == g, self.own, self.buf[0, g]) for g in range(4)]

    def start_z(self, payload):
        h = self.h
        self.own = payload
        mine = self.buf.at[2, 1]
        mine[...] = payload
        for j in (1, 2, 3):
            cp = rcopy(mine, self.buf.at[1, h.z], self.ss.at[2 + j], self.rs.at[3 + h.z], h.dev(z=h.near(j)))
            cp.start()
            self.sent.append(cp)

    def along_z(self):
        h = self.h
        for j in (1, 2, 3):
            land = self.buf.at[1, h.near(j)]
            rcopy(land, land, self.ss.at[0], self.rs.at[3 + h.near(j)], h.sib()).wait_recv()
        return [jnp.where(h.z == g, self.own, self.buf[1, g]) for g in range(4)]


def fold(row):
    return [row[:, 128 * k : 128 * (k + 1)] for k in range(4)]


def pack_rows(*rows):
    rows = rows + (jnp.zeros((1, C), F32),) * (4 - len(rows))
    return jnp.concatenate([part for r in rows for part in fold(r)], axis=0)


def unpack_rows(p):
    return [jnp.concatenate([p[4 * n + k : 4 * n + k + 1] for k in range(4)], axis=1) for n in range(p.shape[0] // 4)]


def column(r):
    return jnp.broadcast_to(r, (128, C)).T


def merge(parts, counts):
    total = sum(counts)
    mass = sum(parts[g][0:4] for g in range(4))
    mean = mass / jnp.maximum(total, 1.0)
    spread = jnp.zeros_like(mass)
    for g in range(4):
        n = jnp.maximum(counts[g], 1.0)
        gap = parts[g][0:4] / n - mean
        spread = spread + parts[g][4:8] + counts[g] * gap * gap
    third = parts[0] + parts[1] + parts[2] + parts[3]
    return jnp.concatenate([mass, spread, third[8:16]], axis=0)


def nn(a, b):
    return lax.dot_general(a, b, (((1,), (0,)), ((), ())), preferred_element_type=F32)


def nt(a, b):
    return lax.dot_general(a, b, (((1,), (1,)), ((), ())), preferred_element_type=F32)


def tn(a, b):
    return lax.dot_general(a, b, (((0,), (0,)), ((), ())), preferred_element_type=F32)


def sigmoid(u):
    return 1.0 / (1.0 + jnp.exp(-u))


def body(
    feat, w1s, w2s, gain, bias, head, hbias, labels, heights, widths, picks,
    pooled_out, fg_out, c1_out, c2_out, gg_out, bg_out, hg_out, hbg_out,
    w1, w2, x3, first, second, slope, dh, base, hid, dw,
    al, edges, bland, hland, sland, fland, fgs, fgl,
    e32, exts, ext, gb, stat, pacc, pz, pg, res, cot, yb, ht, gsc, mc1, mc2,
    l1, lxa, lya, lza, lzb, lyb, lxb,
    sem_g, rem_g, sem_ge, rem_ge, sem_l, sem_h, rem_h, sem_s, rem_s, sem_a, rem_a, sem_p, rem_p, sem_r, rem_r,
):
    h = Here()
    sent = []
    z, y = h.z, h.y

    barrier = pltpu.get_barrier_semaphore()
    peers = [h.dev(z=h.near(j)) for j in (1, 2, 3)]
    for r in range(1, 8):
        yy, xx, cc = h.other(r // 4, (r // 2) % 2, r % 2)
        peers.append(h.dev(y=yy, x=xx, c=cc))
    for dev in peers:
        pl.semaphore_signal(barrier, inc=1, device_id=dev, device_id_type=MESH)
    pl.semaphore_wait(barrier, len(peers))

    def swap_rows(lo, n, r, k):
        src = feat.at[pl.ds(PER * (1 - y) + lo, n), r]
        return rcopy(src, al.at[pl.ds(lo, n), r], sem_a.at[4 + k], rem_a.at[4 + k], h.ydev())

    swap = [swap_rows(0, 3, y, 0), swap_rows(3, 3, y, 1)] + [swap_rows(2 * k, 2, 1 - y, 2 + k) for k in range(3)]
    g1 = Gather(h, w1s, w1, sem_g.at[0], rem_g.at[0], sem_l.at[0], SHARD, CUT, sent)
    sent2 = []
    g2 = Gather(h, w2s, w2, sem_g.at[1], rem_g.at[1], sem_l.at[1], SHARD, CUT, sent2)
    ge = Gather(h, exts, ext, sem_ge, rem_ge, sem_l.at[2], 16, 16, sent)
    g1.start()
    swap[0].start()
    swap[1].start()
    e32[...] = jnp.zeros_like(e32)
    place = lax.broadcasted_iota(jnp.int32, (4, 128), 1) // 16
    both = jnp.concatenate([gain[...].astype(F32), bias[...].astype(F32)], axis=0)
    both = jnp.concatenate([both] * 8, axis=1)
    e32[0:4, 0:128] = jnp.where(place == lax.rem(h.idx(), 8), both, 0.0)
    e32[:, 256 : 256 + TASKS] = head[...].astype(F32)
    e32[0:12, 384 : 384 + TASKS] = labels[...].astype(F32)
    exts[...] = e32[...].astype(BF)
    ge.start()

    image = lax.broadcasted_iota(jnp.int32, (1, 8 * PER), 1)
    high = broad = jnp.zeros((1, 8 * PER), jnp.int32)
    for k in range(8 * PER):
        high = jnp.where(image == k, heights[k], high)
        broad = jnp.where(image == k, widths[k], broad)

    def pixels(zz, lo, n):
        here = (image >= lo) & (image < lo + n)
        cells = jnp.where(here, jnp.clip(high - ROWS * zz, 0, ROWS) * broad, 0).astype(F32)
        return cells.sum(1, keepdims=True)

    n_plane = [pixels(z, 2 * PER * g + PER * y, PER) for g in range(4)]
    n_z = [sum(pixels(zz, 2 * PER * g + PER * y, PER) for g in range(4)) for zz in range(4)]
    total = sum(n_z)
    my_first = h.gy * 2 * PER + PER * y

    col = lax.broadcasted_iota(jnp.int32, (COLS, C), 0)

    def wide(i, r):
        return jnp.where(ROWS * z + r < heights[my_first + i], widths[my_first + i], 0)

    def keep(i, r, v):
        return jnp.where(col < wide(i, r), v, 0.0)

    zero8 = jnp.zeros((8, C), F32)

    def by8(v):
        return v.reshape(COLS // 8, 8, C).sum(0)

    def put3(i, row, v):
        x3[i, row, :, C : 2 * C] = v.astype(BF)
        x3[i, row, :, 0:C] = jnp.where(col == 0, 0.0, pltpu.roll(v, 1, 0)).astype(BF)
        x3[i, row, :, 2 * C : 3 * C] = jnp.where(col == COLS - 1, 0.0, pltpu.roll(v, COLS - 1, 0)).astype(BF)

    def put_halo(land):
        def one(i, _):
            @pl.when(z > 0)
            def _():
                put3(i, 0, land[0, i].astype(F32))

            @pl.when(z == 0)
            def _():
                x3[i, 0] = jnp.zeros((COLS, 3 * C), BF)

            @pl.when(z < 3)
            def _():
                put3(i, 5, land[1, i].astype(F32))

            @pl.when(z == 3)
            def _():
                x3[i, 5] = jnp.zeros((COLS, 3 * C), BF)

            return 0

        lax.fori_loop(0, PER, one, 0)

    def take_row(src, offset, r, row, i, acc):
        v = keep(i, row, src[offset + i, r].astype(F32))
        base[i, row] = v.astype(BF)
        put3(i, row + 1, v)
        return acc + by8(v)

    def take_edge(k, src, offset, r, i, acc):
        acc = take_row(src, offset, r, 3 * k, i, acc)
        edges[k, i] = base[i, 3 * k]
        return acc

    halo = Halo(h, edges, bland, sem_h.at[0], rem_h.at[0])
    base_sum = lax.fori_loop(0, PER, lambda i, acc: take_edge(y, feat, PER * y, y, i, acc), zero8)
    halo.start_one(y)
    base_sum = lax.fori_loop(0, PER, lambda i, acc: take_row(feat, PER * y, 1 - y, 1 + y, i, acc), base_sum)

    def edges_in(k, acc):
        swap[k].wait_recv()
        return lax.fori_loop(3 * k, 3 * k + 3, lambda i, acc: take_edge(1 - y, al, 0, 1 - y, i, acc), acc)

    def rows_in(k, acc):
        swap[2 + k].wait_recv()
        return lax.fori_loop(2 * k, 2 * k + 2, lambda i, acc: take_row(al, 0, y, 2 - y, i, acc), acc)

    todo1, late = g1.steps(), 11
    todo2, todoe = [], ge.steps()
    for t, step in enumerate(todo1):
        step()
        if t >= 1 and todoe:
            todoe.pop(0)()
        if t in (2, 4, 6):
            swap[1 + t // 2].start()
        if t == late - 1:
            g2.start()
            todo2 = g2.steps()
        elif t >= late:
            todo2.pop(0)()
        if t == 5:
            base_sum = edges_in(0, base_sum)
        if t == 8:
            base_sum = edges_in(1, base_sum)
            halo.start_one(1 - y)
        if t in (10, 12, 14):
            base_sum = rows_in((t - 10) // 2, base_sum)
    base_sum = base_sum.sum(0, keepdims=True)
    g1.finish()
    steps = todo2
    def go(todo, n):
        for _ in range(min(n, len(todo))):
            todo.pop(0)()

    def conv(w, out, land, halo, todo=()):
        for p in range(3):
            im = pl.ds(2 * p, 2)
            mid = nn(x3[im, 1:5].reshape(8 * COLS, 3 * C), w[3 * C : 6 * C]).reshape(2, 4, COLS, C)
            go(todo, 1)
            lo = nn(x3[im, 1:4].reshape(6 * COLS, 3 * C), w[0 : 3 * C]).reshape(2, 3, COLS, C)
            hi = nn(x3[im, 2:5].reshape(6 * COLS, 3 * C), w[6 * C : 9 * C]).reshape(2, 3, COLS, C)
            out[im, 0] = mid[:, 0] + hi[:, 0]
            out[im, 1] = mid[:, 1] + lo[:, 0] + hi[:, 1]
            out[im, 2] = mid[:, 2] + lo[:, 1] + hi[:, 2]
            out[im, 3] = mid[:, 3] + lo[:, 2]
            go(todo, 1)
        halo.wait()
        go(todo, 1)
        put_halo(land)
        out[:, 0] += nn(x3[:, 0].reshape(6 * COLS, 3 * C), w[0 : 3 * C]).reshape(PER, COLS, C)
        out[:, 3] += nn(x3[:, 5].reshape(6 * COLS, 3 * C), w[6 * C : 9 * C]).reshape(PER, COLS, C)

    def conv_back(w, out, land, halo, todo=()):

        def taps(lhs, a):
            acc = None
            for b in range(3):
                part = nt(lhs[:, (2 - b) * C : (3 - b) * C], w[(3 * a + b) * C : (3 * a + b + 1) * C])
                acc = part if acc is None else acc + part
            return acc

        for p in range(3):
            im = pl.ds(2 * p, 2)
            mid = taps(x3[im, 1:5].reshape(8 * COLS, 3 * C), 1).reshape(2, 4, COLS, C)
            lo = taps(x3[im, 1:4].reshape(6 * COLS, 3 * C), 2).reshape(2, 3, COLS, C)
            hi = taps(x3[im, 2:5].reshape(6 * COLS, 3 * C), 0).reshape(2, 3, COLS, C)
            out[im, 0] = mid[:, 0] + hi[:, 0]
            out[im, 1] = mid[:, 1] + lo[:, 0] + hi[:, 1]
            out[im, 2] = mid[:, 2] + lo[:, 1] + hi[:, 2]
            out[im, 3] = mid[:, 3] + lo[:, 2]
            if todo:
                todo[p]()
        halo.wait()
        put_halo(land)
        out[:, 0] += taps(x3[:, 0].reshape(6 * COLS, 3 * C), 2).reshape(PER, COLS, C)
        out[:, 3] += taps(x3[:, 5].reshape(6 * COLS, 3 * C), 0).reshape(PER, COLS, C)

    def spread(src):
        def one(i, carry):
            n, mean, dev = carry
            widths_i = [wide(i, r) for r in range(ROWS)]
            ni = sum(widths_i).astype(F32)
            mass = jnp.zeros((8, C), F32)
            for r in range(ROWS):
                v = jnp.where(col < widths_i[r], src[i, r], 0.0)
                mass = mass + v.reshape(COLS // 8, 8, C).sum(0)
            mi = mass.sum(0, keepdims=True) / jnp.maximum(ni, 1.0)
            sq = jnp.zeros((8, C), F32)
            for r in range(ROWS):
                v = jnp.where(col < widths_i[r], src[i, r] - mi, 0.0)
                sq = sq + (v * v).reshape(COLS // 8, 8, C).sum(0)
            both = jnp.maximum(n + ni, 1.0)
            gap = mi - mean
            return (
                n + ni,
                mean + gap * (ni / both),
                dev + sq.sum(0, keepdims=True) + gap * gap * (n * ni / both),
            )

        zero = jnp.zeros((1, C), F32)
        n, mean, dev = lax.fori_loop(0, PER, one, (jnp.float32(0.0), zero, zero))
        return mean * n, dev

    def statistics(src, k, todo, inputs):
        ex = Sums(h, stat.at[k], sem_s.at[k], rem_s.at[k], sent)
        ex.start_plane(pack_rows(*spread(src), inputs))
        go(todo, 1)
        ex.start_z(merge(ex.plane(), n_plane))
        go(todo, 1)
        both = merge(ex.along_z(), n_z)
        mass, dev, inputs, _ = unpack_rows(both)
        return mass / total, lax.rsqrt(dev / total + norm_eps), inputs / total

    def start_sums(k, *rows):
        ex = Sums(h, stat.at[k], sem_s.at[k], rem_s.at[k], sent)
        ex.start_plane(pack_rows(*rows))
        return ex

    def mid_sums(ex):
        parts = ex.plane()
        ex.start_z(parts[0] + parts[1] + parts[2] + parts[3])

    def end_sums(ex):
        parts = ex.along_z()
        return parts[0] + parts[1] + parts[2] + parts[3]

    def edges_first(one, start):
        def edge(i, acc):
            for k, r in enumerate((0, ROWS - 1)):
                v = one(i, r)
                edges[k, i] = v.astype(BF)
                acc = acc + by8(v)
            return acc

        def inner(i, acc):
            for r in range(1, ROWS - 1):
                acc = acc + by8(one(i, r))
            return acc

        acc = lax.fori_loop(0, PER, edge, zero8)
        start()
        return lax.fori_loop(0, PER, inner, acc).sum(0, keepdims=True)

    conv(w1, first, bland, halo, steps)
    center, rs1, base_mean = statistics(first, 0, steps, base_sum)
    go(steps, 99)
    ge.finish()

    for k in range(4):
        tile = sum(ext[16 * d : 16 * d + 16, 0:128].astype(F32) for d in range(8 * k, 8 * k + 8))
        gb[0:4, 128 * k : 128 * (k + 1)] = tile[0:4]
    ht[...] = ext[:, 256:384].astype(F32)
    gain1, bias1 = gb[0:1], gb[2:3]

    def hidden(i, r):
        xh = (first[i, r] - center) * rs1
        first[i, r] = xh
        u = gain1 * xh + bias1
        v = keep(i, r, u * sigmoid(u))
        hid[i, r] = v.astype(BF)
        put3(i, r + 1, v)
        return v

    halo = Halo(h, edges, hland, sem_h.at[1], rem_h.at[1])
    hid_sum = edges_first(hidden, halo.start)
    g2.finish()
    conv(w2, second, hland, halo, [])
    center, rs2, hid_mean = statistics(second, 1, [], hid_sum)
    gain2, bias2 = gb[1:2], gb[3:4]

    pacc[...] = jnp.zeros_like(pacc)

    def finals(i, _):
        acc = [jnp.zeros((8, C), F32) for _ in range(3)]
        for r in range(ROWS):
            xh = (second[i, r] - center) * rs2
            second[i, r] = xh
            pre = gain2 * xh + bias2 + base[i, r].astype(F32)
            s = sigmoid(pre)
            act = keep(i, r, pre * s)
            sl = keep(i, r, s * (1.0 + pre * (1.0 - s)))
            slope[i, r] = sl
            for k, v in enumerate((act, sl, sl * xh)):
                acc[k] = acc[k] + v.reshape(COLS // 8, 8, C).sum(0)
        for k in range(3):
            pacc[k, pl.ds(i, 1)] = acc[k].sum(0, keepdims=True)
        return 0

    lax.fori_loop(0, PER, finals, 0)

    rows8 = lax.broadcasted_iota(jnp.int32, (8, 1), 0)
    inv_pix = jnp.zeros((8, 1), F32)
    for i in range(PER):
        inv_pix = jnp.where(rows8 == i, 1.0 / (heights[my_first + i] * widths[my_first + i]).astype(F32), inv_pix)
    me_z = pz.at[z]
    me_z[...] = pacc[0]
    for j in (1, 2, 3):
        cp = rcopy(me_z, me_z, sem_p.at[j - 1], rem_p.at[z], h.dev(z=h.near(j)))
        cp.start()
        sent.append(cp)
    head_gram = lax.dot_general(ht[...], ht[...], (((0,), (0,)), ((), ())), precision=HIGH, preferred_element_type=F32)
    for j in (1, 2, 3):
        land = pz.at[h.near(j)]
        rcopy(land, land, sem_p.at[0], rem_p.at[h.near(j)], h.sib()).wait_recv()
    slot = (y * 2 + h.x) * 2 + h.c
    me_p = pg.at[slot]
    me_p[...] = (pz[0] + pz[1] + pz[2] + pz[3]) * inv_pix
    for r in range(1, 8):
        yy, xx, cc = h.other(r // 4, (r // 2) % 2, r % 2)
        cp = rcopy(me_p, me_p, sem_p.at[2 + r], rem_p.at[3 + r], h.dev(y=yy, x=xx, c=cc))
        cp.start()
        sent.append(cp)
    lane = lax.broadcasted_iota(jnp.int32, (8, 128), 1)
    row = lax.broadcasted_iota(jnp.int32, (8, 128), 0)
    real = (row < PER) & (lane < TASKS)
    wanted = []
    for s in range(8):
        yy, gy = s // 4, s % 4
        lab = ext[16 * gy : 16 * gy + 16, 384:512].astype(F32)
        lab = lab[PER * yy : PER * yy + PER]
        wanted.append(jnp.concatenate([lab, jnp.zeros((2, 128), F32)], axis=0))
    for r in range(1, 8):
        yy, xx, cc = h.other(r // 4, (r // 2) % 2, r % 2)
        land = pg.at[(yy * 2 + xx) * 2 + cc]
        rcopy(land, land, sem_p.at[0], rem_p.at[3 + r], h.sib()).wait_recv()
    pooled = pg[...].reshape(64, C)
    offset = jnp.concatenate([hbias[...].astype(F32), jnp.zeros((1, 128 - TASKS), F32)], axis=1)
    logits = lax.dot_general(pooled, ht[...], (((1,), (0,)), ((), ())), precision=HIGH, preferred_element_type=F32)
    logits = logits.reshape(8, 8, 128) + offset
    images = 8 * PER
    for s in range(8):
        res[s] = jnp.where(real, (sigmoid(logits[s]) - wanted[s]) / images, 0.0)
    residual = res[...].reshape(64, 128)
    gram = head_gram * lax.dot_general(
        residual, residual, (((0,), (0,)), ((), ())), precision=HIGH, preferred_element_type=F32
    )
    gram = gram[0:TASKS]
    lane1 = lax.broadcasted_iota(jnp.int32, (1, 128), 1)
    sub = lax.broadcasted_iota(jnp.int32, (TASKS, 128), 0)

    def fw(k, carry):
        mix, q = carry
        t = picks[k]
        one = (lane1 == t).astype(F32)
        line = jnp.where(sub == t, gram, 0.0).sum(0, keepdims=True)
        self_dot = (mix * q).sum(1, keepdims=True)
        cross = (one * q).sum(1, keepdims=True)
        vertex = (one * line).sum(1, keepdims=True)
        d = jnp.maximum(self_dot + vertex - 2.0 * cross, 0.1 * vertex)
        step = jnp.clip((self_dot - cross) / d, 0.0, 1.0)
        return (1.0 - step) * mix + step * one, (1.0 - step) * q + step * line

    mix0 = jnp.where(lane1 < TASKS, 1.0 / TASKS, 0.0)
    mix, _ = lax.fori_loop(0, STEPS, fw, (mix0, gram.sum(0, keepdims=True) / TASKS))
    mine = res[slot] * mix
    cot[...] = inv_pix * lax.dot_general(
        mine, ht[...], (((1,), (1,)), ((), ())), precision=HIGH, preferred_element_type=F32
    )
    ex = start_sums(
        2, (cot[...] * pacc[1]).sum(0, keepdims=True), (cot[...] * pacc[2]).sum(0, keepdims=True)
    )

    for yy in range(2):
        pooled_out[PER * yy : PER * (yy + 1)] = pg[(yy * 2 + h.x) * 2 + h.c][0:PER]
    head_grad = lax.dot_general(
        pooled, residual, (((0,), (0,)), ((), ())), precision=HIGH, preferred_element_type=F32
    )
    mid_sums(ex)
    gsc[...] = head_grad
    hg_out[...] = gsc[pl.ds(pl.multiple_of(h.idx() * 16, 16), 16)][:, 0:TASKS]
    hbg_out[...] = residual.sum(0, keepdims=True)[:, 0:TASKS]
    sums2 = end_sums(ex)
    yb[0, 0:8] = sums2[0:8]
    mc1[0:C] = column(base_mean)
    mc1[C:] = mc1[0:256]
    mc2[0:C] = column(hid_mean)
    mc2[C:] = mc2[0:256]
    yb[0, 24:32] = pack_rows(hid_mean, base_mean)[0:8]

    sum_b, sum_g, _, _ = unpack_rows(sums2)
    mean_b, mean_g = sum_b / total, sum_g / total
    scale = gain2 * rs2

    def d_second(i, r):
        xh = second[i, r]
        dp = slope[i, r] * cot[pl.ds(i, 1)]
        v = keep(i, r, scale * (dp - mean_b - xh * mean_g))
        put3(i, r + 1, v)
        return v.astype(BF).astype(F32)

    halo = Halo(h, edges, sland, sem_h.at[2], rem_h.at[2])
    d2_sum = edges_first(d_second, halo.start)
    conv_back(w2, dh, sland, halo)

    def d_norm1(i, carry):
        a, b = carry
        for r in range(ROWS):
            xh = first[i, r]
            u = gain1 * xh + bias1
            s = sigmoid(u)
            v = keep(i, r, dh[i, r] * (s * (1.0 + u * (1.0 - s))))
            dh[i, r] = v
            a = a + v.reshape(COLS // 8, 8, C).sum(0)
            b = b + (v * xh).reshape(COLS // 8, 8, C).sum(0)
        return a, b

    a, b = lax.fori_loop(0, PER, d_norm1, (zero8, zero8))
    ex = start_sums(3, a.sum(0, keepdims=True), b.sum(0, keepdims=True), d2_sum)

    def weight_taps(x, out, mean, d_sum, lo, hi):
        for t in range(lo, hi):
            ta, tb = t // 3, t % 3
            d = x3[:, 2 - ta : 6 - ta, :, (2 - tb) * C : (3 - tb) * C].reshape(PER * ROWS * COLS, C)
            part = tn(x[...].reshape(PER * ROWS * COLS, C), d)
            off = jnp.concatenate([mean[0:C] * f for f in fold(d_sum)], axis=1)
            out[t * C : (t + 1) * C] = (part - off).astype(BF)

    def scatter(k, src, out):
        return Scatter(
            h, src, l1.at[k], lxa.at[k], lya.at[k], lza.at[k], lzb.at[k], lyb.at[k], lxb.at[k], sem_r.at[k], rem_r.at[k],
            out, sent,
        )

    r2 = scatter(0, dw, c2_out)
    weight_taps(hid, dw, mc2, d2_sum, 0, 3)
    r2.s1(0)
    mid_sums(ex)
    weight_taps(hid, dw, mc2, d2_sum, 3, 5)
    r2.s1(1)
    r2.s2(0)
    weight_taps(hid, dw, mc2, d2_sum, 5, 7)
    r2.s1(2)
    r2.s2(1)
    weight_taps(hid, dw, mc2, d2_sum, 7, 9)
    r2.s1(3)
    r2.s2(2)
    sums1 = end_sums(ex)
    yb[0, 8:20] = sums1[0:12]
    sum_b, sum_g, _, _ = unpack_rows(sums1)
    mean_b1, mean_g1 = sum_b / total, sum_g / total
    scale1 = gain1 * rs1

    def d_first(i, r):
        v = keep(i, r, scale1 * (dh[i, r] - mean_b1 - first[i, r] * mean_g1))
        put3(i, r + 1, v)
        return v.astype(BF).astype(F32)

    halo = Halo(h, edges, fland, sem_h.at[3], rem_h.at[3])
    d1_sum = edges_first(d_first, halo.start)
    r2.s2(3)
    ex = start_sums(4, d1_sum)
    conv_back(w1, dh, fland, halo, [functools.partial(r2.s3, q) for q in range(3)])
    mid_sums(ex)
    r2.s4(0)

    def result(i, r):
        return keep(i, r, dh[i, r] + slope[i, r] * cot[pl.ds(i, 1)])

    back = []
    for p in range(3):
        for i in (2 * p, 2 * p + 1):
            for r in range(2):
                fgs[i, r] = result(i, 2 * (1 - y) + r).astype(BF)
        im = pl.ds(2 * p, 2)
        cp = rcopy(fgs.at[im], fgl.at[im], sem_a.at[1 + p], rem_a.at[1 + p], h.ydev())
        cp.start()
        back.append(cp)

    def stay(i, _):
        for r in range(2):
            fg_out[PER * y + i, r] = result(i, 2 * y + r).astype(BF)
        return 0

    lax.fori_loop(0, PER, stay, 0)
    r2.s3(3)
    r2.s4(1)
    yb[0, 20:24] = end_sums(ex)[0:4]
    ysum = rcopy(yb.at[0], yb.at[1], sem_a.at[0], rem_a.at[0], h.ydev())
    ysum.start()

    for cp in sent2:
        cp.wait_send()
    g2.drain()
    r1 = scatter(1, w2, c1_out)
    weight_taps(base, w2, mc1, d1_sum, 0, 3)
    r1.s1(0)
    r2.s4(2)
    weight_taps(base, w2, mc1, d1_sum, 3, 5)
    r1.s1(1)
    r1.s2(0)
    r2.s4(3)
    r2.t1()
    weight_taps(base, w2, mc1, d1_sum, 5, 7)
    r1.s1(2)
    r1.s2(1)
    r2.t2()
    weight_taps(base, w2, mc1, d1_sum, 7, 9)
    r1.s1(3)
    r1.s2(2)

    ysum.wait_recv()
    sb2, sg2, sb1, sg1 = unpack_rows(yb[0, 0:16] + yb[1, 0:16])
    tile = jnp.zeros((4, 128), F32)
    for k in range(4):
        rows = [v[:, 128 * k : 128 * (k + 1)] for v in (sg1, sg2, sb1, sb2)]
        tile = jnp.where(lax.div(h.idx(), 8) == k, jnp.concatenate(rows, axis=0), tile)
    own = jnp.zeros((4, 16), F32)
    for k in range(8):
        own = jnp.where(lax.rem(h.idx(), 8) == k, tile[:, 16 * k : 16 * (k + 1)], own)
    gg_out[...] = own[0:2]
    bg_out[...] = own[2:4]

    r1.s2(3)
    r1.s3(0)

    at = pl.ds(pl.multiple_of(lax.rem(h.idx() * SHARD, C), 16), SHARD)
    d2_all, d1_all, hid_other, base_other = unpack_rows(yb[1, 16:32])
    d2_mine, d1_mine, _, _ = unpack_rows(yb[0, 16:32])

    def taken_off(mean, other, all_mine, all_other):
        off = jnp.concatenate([mean[at] * f for f in fold(all_mine)], axis=1)
        mean[0:C] = column(other)
        mean[C:] = mean[0:256]
        return off + jnp.concatenate([mean[at] * f for f in fold(all_other)], axis=1)

    off2 = taken_off(mc2, hid_other, d2_mine, d2_all)
    off1 = taken_off(mc1, base_other, d1_mine, d1_all)
    r2.finish(off2)
    r1.s3(1)
    r1.s4(0)

    def land_rows(p):
        back[p].wait_recv()
        for i in (2 * p, 2 * p + 1):
            fg_out[PER * (1 - y) + i] = fgl[i]

    land_rows(0)
    r1.s3(2)
    r1.s4(1)
    r1.t1()
    land_rows(1)
    r1.s3(3)
    r1.s4(2)
    r1.t2()
    land_rows(2)
    r1.s4(3)
    r1.finish(off1)

    ysum.wait_send()
    g1.drain()
    ge.drain()
    for cp in swap + back + sent:
        cp.wait_send()
    r1.drain()
    r2.drain()


def fused(features, w1s, w2s, gain, bias, head, head_bias, labels, heights, widths, picks):
    vm = pl.BlockSpec(memory_space=pltpu.VMEM)
    sm = pl.BlockSpec(memory_space=pltpu.SMEM)
    V = pltpu.VMEM
    dma = pltpu.SemaphoreType.DMA
    maps = (PER, ROWS, COLS, C)
    edge = (2, PER, COLS, C)
    half = (PER, 2, COLS, C)
    scratch = [
        V((9 * C, C), BF), V((9 * C, C), BF), V((PER, ROWS + 2, COLS, 3 * C), BF),
        V(maps, F32), V(maps, F32), V(maps, F32), V(maps, F32), V(maps, BF), V(maps, BF), V((9 * C, C), BF),
        V(half, BF), V(edge, BF), V(edge, BF), V(edge, BF), V(edge, BF), V(edge, BF), V(half, BF), V(half, BF),
        V((16, C), F32), V((16, C), BF), V((C, C), BF), V((8, C), F32),
        V((5, 3, 4, 16, 128), F32), V((3, 8, C), F32), V((4, 8, C), F32), V((8, 8, C), F32),
        V((8, 8, 128), F32), V((8, C), F32), V((2, 32, 128), F32), V((C, 128), F32), V((C, 128), F32),
        V((C + 256, 128), F32), V((C + 256, 128), F32),
        V((2, 4, 2, 2, SHARD, C), BF), V((2, 4, 2, SUM_CUT, C), BF), V((2, 4, SUM_CUT, C), BF), V((2, 4, SUM_CUT, C), BF),
        V((2, 4, 2, 2, SHARD - SUM_CUT, C), BF), V((2, 2, SHARD - SUM_CUT, C), BF), V((2, SHARD - SUM_CUT, C), BF),
        dma((2, 48)), dma((2, 48)), dma((48,)), dma((48,)), dma((3,)), dma((4, 2)), dma((4, 2)),
        dma((5, 8)), dma((5, 8)), dma((10,)), dma((10,)), dma((12,)), dma((12,)), dma((2, 48)), dma((2, 48)),
    ]
    f = jax.ShapeDtypeStruct
    outs = pl.pallas_call(
        body,
        out_shape=[
            f((2 * PER, C), F32), f((2 * PER, 2, COLS, C), BF), f((SHARD, C), F32), f((SHARD, C), F32),
            f((2, 16), F32), f((2, 16), F32), f((16, TASKS), F32), f((1, TASKS), F32),
        ],
        in_specs=[vm] * 8 + [sm] * 3,
        out_specs=[vm] * 8,
        scratch_shapes=scratch,
        compiler_params=pltpu.CompilerParams(
            collective_id=0, has_side_effects=True, vmem_limit_bytes=63 * 2**20
        ),
        name="block",
    )(
        features, w1s, w2s, gain.T, bias.T, head, head_bias.reshape(1, TASKS), labels, heights, widths, picks,
    )
    pooled, fg, c1, c2, gg, bg, hg, hbg = outs
    return pooled, fg.astype(F32), c1, c2, gg.T, bg.T, hg, hbg.reshape(TASKS)


def extended(cells, sides, width):
    for axis, dim in sides:
        count = lax.axis_size(axis)
        ends = count - 1
        head = lax.slice_in_dim(cells, 0, width, axis=dim)
        tail = lax.slice_in_dim(cells, cells.shape[dim] - width, cells.shape[dim], axis=dim)
        cells = jnp.concatenate(
            [
                lax.ppermute(tail, axis, [(i, (i + 1) % count) for i in range(ends)]),
                cells,
                lax.ppermute(head, axis, [((i + 1) % count, i) for i in range(ends)]),
            ],
            axis=dim,
        )
    return cells


def make_patches(padded, row_count, col_count):
    widened = jnp.pad(padded, ((0, 0), (0, 0), (1, 1), (0, 0)))
    pieces = [
        widened[:, row_off : row_off + row_count, col_off : col_off + col_count, :]
        for row_off in range(3)
        for col_off in range(3)
    ]
    joined = jnp.concatenate(pieces, axis=-1)
    return joined.reshape(-1, joined.shape[-1])


def conv_rows(act, weight):
    padded = extended(act, (("gx", 1),), 1)
    patches = make_patches(padded, act.shape[1], act.shape[2])
    output = jnp.dot(patches, weight, preferred_element_type=jnp.float32)
    return (output.reshape(act.shape[:3] + (weight.shape[1],)), padded)


def reversed_taps(weight):
    channels = weight.shape[1]
    taps = weight.reshape(9, channels, channels)[::-1]
    return jnp.transpose(taps, (0, 2, 1)).reshape(9 * channels, channels)


def weight_term(padded, grad_bf):
    patches = make_patches(padded, grad_bf.shape[1], grad_bf.shape[2])
    flat_grad = grad_bf.reshape(-1, grad_bf.shape[-1])
    return lax.dot_general(
        patches, flat_grad, (((0,), (0,)), ((), ())), preferred_element_type=jnp.float32
    )


def batch_statistics(values, inner_result, pixel_total):
    center_val = (
        lax.psum(jnp.sum(values * inner_result, axis=(0, 1, 2)), ("gx", "gy")) / pixel_total
    )
    centered = values - center_val
    spread_sq = (
        lax.psum(jnp.sum(inner_result * centered * centered, axis=(0, 1, 2)), ("gx", "gy"))
        / pixel_total
    )
    inverse_scale = lax.rsqrt(spread_sq + norm_eps)
    return (centered * inverse_scale, inverse_scale)


def norm_backward(
    output_gradient, normalized_input, inverse_scale, norm_scale_factor, inner_result, pixel_total
):
    bias_gradient_total, scale_gradient_total = lax.psum(
        (
            jnp.sum(output_gradient, axis=(0, 1, 2)),
            jnp.sum(output_gradient * normalized_input, axis=(0, 1, 2)),
        ),
        ("gx", "gy"),
    )
    backward_result = (
        norm_scale_factor
        * inverse_scale
        * (
            output_gradient
            - bias_gradient_total / pixel_total
            - normalized_input * scale_gradient_total / pixel_total
        )
        * inner_result
    )
    return (backward_result, scale_gradient_total, bias_gradient_total)


def silu_slope(values):
    sig_val = jax.nn.sigmoid(values)
    return sig_val * (1.0 + values * (1.0 - sig_val))


def frank_wolfe(gram, picks):
    task_ids = jnp.arange(TASKS)

    def fw_step(index, task_mix):
        onehot = (task_ids == picks[index]).astype(jnp.float32)
        mixed_vec = jnp.dot(gram, task_mix, precision=lax.Precision.HIGHEST)
        self_dot = jnp.sum(task_mix * mixed_vec)
        cross_dot = jnp.sum(onehot * mixed_vec)
        vertex_dot = jnp.sum(onehot * jnp.dot(gram, onehot, precision=lax.Precision.HIGHEST))
        distance = jnp.maximum(self_dot + vertex_dot - 2.0 * cross_dot, 0.1 * vertex_dot)
        step_size = jnp.clip((self_dot - cross_dot) / distance, 0.0, 1.0)
        return (1.0 - step_size) * task_mix + step_size * onehot

    start = jnp.full((TASKS,), 1.0 / TASKS, jnp.float32)
    return lax.fori_loop(0, STEPS, fw_step, start)


def on_device(
    features,
    conv1_weight,
    conv2_weight,
    norm_gain,
    norm_bias,
    head_weight,
    head_bias,
    labels,
    heights,
    widths,
    picks,
):
    image_count, row_count, col_count, channels = features.shape
    per_micro = image_count // MICRO
    total_images = image_count * lax.axis_size("gy")
    row_ids = lax.axis_index("gx") * row_count + jnp.arange(row_count)
    my_heights = lax.dynamic_slice_in_dim(heights, lax.axis_index("gy") * image_count, image_count)
    my_widths = lax.dynamic_slice_in_dim(widths, lax.axis_index("gy") * image_count, image_count)
    inside_all = (
        (row_ids[None, :, None] < my_heights[:, None, None])
        & (jnp.arange(col_count)[None, None, :] < my_widths[:, None, None])
    ).astype(jnp.float32)[..., None]
    pixel_count = (my_heights * my_widths).astype(jnp.float32)
    micro_pixels = jnp.sum((heights * widths).reshape(-1, MICRO, per_micro), axis=(0, 2)).astype(
        jnp.float32
    )

    def weights_now():
        return (
            lax.all_gather(conv1_weight, ("gx", "gy"), axis=0, tiled=True),
            lax.all_gather(conv2_weight, ("gx", "gy"), axis=0, tiled=True),
            lax.all_gather(norm_gain, ("gx", "gy"), axis=0, tiled=True),
            lax.all_gather(norm_bias, ("gx", "gy"), axis=0, tiled=True),
            lax.all_gather(head_weight, ("gx", "gy"), axis=0, tiled=True),
        )

    saved = []
    pooled_parts = []
    head_full = None
    for index in range(MICRO):
        conv_one, conv_two, gain_full, bias_full, head_full = weights_now()
        scale_factors = gain_full.astype(jnp.float32)
        bias_values = bias_full.astype(jnp.float32)
        inner_result = inside_all[index * per_micro : (index + 1) * per_micro]
        pixel_total = micro_pixels[index]
        base_input_bfloat = features[
            index * per_micro : (index + 1) * per_micro
        ] * inner_result.astype(jnp.bfloat16)
        first_convolution, padded_input = conv_rows(base_input_bfloat, conv_one)
        first_normalized, first_scale = batch_statistics(
            first_convolution, inner_result, pixel_total
        )
        first_norm_output = scale_factors[:, 0] * first_normalized + bias_values[:, 0]
        hidden_bf = (jax.nn.silu(first_norm_output) * inner_result).astype(jnp.bfloat16)
        second_convolution, padded_hidden_state = conv_rows(hidden_bf, conv_two)
        second_normalized, second_scale = batch_statistics(
            second_convolution, inner_result, pixel_total
        )
        before_activation = (
            scale_factors[:, 1] * second_normalized
            + bias_values[:, 1]
            + base_input_bfloat.astype(jnp.float32)
        )
        final_act = jax.nn.silu(before_activation) * inner_result
        pooled_parts.append(jnp.sum(final_act, axis=(1, 2)))
        saved.append(
            (
                padded_input,
                padded_hidden_state,
                first_normalized,
                first_scale,
                first_norm_output,
                second_normalized,
                second_scale,
                before_activation,
            )
        )
    pooled = lax.psum(jnp.concatenate(pooled_parts, axis=0), "gx") / pixel_count[:, None]
    head_mat = head_full.astype(jnp.float32)
    logits = jnp.dot(pooled, head_mat, precision=lax.Precision.HIGHEST) + head_bias.astype(
        jnp.float32
    )
    residual = (jax.nn.sigmoid(logits) - labels.astype(jnp.float32)) / total_images
    gram_part = jnp.dot(residual.T, residual, precision=lax.Precision.HIGHEST)
    head_part = jnp.dot(pooled.T, residual, precision=lax.Precision.HIGHEST)
    gram_sum, head_bias_grad, head_total = (
        lax.psum(gram_part.astype(jnp.bfloat16), "gy").astype(jnp.float32),
        lax.psum(jnp.sum(residual, axis=0).astype(jnp.bfloat16), "gy").astype(jnp.float32),
        lax.psum(head_part.astype(jnp.bfloat16), "gy").astype(jnp.float32),
    )
    gram = gram_sum * jnp.dot(head_mat.T, head_mat, precision=lax.Precision.HIGHEST)
    task_mix = frank_wolfe(gram, picks)
    pooled_cot = jnp.dot(residual * task_mix, head_mat.T, precision=lax.Precision.HIGHEST)
    shard_rows = 9 * channels // lax.axis_size(("gx", "gy"))
    conv1_grad = jnp.zeros((shard_rows, channels), jnp.float32)
    conv2_grad = jnp.zeros((shard_rows, channels), jnp.float32)
    gain_total = jnp.zeros((channels, 2), jnp.float32)
    bias_total = jnp.zeros((channels, 2), jnp.float32)
    feat_parts = []
    for index in range(MICRO):
        conv_one, conv_two, gain_full, bias_full, unused_heads = weights_now()
        scale_factors = gain_full.astype(jnp.float32)
        (
            padded_input,
            padded_hidden_state,
            first_normalized,
            first_scale,
            first_norm_output,
            second_normalized,
            second_scale,
            before_activation,
        ) = saved[index]
        inner_result = inside_all[index * per_micro : (index + 1) * per_micro]
        pixel_total = micro_pixels[index]
        cot_part = (
            pooled_cot[index * per_micro : (index + 1) * per_micro]
            / pixel_count[index * per_micro : (index + 1) * per_micro, None]
        )
        gradient_before_relu = (
            cot_part[:, None, None, :] * inner_result * silu_slope(before_activation)
        )
        d_second, gain_two, bias_two = norm_backward(
            gradient_before_relu,
            second_normalized,
            second_scale,
            scale_factors[:, 1],
            inner_result,
            pixel_total,
        )
        second_bf = d_second.astype(jnp.bfloat16)
        term_two = weight_term(padded_hidden_state, second_bf)
        d_hidden, unused_pad = conv_rows(second_bf, reversed_taps(conv_two))
        gradient_norm_first = d_hidden * inner_result * silu_slope(first_norm_output)
        d_first, gain_one, bias_one = norm_backward(
            gradient_norm_first,
            first_normalized,
            first_scale,
            scale_factors[:, 0],
            inner_result,
            pixel_total,
        )
        first_bf = d_first.astype(jnp.bfloat16)
        term_one = weight_term(padded_input, first_bf)
        d_base, unused_pad_two = conv_rows(first_bf, reversed_taps(conv_one))
        feat_parts.append((d_base + gradient_before_relu) * inner_result)
        gain_total = gain_total + jnp.stack([gain_one, gain_two], axis=1)
        bias_total = bias_total + jnp.stack([bias_one, bias_two], axis=1)
        shard_one, shard_two = (
            lax.psum_scatter(term_one, ("gx", "gy"), scatter_dimension=0, tiled=True),
            lax.psum_scatter(term_two, ("gx", "gy"), scatter_dimension=0, tiled=True),
        )
        conv1_grad = conv1_grad + shard_one
        conv2_grad = conv2_grad + shard_two
    flat_index = lax.axis_index(("gx", "gy"))
    chan_rows = channels // lax.axis_size(("gx", "gy"))
    gain_grad = lax.dynamic_slice_in_dim(gain_total, flat_index * chan_rows, chan_rows, 0)
    bias_grad = lax.dynamic_slice_in_dim(bias_total, flat_index * chan_rows, chan_rows, 0)
    head_grad = lax.dynamic_slice_in_dim(head_total, flat_index * chan_rows, chan_rows, 0)
    features_grad = jnp.concatenate(feat_parts, axis=0)
    return (
        pooled,
        features_grad,
        conv1_grad,
        conv2_grad,
        gain_grad,
        bias_grad,
        head_grad,
        head_bias_grad,
    )


def solution(mesh):
    in_specs = (
        P("gy", "gx", None, None),
        P(("gx", "gy"), None),
        P(("gx", "gy"), None),
        P(("gx", "gy"), None),
        P(("gx", "gy"), None),
        P(("gx", "gy"), None),
        P(),
        P("gy", None),
        P(),
        P(),
        P(),
    )
    out_specs = (
        P("gy", None),
        P("gy", "gx", None, None),
        P(("gx", "gy"), None),
        P(("gx", "gy"), None),
        P(("gx", "gy"), None),
        P(("gx", "gy"), None),
        P(("gx", "gy"), None),
        P(),
    )
    whole = dict(mesh.shape) != {"gx": 8, "gy": 4}
    return jax.shard_map(
        on_device if whole else fused, mesh=mesh, in_specs=in_specs, out_specs=out_specs, check_vma=False
    )
```

```python
import functools

import jax
import jax.numpy as jnp
from jax import lax
from jax.experimental import pallas as pl
from jax.experimental.pallas import tpu as pltpu
from jax.sharding import PartitionSpec as P

TASKS = 40
MICRO = 2
STEPS = 20
norm_eps = 1e-05
BF = jnp.bfloat16
F32 = jnp.float32
HIGH = lax.Precision.HIGHEST
MESH = pl.DeviceIdType.MESH

C = 512
COLS = 64
PER = 6
ROWS = 4
SHARD = 144
CUT = 112
SUM_CUT = 112


class Here:
    def __init__(self):
        gx = lax.axis_index("gx")
        gy = lax.axis_index("gy")
        self.z = lax.div(gx, 2)
        self.y = lax.rem(gx, 2)
        self.x = lax.div(gy, 2)
        self.c = lax.rem(gy, 2)
        self.gy = gy
        self.middle = lax.rem(self.z + 1, 4) >= 2

    def _fill(self, z, y, x, c):
        return (
            self.z if z is None else z,
            self.y if y is None else y,
            self.x if x is None else x,
            self.c if c is None else c,
        )

    def dev(self, z=None, y=None, x=None, c=None):
        z, y, x, c = self._fill(z, y, x, c)
        return {"gx": z * 2 + y, "gy": x * 2 + c}

    def idx(self, z=None, y=None, x=None, c=None):
        z, y, x, c = self._fill(z, y, x, c)
        return ((z * 2 + y) * 2 + x) * 2 + c

    def near(self, j):
        z = self.z
        if j == 0:
            return z
        if j == 1:
            return z + 1 - 2 * lax.rem(z, 2)
        if j == 2:
            return 2 - lax.div(z, 2)
        return 3 - 3 * lax.div(z, 2)

    def other(self, dy, dx, dc):
        return (
            1 - self.y if dy else self.y,
            1 - self.x if dx else self.x,
            1 - self.c if dc else self.c,
        )

    def ydev(self):
        return self.dev(y=1 - self.y)

    def xdev(self):
        return self.dev(x=1 - self.x)

    def sib(self):
        return self.dev(c=1 - self.c)


def rcopy(src, dst, ss, rs, dev):
    return pltpu.make_async_remote_copy(
        src_ref=src, dst_ref=dst, send_sem=ss, recv_sem=rs, device_id=dev, device_id_type=MESH
    )


class Gather:
    def __init__(self, h, own, out, ss, rs, lsem, rows, cut, sent):
        self.h, self.own, self.ss, self.rs = h, own, ss, rs
        self.lsem, self.rows, self.cut, self.sent = lsem, rows, cut, sent
        self.all = out.reshape(4, 2, 2, 2, rows, C)
        self.split = cut < rows
        self.mids = []

    def head(self, z, y, x):
        return self.all.at[z, y, x, self.h.c, pl.ds(0, self.cut)]

    def tail(self, z, y, x):
        return self.all.at[z, y, x, self.h.c, pl.ds(self.cut, self.rows - self.cut)]

    def pair(self, z, x, c):
        return self.all.at[z, :, x, c, pl.ds(0, self.cut)]

    def plane(self, z, c):
        return self.all.at[z, :, :, c, pl.ds(self.cut, self.rows - self.cut)]

    def send(self, k, ref, dev, src=None):
        cp = rcopy(ref if src is None else src, ref, self.ss.at[k], self.rs.at[k], dev)
        cp.start()
        self.sent.append(cp)

    def mid_send(self, k, ref, j, rk, src=None):
        cp = rcopy(ref if src is None else src, ref, self.ss.at[k], self.rs.at[rk], self.h.dev(z=self.h.near(j)))
        pl.when(self.h.middle)(lambda: cp.start())
        self.mids.append(cp)

    def wait(self, k, ref):
        rcopy(ref, ref, self.ss.at[0], self.rs.at[k], self.h.sib()).wait_recv()

    def start(self):
        h = self.h
        self.local = pltpu.make_async_copy(self.own, self.all.at[h.z, h.y, h.x, h.c], self.lsem)
        self.local.start()
        me = self.head(h.z, h.y, h.x)
        own = self.own.at[pl.ds(0, self.cut)]
        self.send(8, me, h.xdev(), own)
        self.send(4, me, h.ydev(), own)
        self.send(0, me, h.dev(z=h.near(1)), own)
        self.mid_send(34, me, 2, 1, own)
        if self.split:
            self.send(24, self.tail(h.z, h.y, h.x), h.xdev(), self.own.at[pl.ds(self.cut, self.rows - self.cut)])

    def along_z(self, j):
        h = self.h
        part = self.head(h.near(j), h.y, h.x)
        self.wait(j - 1, part)
        if j == 1:
            self.mid_send(35, part, 2, 2)
        else:
            self.mid_send(34 + j, part, 1, j - 1)
        self.send(8 + j, part, h.xdev())
        self.send(4 + j, part, h.ydev())

    def along_y(self, j):
        h = self.h
        z = h.near(j)
        part = self.head(z, 1 - h.y, h.x)
        self.wait(4 + j, part)
        self.send(12 + j, part, h.xdev())
        self.send(16 + j, self.pair(z, h.x, h.c), h.sib())

    def along_x(self, j):
        h = self.h
        z = h.near(j)
        self.wait(8 + j, self.head(z, h.y, 1 - h.x))
        self.wait(12 + j, self.head(z, 1 - h.y, 1 - h.x))
        self.send(20 + j, self.pair(z, 1 - h.x, h.c), h.sib())

    def tail_x(self):
        h = self.h
        self.wait(24, self.tail(h.z, h.y, 1 - h.x))
        self.send(25, self.all.at[h.z, h.y, :, h.c, pl.ds(self.cut, self.rows - self.cut)], h.ydev())

    def tail_y(self):
        h = self.h
        self.wait(25, self.all.at[h.z, 1 - h.y, :, h.c, pl.ds(self.cut, self.rows - self.cut)])
        part = self.plane(h.z, h.c)
        self.send(26, part, h.dev(z=h.near(1)))
        self.mid_send(38, part, 2, 27)
        self.send(30, part, h.sib())

    def tail_z(self, j):
        h = self.h
        part = self.plane(h.near(j), h.c)
        self.wait(25 + j, part)
        if j == 1:
            self.mid_send(39, part, 2, 28)
        else:
            self.mid_send(38 + j, part, 1, 25 + j)
        self.send(30 + j, part, h.sib())

    def steps(self):
        p = functools.partial
        x, y, z = self.along_x, self.along_y, self.along_z
        tx, ty, tz = ([p(f)] if self.split else [] for f in (self.tail_x, self.tail_y, self.tail_z))
        order = [self.local.wait, p(y, 0), p(z, 1)] + tx + [p(x, 0), p(z, 2), p(y, 1)] + ty
        order += [p(z, 3), p(x, 1), p(y, 2)] + [p(f, 1) for f in tz] + [p(x, 2), p(y, 3)]
        return order + [p(f, j) for f in tz for j in (2, 3)] + [p(x, 3)]

    def finish(self):
        h = self.h
        c = 1 - h.c
        for j in range(4):
            z = h.near(j)
            self.wait(16 + j, self.pair(z, h.x, c))
            self.wait(20 + j, self.pair(z, 1 - h.x, c))
            if self.split:
                self.wait(30 + j, self.plane(z, c))

    def drain(self):
        for cp in self.mids:
            pl.when(self.h.middle)(lambda cp=cp: cp.wait_send())


class Scatter:
    def __init__(self, h, dw, l1, lxa, lya, lza, lzb, lyb, lxb, ss, rs, out, sent):
        self.h, self.dw, self.l1, self.lxa, self.lya = h, dw, l1, lxa, lya
        self.lza, self.lzb, self.lyb, self.lxb, self.ss, self.rs = lza, lzb, lyb, lxb, ss, rs
        self.out, self.sent = out, sent
        self.all = dw.reshape(4, 2, 2, 2, SHARD, C)
        self.head, self.tail = pl.ds(0, SUM_CUT), pl.ds(SUM_CUT, SHARD - SUM_CUT)

    def at(self, i, lo=0, n=SHARD):
        return self.dw.at[pl.ds(pl.multiple_of(i * SHARD + lo, 16), n)]

    def send(self, k, src, dst, dev):
        cp = rcopy(src, dst, self.ss.at[k], self.rs.at[k], dev)
        cp.start()
        self.sent.append(cp)

    def wait(self, k, land):
        rcopy(land, land, self.ss.at[0], self.rs.at[k], self.h.sib()).wait_recv()

    def add(self, i, lo, n, *parts):
        d = self.at(i, lo, n)
        total = d[...].astype(F32)
        for part in parts:
            total = total + part.astype(F32)
        d[...] = total.astype(BF)

    def s1(self, q):
        self.send(q, self.all.at[q, :, :, 1 - self.h.c], self.l1.at[q], self.h.sib())

    def _far(self, q):
        h = self.h
        return rcopy(
            self.all.at[q, :, :, h.c, self.tail], self.lzb.at[h.z], self.ss.at[16 + q], self.rs.at[20 + h.z], h.dev(z=q)
        )

    def s2(self, q):
        h = self.h
        self.wait(q, self.l1.at[q])
        for j in range(4):
            self.add(h.idx(q, j // 2, j % 2), 0, SHARD, self.l1[q, j // 2, j % 2])
        self.send(4 + q, self.all.at[q, :, 1 - h.x, h.c, self.head], self.lxa.at[q], h.xdev())
        pl.when(h.z != q)(lambda: self._far(q).start())

    def s3(self, q):
        h = self.h
        self.wait(4 + q, self.lxa.at[q])
        for j in range(2):
            self.add(h.idx(q, j), 0, SUM_CUT, self.lxa[q, j])
        self.send(8 + q, self.all.at[q, 1 - h.y, h.x, h.c, self.head], self.lya.at[q], h.ydev())

    def _near(self, q):
        h = self.h
        return rcopy(
            self.all.at[q, h.y, h.x, h.c, self.head], self.lza.at[h.z], self.ss.at[12 + q], self.rs.at[24 + h.z], h.dev(z=q)
        )

    def s4(self, q):
        h = self.h
        self.wait(8 + q, self.lya.at[q])
        self.add(h.idx(q), 0, SUM_CUT, self.lya[q])
        pl.when(h.z != q)(lambda: self._near(q).start())

    def t1(self):
        h = self.h
        for j in (1, 2, 3):
            self.wait(20 + h.near(j), self.lzb.at[h.near(j)])
        for j in range(4):
            parts = [self.lzb[h.near(k), j // 2, j % 2] for k in (1, 2, 3)]
            self.add(h.idx(None, j // 2, j % 2), SUM_CUT, SHARD - SUM_CUT, *parts)
        self.send(28, self.all.at[h.z, 1 - h.y, :, h.c, self.tail], self.lyb, h.ydev())

    def t2(self):
        h = self.h
        self.wait(28, self.lyb)
        for j in range(2):
            self.add(h.idx(None, None, j), SUM_CUT, SHARD - SUM_CUT, self.lyb[j])
        self.send(29, self.all.at[h.z, h.y, 1 - h.x, h.c, self.tail], self.lxb, h.xdev())

    def finish(self, extra):
        h = self.h
        self.wait(29, self.lxb)
        self.out[SUM_CUT:] = (
            self.at(h.idx(), SUM_CUT, SHARD - SUM_CUT)[...].astype(F32) + self.lxb[...].astype(F32) + extra[SUM_CUT:]
        )
        total = self.at(h.idx(), 0, SUM_CUT)[...].astype(F32) + extra[:SUM_CUT]
        for j in (1, 2, 3):
            self.wait(24 + h.near(j), self.lza.at[h.near(j)])
            total = total + self.lza[h.near(j)].astype(F32)
        self.out[:SUM_CUT] = total

    def drain(self):
        for q in range(4):

            @pl.when(self.h.z != q)
            def _(q=q):
                self._near(q).wait_send()
                self._far(q).wait_send()


class Halo:
    def __init__(self, h, edges, land, ss, rs):
        self.h, self.edges, self.land, self.ss, self.rs = h, edges, land, ss, rs
        self.up = rcopy(edges.at[0], land.at[1], ss.at[0], rs.at[0], h.dev(z=h.z - 1))
        self.down = rcopy(edges.at[1], land.at[0], ss.at[1], rs.at[1], h.dev(z=h.z + 1))

    def start_one(self, k):
        to = self.h.z + 2 * k - 1
        cp = rcopy(self.edges.at[k], self.land.at[1 - k], self.ss.at[k], self.rs.at[k], self.h.dev(z=to))
        pl.when((to >= 0) & (to <= 3))(lambda: cp.start())

    def start(self):
        pl.when(self.h.z > 0)(lambda: self.up.start())
        pl.when(self.h.z < 3)(lambda: self.down.start())

    def wait(self):
        @pl.when(self.h.z > 0)
        def _():
            self.up.wait_send()
            self.down.wait_recv()

        @pl.when(self.h.z < 3)
        def _():
            self.down.wait_send()
            self.up.wait_recv()


class Sums:
    def __init__(self, h, buf, ss, rs, sent):
        self.h, self.buf, self.ss, self.rs, self.sent = h, buf, ss, rs, sent

    def start_plane(self, payload):
        h = self.h
        self.own = payload
        mine = self.buf.at[2, 0]
        mine[...] = payload
        for r in (1, 2, 3):
            _, x, c = h.other(0, r // 2, r % 2)
            cp = rcopy(mine, self.buf.at[0, h.gy], self.ss.at[r - 1], self.rs.at[r - 1], h.dev(x=x, c=c))
            cp.start()
            self.sent.append(cp)

    def plane(self):
        h = self.h
        for r in (1, 2, 3):
            _, x, c = h.other(0, r // 2, r % 2)
            land = self.buf.at[0, x * 2 + c]
            rcopy(land, land, self.ss.at[0], self.rs.at[r - 1], h.sib()).wait_recv()
        return [jnp.where(h.gy == g, self.own, self.buf[0, g]) for g in range(4)]

    def start_z(self, payload):
        h = self.h
        self.own = payload
        mine = self.buf.at[2, 1]
        mine[...] = payload
        for j in (1, 2, 3):
            cp = rcopy(mine, self.buf.at[1, h.z], self.ss.at[2 + j], self.rs.at[3 + h.z], h.dev(z=h.near(j)))
            cp.start()
            self.sent.append(cp)

    def along_z(self):
        h = self.h
        for j in (1, 2, 3):
            land = self.buf.at[1, h.near(j)]
            rcopy(land, land, self.ss.at[0], self.rs.at[3 + h.near(j)], h.sib()).wait_recv()
        return [jnp.where(h.z == g, self.own, self.buf[1, g]) for g in range(4)]


def fold(row):
    return [row[:, 128 * k : 128 * (k + 1)] for k in range(4)]


def pack_rows(*rows):
    rows = rows + (jnp.zeros((1, C), F32),) * (4 - len(rows))
    return jnp.concatenate([part for r in rows for part in fold(r)], axis=0)


def unpack_rows(p):
    return [jnp.concatenate([p[4 * n + k : 4 * n + k + 1] for k in range(4)], axis=1) for n in range(p.shape[0] // 4)]


def column(r):
    return jnp.broadcast_to(r, (128, C)).T


def merge(parts, counts):
    total = sum(counts)
    mass = sum(parts[g][0:4] for g in range(4))
    mean = mass / jnp.maximum(total, 1.0)
    spread = jnp.zeros_like(mass)
    for g in range(4):
        n = jnp.maximum(counts[g], 1.0)
        gap = parts[g][0:4] / n - mean
        spread = spread + parts[g][4:8] + counts[g] * gap * gap
    third = parts[0] + parts[1] + parts[2] + parts[3]
    return jnp.concatenate([mass, spread, third[8:16]], axis=0)


def nn(a, b):
    return lax.dot_general(a, b, (((1,), (0,)), ((), ())), preferred_element_type=F32)


def nt(a, b):
    return lax.dot_general(a, b, (((1,), (1,)), ((), ())), preferred_element_type=F32)


def tn(a, b):
    return lax.dot_general(a, b, (((0,), (0,)), ((), ())), preferred_element_type=F32)


def sigmoid(u):
    return 1.0 / (1.0 + jnp.exp(-u))


def body(
    feat, w1s, w2s, gain, bias, head, hbias, labels, heights, widths, picks,
    pooled_out, fg_out, c1_out, c2_out, gg_out, bg_out, hg_out, hbg_out,
    w1, w2, x3, first, second, slope, dh, base, hid, dw,
    al, edges, bland, hland, sland, fland, fgs, fgl,
    e32, exts, ext, gb, stat, pacc, pz, pg, res, cot, yb, ht, gsc, mc1, mc2,
    l1, lxa, lya, lza, lzb, lyb, lxb,
    sem_g, rem_g, sem_ge, rem_ge, sem_l, sem_h, rem_h, sem_s, rem_s, sem_a, rem_a, sem_p, rem_p, sem_r, rem_r,
):
    h = Here()
    sent = []
    z, y = h.z, h.y

    barrier = pltpu.get_barrier_semaphore()
    peers = [h.dev(z=h.near(j)) for j in (1, 2, 3)]
    for r in range(1, 8):
        yy, xx, cc = h.other(r // 4, (r // 2) % 2, r % 2)
        peers.append(h.dev(y=yy, x=xx, c=cc))
    for dev in peers:
        pl.semaphore_signal(barrier, inc=1, device_id=dev, device_id_type=MESH)
    pl.semaphore_wait(barrier, len(peers))

    def swap_rows(lo, n, r, k):
        src = feat.at[pl.ds(PER * (1 - y) + lo, n), r]
        return rcopy(src, al.at[pl.ds(lo, n), r], sem_a.at[4 + k], rem_a.at[4 + k], h.ydev())

    swap = [swap_rows(0, 3, y, 0), swap_rows(3, 3, y, 1)] + [swap_rows(2 * k, 2, 1 - y, 2 + k) for k in range(3)]
    g1 = Gather(h, w1s, w1, sem_g.at[0], rem_g.at[0], sem_l.at[0], SHARD, CUT, sent)
    sent2 = []
    g2 = Gather(h, w2s, w2, sem_g.at[1], rem_g.at[1], sem_l.at[1], SHARD, CUT, sent2)
    ge = Gather(h, exts, ext, sem_ge, rem_ge, sem_l.at[2], 16, 16, sent)
    g1.start()
    swap[0].start()
    swap[1].start()
    e32[...] = jnp.zeros_like(e32)
    place = lax.broadcasted_iota(jnp.int32, (4, 128), 1) // 16
    both = jnp.concatenate([gain[...].astype(F32), bias[...].astype(F32)], axis=0)
    both = jnp.concatenate([both] * 8, axis=1)
    e32[0:4, 0:128] = jnp.where(place == lax.rem(h.idx(), 8), both, 0.0)
    e32[:, 256 : 256 + TASKS] = head[...].astype(F32)
    e32[0:12, 384 : 384 + TASKS] = labels[...].astype(F32)
    exts[...] = e32[...].astype(BF)
    ge.start()

    image = lax.broadcasted_iota(jnp.int32, (1, 8 * PER), 1)
    high = broad = jnp.zeros((1, 8 * PER), jnp.int32)
    for k in range(8 * PER):
        high = jnp.where(image == k, heights[k], high)
        broad = jnp.where(image == k, widths[k], broad)

    def pixels(zz, lo, n):
        here = (image >= lo) & (image < lo + n)
        cells = jnp.where(here, jnp.clip(high - ROWS * zz, 0, ROWS) * broad, 0).astype(F32)
        return cells.sum(1, keepdims=True)

    n_plane = [pixels(z, 2 * PER * g + PER * y, PER) for g in range(4)]
    n_z = [sum(pixels(zz, 2 * PER * g + PER * y, PER) for g in range(4)) for zz in range(4)]
    total = sum(n_z)
    my_first = h.gy * 2 * PER + PER * y

    col = lax.broadcasted_iota(jnp.int32, (COLS, C), 0)

    def wide(i, r):
        return jnp.where(ROWS * z + r < heights[my_first + i], widths[my_first + i], 0)

    def keep(i, r, v):
        return jnp.where(col < wide(i, r), v, 0.0)

    zero8 = jnp.zeros((8, C), F32)

    def by8(v):
        return v.reshape(COLS // 8, 8, C).sum(0)

    def put3(i, row, v):
        x3[i, row, :, C : 2 * C] = v.astype(BF)
        x3[i, row, :, 0:C] = jnp.where(col == 0, 0.0, pltpu.roll(v, 1, 0)).astype(BF)
        x3[i, row, :, 2 * C : 3 * C] = jnp.where(col == COLS - 1, 0.0, pltpu.roll(v, COLS - 1, 0)).astype(BF)

    def put_halo(land):
        def one(i, _):
            @pl.when(z > 0)
            def _():
                put3(i, 0, land[0, i].astype(F32))

            @pl.when(z == 0)
            def _():
                x3[i, 0] = jnp.zeros((COLS, 3 * C), BF)

            @pl.when(z < 3)
            def _():
                put3(i, 5, land[1, i].astype(F32))

            @pl.when(z == 3)
            def _():
                x3[i, 5] = jnp.zeros((COLS, 3 * C), BF)

            return 0

        lax.fori_loop(0, PER, one, 0)

    def take_row(src, offset, r, row, i, acc):
        v = keep(i, row, src[offset + i, r].astype(F32))
        base[i, row] = v.astype(BF)
        put3(i, row + 1, v)
        return acc + by8(v)

    def take_edge(k, src, offset, r, i, acc):
        acc = take_row(src, offset, r, 3 * k, i, acc)
        edges[k, i] = base[i, 3 * k]
        return acc

    halo = Halo(h, edges, bland, sem_h.at[0], rem_h.at[0])
    base_sum = lax.fori_loop(0, PER, lambda i, acc: take_edge(y, feat, PER * y, y, i, acc), zero8)
    halo.start_one(y)
    base_sum = lax.fori_loop(0, PER, lambda i, acc: take_row(feat, PER * y, 1 - y, 1 + y, i, acc), base_sum)

    def edges_in(k, acc):
        swap[k].wait_recv()
        return lax.fori_loop(3 * k, 3 * k + 3, lambda i, acc: take_edge(1 - y, al, 0, 1 - y, i, acc), acc)

    def rows_in(k, acc):
        swap[2 + k].wait_recv()
        return lax.fori_loop(2 * k, 2 * k + 2, lambda i, acc: take_row(al, 0, y, 2 - y, i, acc), acc)

    todo1, late = g1.steps(), 9
    todo2, todoe = [], ge.steps()
    for t, step in enumerate(todo1):
        step()
        if t >= 1 and todoe:
            todoe.pop(0)()
        if t in (2, 4, 6):
            swap[1 + t // 2].start()
        if t == late - 1:
            g2.start()
            todo2 = g2.steps()
        elif t >= late:
            todo2.pop(0)()
        if t == 5:
            base_sum = edges_in(0, base_sum)
        if t == 8:
            base_sum = edges_in(1, base_sum)
            halo.start_one(1 - y)
        if t in (10, 12, 14):
            base_sum = rows_in((t - 10) // 2, base_sum)
    base_sum = base_sum.sum(0, keepdims=True)
    g1.finish()
    steps = todo2
    def go(todo, n):
        for _ in range(min(n, len(todo))):
            todo.pop(0)()

    def conv(w, out, land, halo, todo=()):
        for p in range(3):
            im = pl.ds(2 * p, 2)
            mid = nn(x3[im, 1:5].reshape(8 * COLS, 3 * C), w[3 * C : 6 * C]).reshape(2, 4, COLS, C)
            lo = nn(x3[im, 1:4].reshape(6 * COLS, 3 * C), w[0 : 3 * C]).reshape(2, 3, COLS, C)
            hi = nn(x3[im, 2:5].reshape(6 * COLS, 3 * C), w[6 * C : 9 * C]).reshape(2, 3, COLS, C)
            out[im, 0] = mid[:, 0] + hi[:, 0]
            out[im, 1] = mid[:, 1] + lo[:, 0] + hi[:, 1]
            out[im, 2] = mid[:, 2] + lo[:, 1] + hi[:, 2]
            out[im, 3] = mid[:, 3] + lo[:, 2]
            go(todo, 1)
        halo.wait()
        go(todo, 1)
        put_halo(land)
        out[:, 0] += nn(x3[:, 0].reshape(6 * COLS, 3 * C), w[0 : 3 * C]).reshape(PER, COLS, C)
        out[:, 3] += nn(x3[:, 5].reshape(6 * COLS, 3 * C), w[6 * C : 9 * C]).reshape(PER, COLS, C)

    def conv_back(w, out, land, halo, todo=()):

        def taps(lhs, a):
            acc = None
            for b in range(3):
                part = nt(lhs[:, (2 - b) * C : (3 - b) * C], w[(3 * a + b) * C : (3 * a + b + 1) * C])
                acc = part if acc is None else acc + part
            return acc

        for p in range(3):
            im = pl.ds(2 * p, 2)
            mid = taps(x3[im, 1:5].reshape(8 * COLS, 3 * C), 1).reshape(2, 4, COLS, C)
            lo = taps(x3[im, 1:4].reshape(6 * COLS, 3 * C), 2).reshape(2, 3, COLS, C)
            hi = taps(x3[im, 2:5].reshape(6 * COLS, 3 * C), 0).reshape(2, 3, COLS, C)
            out[im, 0] = mid[:, 0] + hi[:, 0]
            out[im, 1] = mid[:, 1] + lo[:, 0] + hi[:, 1]
            out[im, 2] = mid[:, 2] + lo[:, 1] + hi[:, 2]
            out[im, 3] = mid[:, 3] + lo[:, 2]
            if todo:
                todo[p]()
        halo.wait()
        put_halo(land)
        if todo:
            todo[3]()
        out[:, 0] += taps(x3[:, 0].reshape(6 * COLS, 3 * C), 2).reshape(PER, COLS, C)
        out[:, 3] += taps(x3[:, 5].reshape(6 * COLS, 3 * C), 0).reshape(PER, COLS, C)

    def spread(src):
        def one(i, carry):
            n, mean, dev = carry
            widths_i = [wide(i, r) for r in range(ROWS)]
            ni = sum(widths_i).astype(F32)
            mass = jnp.zeros((8, C), F32)
            for r in range(ROWS):
                v = jnp.where(col < widths_i[r], src[i, r], 0.0)
                mass = mass + v.reshape(COLS // 8, 8, C).sum(0)
            mi = mass.sum(0, keepdims=True) / jnp.maximum(ni, 1.0)
            sq = jnp.zeros((8, C), F32)
            for r in range(ROWS):
                v = jnp.where(col < widths_i[r], src[i, r] - mi, 0.0)
                sq = sq + (v * v).reshape(COLS // 8, 8, C).sum(0)
            both = jnp.maximum(n + ni, 1.0)
            gap = mi - mean
            return (
                n + ni,
                mean + gap * (ni / both),
                dev + sq.sum(0, keepdims=True) + gap * gap * (n * ni / both),
            )

        zero = jnp.zeros((1, C), F32)
        n, mean, dev = lax.fori_loop(0, PER, one, (jnp.float32(0.0), zero, zero))
        return mean * n, dev

    def statistics(src, k, todo, inputs):
        ex = Sums(h, stat.at[k], sem_s.at[k], rem_s.at[k], sent)
        ex.start_plane(pack_rows(*spread(src), inputs))
        go(todo, 2)
        ex.start_z(merge(ex.plane(), n_plane))
        go(todo, 2)
        both = merge(ex.along_z(), n_z)
        mass, dev, inputs, _ = unpack_rows(both)
        return mass / total, lax.rsqrt(dev / total + norm_eps), inputs / total

    def start_sums(k, *rows):
        ex = Sums(h, stat.at[k], sem_s.at[k], rem_s.at[k], sent)
        ex.start_plane(pack_rows(*rows))
        return ex

    def mid_sums(ex):
        parts = ex.plane()
        ex.start_z(parts[0] + parts[1] + parts[2] + parts[3])

    def end_sums(ex):
        parts = ex.along_z()
        return parts[0] + parts[1] + parts[2] + parts[3]

    def edges_first(one, start):
        def edge(i, acc):
            for k, r in enumerate((0, ROWS - 1)):
                v = one(i, r)
                edges[k, i] = v.astype(BF)
                acc = acc + by8(v)
            return acc

        def inner(i, acc):
            for r in range(1, ROWS - 1):
                acc = acc + by8(one(i, r))
            return acc

        acc = lax.fori_loop(0, PER, edge, zero8)
        start()
        return lax.fori_loop(0, PER, inner, acc).sum(0, keepdims=True)

    conv(w1, first, bland, halo, steps)
    center, rs1, base_mean = statistics(first, 0, steps, base_sum)
    ge.finish()

    for k in range(4):
        tile = sum(ext[16 * d : 16 * d + 16, 0:128].astype(F32) for d in range(8 * k, 8 * k + 8))
        gb[0:4, 128 * k : 128 * (k + 1)] = tile[0:4]
    ht[...] = ext[:, 256:384].astype(F32)
    gain1, bias1 = gb[0:1], gb[2:3]

    def hidden(i, r):
        xh = (first[i, r] - center) * rs1
        first[i, r] = xh
        u = gain1 * xh + bias1
        v = keep(i, r, u * sigmoid(u))
        hid[i, r] = v.astype(BF)
        put3(i, r + 1, v)
        return v

    halo = Halo(h, edges, hland, sem_h.at[1], rem_h.at[1])
    def after_hidden():
        halo.start()
        go(steps, 2)

    hid_sum = edges_first(hidden, after_hidden)
    go(steps, 99)
    g2.finish()
    conv(w2, second, hland, halo, [])
    center, rs2, hid_mean = statistics(second, 1, [], hid_sum)
    gain2, bias2 = gb[1:2], gb[3:4]

    pacc[...] = jnp.zeros_like(pacc)

    def finals(i, _):
        acc = [jnp.zeros((8, C), F32) for _ in range(3)]
        for r in range(ROWS):
            xh = (second[i, r] - center) * rs2
            second[i, r] = xh
            pre = gain2 * xh + bias2 + base[i, r].astype(F32)
            s = sigmoid(pre)
            act = keep(i, r, pre * s)
            sl = keep(i, r, s * (1.0 + pre * (1.0 - s)))
            slope[i, r] = sl
            for k, v in enumerate((act, sl, sl * xh)):
                acc[k] = acc[k] + v.reshape(COLS // 8, 8, C).sum(0)
        for k in range(3):
            pacc[k, pl.ds(i, 1)] = acc[k].sum(0, keepdims=True)
        return 0

    lax.fori_loop(0, PER, finals, 0)

    rows8 = lax.broadcasted_iota(jnp.int32, (8, 1), 0)
    inv_pix = jnp.zeros((8, 1), F32)
    for i in range(PER):
        inv_pix = jnp.where(rows8 == i, 1.0 / (heights[my_first + i] * widths[my_first + i]).astype(F32), inv_pix)
    me_z = pz.at[z]
    me_z[...] = pacc[0]
    for j in (1, 2, 3):
        cp = rcopy(me_z, me_z, sem_p.at[j - 1], rem_p.at[z], h.dev(z=h.near(j)))
        cp.start()
        sent.append(cp)
    head_gram = lax.dot_general(ht[...], ht[...], (((0,), (0,)), ((), ())), precision=HIGH, preferred_element_type=F32)
    for j in (1, 2, 3):
        land = pz.at[h.near(j)]
        rcopy(land, land, sem_p.at[0], rem_p.at[h.near(j)], h.sib()).wait_recv()
    slot = (y * 2 + h.x) * 2 + h.c
    me_p = pg.at[slot]
    me_p[...] = (pz[0] + pz[1] + pz[2] + pz[3]) * inv_pix
    for r in range(1, 8):
        yy, xx, cc = h.other(r // 4, (r // 2) % 2, r % 2)
        cp = rcopy(me_p, me_p, sem_p.at[2 + r], rem_p.at[3 + r], h.dev(y=yy, x=xx, c=cc))
        cp.start()
        sent.append(cp)
    lane = lax.broadcasted_iota(jnp.int32, (8, 128), 1)
    row = lax.broadcasted_iota(jnp.int32, (8, 128), 0)
    real = (row < PER) & (lane < TASKS)
    wanted = []
    for s in range(8):
        yy, gy = s // 4, s % 4
        lab = ext[16 * gy : 16 * gy + 16, 384:512].astype(F32)
        lab = lab[PER * yy : PER * yy + PER]
        wanted.append(jnp.concatenate([lab, jnp.zeros((2, 128), F32)], axis=0))
    for r in range(1, 8):
        yy, xx, cc = h.other(r // 4, (r // 2) % 2, r % 2)
        land = pg.at[(yy * 2 + xx) * 2 + cc]
        rcopy(land, land, sem_p.at[0], rem_p.at[3 + r], h.sib()).wait_recv()
    pooled = pg[...].reshape(64, C)
    offset = jnp.concatenate([hbias[...].astype(F32), jnp.zeros((1, 128 - TASKS), F32)], axis=1)
    logits = lax.dot_general(pooled, ht[...], (((1,), (0,)), ((), ())), precision=HIGH, preferred_element_type=F32)
    logits = logits.reshape(8, 8, 128) + offset
    images = 8 * PER
    for s in range(8):
        res[s] = jnp.where(real, (sigmoid(logits[s]) - wanted[s]) / images, 0.0)
    residual = res[...].reshape(64, 128)
    gram = head_gram * lax.dot_general(
        residual, residual, (((0,), (0,)), ((), ())), precision=HIGH, preferred_element_type=F32
    )
    gram = gram[0:TASKS]
    lane1 = lax.broadcasted_iota(jnp.int32, (1, 128), 1)
    sub = lax.broadcasted_iota(jnp.int32, (TASKS, 128), 0)

    def fw(k, carry):
        mix, q = carry
        t = picks[k]
        one = (lane1 == t).astype(F32)
        line = jnp.where(sub == t, gram, 0.0).sum(0, keepdims=True)
        self_dot = (mix * q).sum(1, keepdims=True)
        cross = (one * q).sum(1, keepdims=True)
        vertex = (one * line).sum(1, keepdims=True)
        d = jnp.maximum(self_dot + vertex - 2.0 * cross, 0.1 * vertex)
        step = jnp.clip((self_dot - cross) / d, 0.0, 1.0)
        return (1.0 - step) * mix + step * one, (1.0 - step) * q + step * line

    mix0 = jnp.where(lane1 < TASKS, 1.0 / TASKS, 0.0)
    mix, _ = lax.fori_loop(0, STEPS, fw, (mix0, gram.sum(0, keepdims=True) / TASKS))
    mine = res[slot] * mix
    cot[...] = inv_pix * lax.dot_general(
        mine, ht[...], (((1,), (1,)), ((), ())), precision=HIGH, preferred_element_type=F32
    )
    ex = start_sums(
        2, (cot[...] * pacc[1]).sum(0, keepdims=True), (cot[...] * pacc[2]).sum(0, keepdims=True)
    )

    for yy in range(2):
        pooled_out[PER * yy : PER * (yy + 1)] = pg[(yy * 2 + h.x) * 2 + h.c][0:PER]
    head_grad = lax.dot_general(
        pooled, residual, (((0,), (0,)), ((), ())), precision=HIGH, preferred_element_type=F32
    )
    mid_sums(ex)
    gsc[...] = head_grad
    hg_out[...] = gsc[pl.ds(pl.multiple_of(h.idx() * 16, 16), 16)][:, 0:TASKS]
    hbg_out[...] = residual.sum(0, keepdims=True)[:, 0:TASKS]
    sums2 = end_sums(ex)
    yb[0, 0:8] = sums2[0:8]
    mc1[0:C] = column(base_mean)
    mc1[C:] = mc1[0:256]
    mc2[0:C] = column(hid_mean)
    mc2[C:] = mc2[0:256]
    yb[0, 24:32] = pack_rows(hid_mean, base_mean)[0:8]

    sum_b, sum_g, _, _ = unpack_rows(sums2)
    mean_b, mean_g = sum_b / total, sum_g / total
    scale = gain2 * rs2

    def d_second(i, r):
        xh = second[i, r]
        dp = slope[i, r] * cot[pl.ds(i, 1)]
        v = keep(i, r, scale * (dp - mean_b - xh * mean_g))
        put3(i, r + 1, v)
        return v.astype(BF).astype(F32)

    halo = Halo(h, edges, sland, sem_h.at[2], rem_h.at[2])
    d2_sum = edges_first(d_second, halo.start)
    conv_back(w2, dh, sland, halo)

    def d_norm1(i, carry):
        a, b = carry
        for r in range(ROWS):
            xh = first[i, r]
            u = gain1 * xh + bias1
            s = sigmoid(u)
            v = keep(i, r, dh[i, r] * (s * (1.0 + u * (1.0 - s))))
            dh[i, r] = v
            a = a + v.reshape(COLS // 8, 8, C).sum(0)
            b = b + (v * xh).reshape(COLS // 8, 8, C).sum(0)
        return a, b

    a, b = lax.fori_loop(0, PER, d_norm1, (zero8, zero8))
    ex = start_sums(3, a.sum(0, keepdims=True), b.sum(0, keepdims=True), d2_sum)

    def weight_taps(x, out, mean, d_sum, lo, hi):
        for t in range(lo, hi):
            ta, tb = t // 3, t % 3
            d = x3[:, 2 - ta : 6 - ta, :, (2 - tb) * C : (3 - tb) * C].reshape(PER * ROWS * COLS, C)
            part = tn(x[...].reshape(PER * ROWS * COLS, C), d)
            off = jnp.concatenate([mean[0:C] * f for f in fold(d_sum)], axis=1)
            out[t * C : (t + 1) * C] = (part - off).astype(BF)

    def scatter(k, src, out):
        return Scatter(
            h, src, l1.at[k], lxa.at[k], lya.at[k], lza.at[k], lzb.at[k], lyb.at[k], lxb.at[k], sem_r.at[k], rem_r.at[k],
            out, sent,
        )

    r2 = scatter(0, dw, c2_out)
    weight_taps(hid, dw, mc2, d2_sum, 0, 3)
    r2.s1(0)
    mid_sums(ex)
    weight_taps(hid, dw, mc2, d2_sum, 3, 5)
    r2.s1(1)
    r2.s2(0)
    weight_taps(hid, dw, mc2, d2_sum, 5, 7)
    r2.s1(2)
    r2.s2(1)
    weight_taps(hid, dw, mc2, d2_sum, 7, 9)
    r2.s1(3)
    r2.s2(2)
    sums1 = end_sums(ex)
    yb[0, 8:20] = sums1[0:12]
    sum_b, sum_g, _, _ = unpack_rows(sums1)
    mean_b1, mean_g1 = sum_b / total, sum_g / total
    scale1 = gain1 * rs1

    def d_first(i, r):
        v = keep(i, r, scale1 * (dh[i, r] - mean_b1 - first[i, r] * mean_g1))
        put3(i, r + 1, v)
        return v.astype(BF).astype(F32)

    halo = Halo(h, edges, fland, sem_h.at[3], rem_h.at[3])
    d1_sum = edges_first(d_first, halo.start)
    r2.s2(3)
    ex = start_sums(4, d1_sum)
    for cp in sent2:
        cp.wait_send()
    g2.drain()
    r1 = scatter(1, w2, c1_out)
    weight_taps(base, w2, mc1, d1_sum, 3, 6)

    def other_taps():
        weight_taps(base, w2, mc1, d1_sum, 0, 3)
        r1.s1(0)
        r1.s1(1)
        weight_taps(base, w2, mc1, d1_sum, 6, 7)
        r1.s1(2)
        weight_taps(base, w2, mc1, d1_sum, 7, 8)
        r1.s2(0)
        weight_taps(base, w2, mc1, d1_sum, 8, 9)
        r1.s1(3)
        r1.s2(1)

    conv_back(w1, dh, fland, halo, [functools.partial(r2.s3, q) for q in range(3)] + [other_taps])
    r1.s2(2)
    mid_sums(ex)
    r2.s4(0)

    def result(i, r):
        return keep(i, r, dh[i, r] + slope[i, r] * cot[pl.ds(i, 1)])

    back = []
    for p in range(3):
        for i in (2 * p, 2 * p + 1):
            for r in range(2):
                fgs[i, r] = result(i, 2 * (1 - y) + r).astype(BF)
        im = pl.ds(2 * p, 2)
        cp = rcopy(fgs.at[im], fgl.at[im], sem_a.at[1 + p], rem_a.at[1 + p], h.ydev())
        cp.start()
        back.append(cp)

    def stay(i, _):
        for r in range(2):
            fg_out[PER * y + i, r] = result(i, 2 * y + r).astype(BF)
        return 0

    lax.fori_loop(0, PER, stay, 0)
    r1.s2(3)
    r2.s3(3)
    r2.s4(1)
    yb[0, 20:24] = end_sums(ex)[0:4]
    ysum = rcopy(yb.at[0], yb.at[1], sem_a.at[0], rem_a.at[0], h.ydev())
    ysum.start()
    r2.s4(2)
    r1.s3(0)
    r2.s4(3)
    r2.t1()
    r1.s3(1)
    r1.s4(0)

    ysum.wait_recv()
    sb2, sg2, sb1, sg1 = unpack_rows(yb[0, 0:16] + yb[1, 0:16])
    tile = jnp.zeros((4, 128), F32)
    for k in range(4):
        rows = [v[:, 128 * k : 128 * (k + 1)] for v in (sg1, sg2, sb1, sb2)]
        tile = jnp.where(lax.div(h.idx(), 8) == k, jnp.concatenate(rows, axis=0), tile)
    own = jnp.zeros((4, 16), F32)
    for k in range(8):
        own = jnp.where(lax.rem(h.idx(), 8) == k, tile[:, 16 * k : 16 * (k + 1)], own)
    gg_out[...] = own[0:2]
    bg_out[...] = own[2:4]

    r2.t2()

    at = pl.ds(pl.multiple_of(lax.rem(h.idx() * SHARD, C), 16), SHARD)
    d2_all, d1_all, hid_other, base_other = unpack_rows(yb[1, 16:32])
    d2_mine, d1_mine, _, _ = unpack_rows(yb[0, 16:32])

    def taken_off(mean, other, all_mine, all_other):
        off = jnp.concatenate([mean[at] * f for f in fold(all_mine)], axis=1)
        mean[0:C] = column(other)
        mean[C:] = mean[0:256]
        return off + jnp.concatenate([mean[at] * f for f in fold(all_other)], axis=1)

    off2 = taken_off(mc2, hid_other, d2_mine, d2_all)
    off1 = taken_off(mc1, base_other, d1_mine, d1_all)
    r2.finish(off2)

    def land_rows(p):
        back[p].wait_recv()
        for i in (2 * p, 2 * p + 1):
            fg_out[PER * (1 - y) + i] = fgl[i]

    land_rows(0)
    r1.s3(2)
    r1.s4(1)
    r1.t1()
    land_rows(1)
    r1.s3(3)
    r1.s4(2)
    r1.t2()
    land_rows(2)
    r1.s4(3)
    r1.finish(off1)

    ysum.wait_send()
    g1.drain()
    ge.drain()
    for cp in swap + back + sent:
        cp.wait_send()
    r1.drain()
    r2.drain()


def fused(features, w1s, w2s, gain, bias, head, head_bias, labels, heights, widths, picks):
    vm = pl.BlockSpec(memory_space=pltpu.VMEM)
    sm = pl.BlockSpec(memory_space=pltpu.SMEM)
    V = pltpu.VMEM
    dma = pltpu.SemaphoreType.DMA
    maps = (PER, ROWS, COLS, C)
    edge = (2, PER, COLS, C)
    half = (PER, 2, COLS, C)
    scratch = [
        V((9 * C, C), BF), V((9 * C, C), BF), V((PER, ROWS + 2, COLS, 3 * C), BF),
        V(maps, F32), V(maps, F32), V(maps, F32), V(maps, F32), V(maps, BF), V(maps, BF), V((9 * C, C), BF),
        V(half, BF), V(edge, BF), V(edge, BF), V(edge, BF), V(edge, BF), V(edge, BF), V(half, BF), V(half, BF),
        V((16, C), F32), V((16, C), BF), V((C, C), BF), V((8, C), F32),
        V((5, 3, 4, 16, 128), F32), V((3, 8, C), F32), V((4, 8, C), F32), V((8, 8, C), F32),
        V((8, 8, 128), F32), V((8, C), F32), V((2, 32, 128), F32), V((C, 128), F32), V((C, 128), F32),
        V((C + 256, 128), F32), V((C + 256, 128), F32),
        V((2, 4, 2, 2, SHARD, C), BF), V((2, 4, 2, SUM_CUT, C), BF), V((2, 4, SUM_CUT, C), BF), V((2, 4, SUM_CUT, C), BF),
        V((2, 4, 2, 2, SHARD - SUM_CUT, C), BF), V((2, 2, SHARD - SUM_CUT, C), BF), V((2, SHARD - SUM_CUT, C), BF),
        dma((2, 48)), dma((2, 48)), dma((48,)), dma((48,)), dma((3,)), dma((4, 2)), dma((4, 2)),
        dma((5, 8)), dma((5, 8)), dma((10,)), dma((10,)), dma((12,)), dma((12,)), dma((2, 48)), dma((2, 48)),
    ]
    f = jax.ShapeDtypeStruct
    outs = pl.pallas_call(
        body,
        out_shape=[
            f((2 * PER, C), F32), f((2 * PER, 2, COLS, C), BF), f((SHARD, C), F32), f((SHARD, C), F32),
            f((2, 16), F32), f((2, 16), F32), f((16, TASKS), F32), f((1, TASKS), F32),
        ],
        in_specs=[vm] * 8 + [sm] * 3,
        out_specs=[vm] * 8,
        scratch_shapes=scratch,
        compiler_params=pltpu.CompilerParams(
            collective_id=0, has_side_effects=True, vmem_limit_bytes=63 * 2**20
        ),
        name="block",
    )(
        features, w1s, w2s, gain.T, bias.T, head, head_bias.reshape(1, TASKS), labels, heights, widths, picks,
    )
    pooled, fg, c1, c2, gg, bg, hg, hbg = outs
    return pooled, fg.astype(F32), c1, c2, gg.T, bg.T, hg, hbg.reshape(TASKS)


def extended(cells, sides, width):
    for axis, dim in sides:
        count = lax.axis_size(axis)
        ends = count - 1
        head = lax.slice_in_dim(cells, 0, width, axis=dim)
        tail = lax.slice_in_dim(cells, cells.shape[dim] - width, cells.shape[dim], axis=dim)
        cells = jnp.concatenate(
            [
                lax.ppermute(tail, axis, [(i, (i + 1) % count) for i in range(ends)]),
                cells,
                lax.ppermute(head, axis, [((i + 1) % count, i) for i in range(ends)]),
            ],
            axis=dim,
        )
    return cells


def make_patches(padded, row_count, col_count):
    widened = jnp.pad(padded, ((0, 0), (0, 0), (1, 1), (0, 0)))
    pieces = [
        widened[:, row_off : row_off + row_count, col_off : col_off + col_count, :]
        for row_off in range(3)
        for col_off in range(3)
    ]
    joined = jnp.concatenate(pieces, axis=-1)
    return joined.reshape(-1, joined.shape[-1])


def conv_rows(act, weight):
    padded = extended(act, (("gx", 1),), 1)
    patches = make_patches(padded, act.shape[1], act.shape[2])
    output = jnp.dot(patches, weight, preferred_element_type=jnp.float32)
    return (output.reshape(act.shape[:3] + (weight.shape[1],)), padded)


def reversed_taps(weight):
    channels = weight.shape[1]
    taps = weight.reshape(9, channels, channels)[::-1]
    return jnp.transpose(taps, (0, 2, 1)).reshape(9 * channels, channels)


def weight_term(padded, grad_bf):
    patches = make_patches(padded, grad_bf.shape[1], grad_bf.shape[2])
    flat_grad = grad_bf.reshape(-1, grad_bf.shape[-1])
    return lax.dot_general(
        patches, flat_grad, (((0,), (0,)), ((), ())), preferred_element_type=jnp.float32
    )


def batch_statistics(values, inner_result, pixel_total):
    center_val = (
        lax.psum(jnp.sum(values * inner_result, axis=(0, 1, 2)), ("gx", "gy")) / pixel_total
    )
    centered = values - center_val
    spread_sq = (
        lax.psum(jnp.sum(inner_result * centered * centered, axis=(0, 1, 2)), ("gx", "gy"))
        / pixel_total
    )
    inverse_scale = lax.rsqrt(spread_sq + norm_eps)
    return (centered * inverse_scale, inverse_scale)


def norm_backward(
    output_gradient, normalized_input, inverse_scale, norm_scale_factor, inner_result, pixel_total
):
    bias_gradient_total, scale_gradient_total = lax.psum(
        (
            jnp.sum(output_gradient, axis=(0, 1, 2)),
            jnp.sum(output_gradient * normalized_input, axis=(0, 1, 2)),
        ),
        ("gx", "gy"),
    )
    backward_result = (
        norm_scale_factor
        * inverse_scale
        * (
            output_gradient
            - bias_gradient_total / pixel_total
            - normalized_input * scale_gradient_total / pixel_total
        )
        * inner_result
    )
    return (backward_result, scale_gradient_total, bias_gradient_total)


def silu_slope(values):
    sig_val = jax.nn.sigmoid(values)
    return sig_val * (1.0 + values * (1.0 - sig_val))


def frank_wolfe(gram, picks):
    task_ids = jnp.arange(TASKS)

    def fw_step(index, task_mix):
        onehot = (task_ids == picks[index]).astype(jnp.float32)
        mixed_vec = jnp.dot(gram, task_mix, precision=lax.Precision.HIGHEST)
        self_dot = jnp.sum(task_mix * mixed_vec)
        cross_dot = jnp.sum(onehot * mixed_vec)
        vertex_dot = jnp.sum(onehot * jnp.dot(gram, onehot, precision=lax.Precision.HIGHEST))
        distance = jnp.maximum(self_dot + vertex_dot - 2.0 * cross_dot, 0.1 * vertex_dot)
        step_size = jnp.clip((self_dot - cross_dot) / distance, 0.0, 1.0)
        return (1.0 - step_size) * task_mix + step_size * onehot

    start = jnp.full((TASKS,), 1.0 / TASKS, jnp.float32)
    return lax.fori_loop(0, STEPS, fw_step, start)


def on_device(
    features,
    conv1_weight,
    conv2_weight,
    norm_gain,
    norm_bias,
    head_weight,
    head_bias,
    labels,
    heights,
    widths,
    picks,
):
    image_count, row_count, col_count, channels = features.shape
    per_micro = image_count // MICRO
    total_images = image_count * lax.axis_size("gy")
    row_ids = lax.axis_index("gx") * row_count + jnp.arange(row_count)
    my_heights = lax.dynamic_slice_in_dim(heights, lax.axis_index("gy") * image_count, image_count)
    my_widths = lax.dynamic_slice_in_dim(widths, lax.axis_index("gy") * image_count, image_count)
    inside_all = (
        (row_ids[None, :, None] < my_heights[:, None, None])
        & (jnp.arange(col_count)[None, None, :] < my_widths[:, None, None])
    ).astype(jnp.float32)[..., None]
    pixel_count = (my_heights * my_widths).astype(jnp.float32)
    micro_pixels = jnp.sum((heights * widths).reshape(-1, MICRO, per_micro), axis=(0, 2)).astype(
        jnp.float32
    )

    def weights_now():
        return (
            lax.all_gather(conv1_weight, ("gx", "gy"), axis=0, tiled=True),
            lax.all_gather(conv2_weight, ("gx", "gy"), axis=0, tiled=True),
            lax.all_gather(norm_gain, ("gx", "gy"), axis=0, tiled=True),
            lax.all_gather(norm_bias, ("gx", "gy"), axis=0, tiled=True),
            lax.all_gather(head_weight, ("gx", "gy"), axis=0, tiled=True),
        )

    saved = []
    pooled_parts = []
    head_full = None
    for index in range(MICRO):
        conv_one, conv_two, gain_full, bias_full, head_full = weights_now()
        scale_factors = gain_full.astype(jnp.float32)
        bias_values = bias_full.astype(jnp.float32)
        inner_result = inside_all[index * per_micro : (index + 1) * per_micro]
        pixel_total = micro_pixels[index]
        base_input_bfloat = features[
            index * per_micro : (index + 1) * per_micro
        ] * inner_result.astype(jnp.bfloat16)
        first_convolution, padded_input = conv_rows(base_input_bfloat, conv_one)
        first_normalized, first_scale = batch_statistics(
            first_convolution, inner_result, pixel_total
        )
        first_norm_output = scale_factors[:, 0] * first_normalized + bias_values[:, 0]
        hidden_bf = (jax.nn.silu(first_norm_output) * inner_result).astype(jnp.bfloat16)
        second_convolution, padded_hidden_state = conv_rows(hidden_bf, conv_two)
        second_normalized, second_scale = batch_statistics(
            second_convolution, inner_result, pixel_total
        )
        before_activation = (
            scale_factors[:, 1] * second_normalized
            + bias_values[:, 1]
            + base_input_bfloat.astype(jnp.float32)
        )
        final_act = jax.nn.silu(before_activation) * inner_result
        pooled_parts.append(jnp.sum(final_act, axis=(1, 2)))
        saved.append(
            (
                padded_input,
                padded_hidden_state,
                first_normalized,
                first_scale,
                first_norm_output,
                second_normalized,
                second_scale,
                before_activation,
            )
        )
    pooled = lax.psum(jnp.concatenate(pooled_parts, axis=0), "gx") / pixel_count[:, None]
    head_mat = head_full.astype(jnp.float32)
    logits = jnp.dot(pooled, head_mat, precision=lax.Precision.HIGHEST) + head_bias.astype(
        jnp.float32
    )
    residual = (jax.nn.sigmoid(logits) - labels.astype(jnp.float32)) / total_images
    gram_part = jnp.dot(residual.T, residual, precision=lax.Precision.HIGHEST)
    head_part = jnp.dot(pooled.T, residual, precision=lax.Precision.HIGHEST)
    gram_sum, head_bias_grad, head_total = (
        lax.psum(gram_part.astype(jnp.bfloat16), "gy").astype(jnp.float32),
        lax.psum(jnp.sum(residual, axis=0).astype(jnp.bfloat16), "gy").astype(jnp.float32),
        lax.psum(head_part.astype(jnp.bfloat16), "gy").astype(jnp.float32),
    )
    gram = gram_sum * jnp.dot(head_mat.T, head_mat, precision=lax.Precision.HIGHEST)
    task_mix = frank_wolfe(gram, picks)
    pooled_cot = jnp.dot(residual * task_mix, head_mat.T, precision=lax.Precision.HIGHEST)
    shard_rows = 9 * channels // lax.axis_size(("gx", "gy"))
    conv1_grad = jnp.zeros((shard_rows, channels), jnp.float32)
    conv2_grad = jnp.zeros((shard_rows, channels), jnp.float32)
    gain_total = jnp.zeros((channels, 2), jnp.float32)
    bias_total = jnp.zeros((channels, 2), jnp.float32)
    feat_parts = []
    for index in range(MICRO):
        conv_one, conv_two, gain_full, bias_full, unused_heads = weights_now()
        scale_factors = gain_full.astype(jnp.float32)
        (
            padded_input,
            padded_hidden_state,
            first_normalized,
            first_scale,
            first_norm_output,
            second_normalized,
            second_scale,
            before_activation,
        ) = saved[index]
        inner_result = inside_all[index * per_micro : (index + 1) * per_micro]
        pixel_total = micro_pixels[index]
        cot_part = (
            pooled_cot[index * per_micro : (index + 1) * per_micro]
            / pixel_count[index * per_micro : (index + 1) * per_micro, None]
        )
        gradient_before_relu = (
            cot_part[:, None, None, :] * inner_result * silu_slope(before_activation)
        )
        d_second, gain_two, bias_two = norm_backward(
            gradient_before_relu,
            second_normalized,
            second_scale,
            scale_factors[:, 1],
            inner_result,
            pixel_total,
        )
        second_bf = d_second.astype(jnp.bfloat16)
        term_two = weight_term(padded_hidden_state, second_bf)
        d_hidden, unused_pad = conv_rows(second_bf, reversed_taps(conv_two))
        gradient_norm_first = d_hidden * inner_result * silu_slope(first_norm_output)
        d_first, gain_one, bias_one = norm_backward(
            gradient_norm_first,
            first_normalized,
            first_scale,
            scale_factors[:, 0],
            inner_result,
            pixel_total,
        )
        first_bf = d_first.astype(jnp.bfloat16)
        term_one = weight_term(padded_input, first_bf)
        d_base, unused_pad_two = conv_rows(first_bf, reversed_taps(conv_one))
        feat_parts.append((d_base + gradient_before_relu) * inner_result)
        gain_total = gain_total + jnp.stack([gain_one, gain_two], axis=1)
        bias_total = bias_total + jnp.stack([bias_one, bias_two], axis=1)
        shard_one, shard_two = (
            lax.psum_scatter(term_one, ("gx", "gy"), scatter_dimension=0, tiled=True),
            lax.psum_scatter(term_two, ("gx", "gy"), scatter_dimension=0, tiled=True),
        )
        conv1_grad = conv1_grad + shard_one
        conv2_grad = conv2_grad + shard_two
    flat_index = lax.axis_index(("gx", "gy"))
    chan_rows = channels // lax.axis_size(("gx", "gy"))
    gain_grad = lax.dynamic_slice_in_dim(gain_total, flat_index * chan_rows, chan_rows, 0)
    bias_grad = lax.dynamic_slice_in_dim(bias_total, flat_index * chan_rows, chan_rows, 0)
    head_grad = lax.dynamic_slice_in_dim(head_total, flat_index * chan_rows, chan_rows, 0)
    features_grad = jnp.concatenate(feat_parts, axis=0)
    return (
        pooled,
        features_grad,
        conv1_grad,
        conv2_grad,
        gain_grad,
        bias_grad,
        head_grad,
        head_bias_grad,
    )


def solution(mesh):
    in_specs = (
        P("gy", "gx", None, None),
        P(("gx", "gy"), None),
        P(("gx", "gy"), None),
        P(("gx", "gy"), None),
        P(("gx", "gy"), None),
        P(("gx", "gy"), None),
        P(),
        P("gy", None),
        P(),
        P(),
        P(),
    )
    out_specs = (
        P("gy", None),
        P("gy", "gx", None, None),
        P(("gx", "gy"), None),
        P(("gx", "gy"), None),
        P(("gx", "gy"), None),
        P(("gx", "gy"), None),
        P(("gx", "gy"), None),
        P(),
    )
    whole = dict(mesh.shape) != {"gx": 8, "gy": 4}
    return jax.shard_map(
        on_device if whole else fused, mesh=mesh, in_specs=in_specs, out_specs=out_specs, check_vma=False
    )
```

```python
import functools

import jax
import jax.numpy as jnp
from jax import lax
from jax.experimental import pallas as pl
from jax.experimental.pallas import tpu as pltpu
from jax.sharding import PartitionSpec as P

TASKS = 40
MICRO = 2
STEPS = 20
norm_eps = 1e-05
BF = jnp.bfloat16
F32 = jnp.float32
HIGH = lax.Precision.HIGHEST
MESH = pl.DeviceIdType.MESH

C = 512
COLS = 64
PER = 6
ROWS = 4
SHARD = 144
CUT = 112
SUM_CUT = 112


class Here:
    def __init__(self):
        gx = lax.axis_index("gx")
        gy = lax.axis_index("gy")
        self.z = lax.div(gx, 2)
        self.y = lax.rem(gx, 2)
        self.x = lax.div(gy, 2)
        self.c = lax.rem(gy, 2)
        self.gy = gy
        self.middle = lax.rem(self.z + 1, 4) >= 2

    def _fill(self, z, y, x, c):
        return (
            self.z if z is None else z,
            self.y if y is None else y,
            self.x if x is None else x,
            self.c if c is None else c,
        )

    def dev(self, z=None, y=None, x=None, c=None):
        z, y, x, c = self._fill(z, y, x, c)
        return {"gx": z * 2 + y, "gy": x * 2 + c}

    def idx(self, z=None, y=None, x=None, c=None):
        z, y, x, c = self._fill(z, y, x, c)
        return ((z * 2 + y) * 2 + x) * 2 + c

    def near(self, j):
        z = self.z
        if j == 0:
            return z
        if j == 1:
            return z + 1 - 2 * lax.rem(z, 2)
        if j == 2:
            return 2 - lax.div(z, 2)
        return 3 - 3 * lax.div(z, 2)

    def other(self, dy, dx, dc):
        return (
            1 - self.y if dy else self.y,
            1 - self.x if dx else self.x,
            1 - self.c if dc else self.c,
        )

    def ydev(self):
        return self.dev(y=1 - self.y)

    def xdev(self):
        return self.dev(x=1 - self.x)

    def sib(self):
        return self.dev(c=1 - self.c)


def rcopy(src, dst, ss, rs, dev):
    return pltpu.make_async_remote_copy(
        src_ref=src, dst_ref=dst, send_sem=ss, recv_sem=rs, device_id=dev, device_id_type=MESH
    )


class Gather:
    def __init__(self, h, own, out, ss, rs, lsem, rows, cut, sent):
        self.h, self.own, self.ss, self.rs = h, own, ss, rs
        self.lsem, self.rows, self.cut, self.sent = lsem, rows, cut, sent
        self.all = out.reshape(4, 2, 2, 2, rows, C)
        self.split = cut < rows
        self.mids = []

    def head(self, z, y, x):
        return self.all.at[z, y, x, self.h.c, pl.ds(0, self.cut)]

    def tail(self, z, y, x):
        return self.all.at[z, y, x, self.h.c, pl.ds(self.cut, self.rows - self.cut)]

    def pair(self, z, x, c):
        return self.all.at[z, :, x, c, pl.ds(0, self.cut)]

    def plane(self, z, c):
        return self.all.at[z, :, :, c, pl.ds(self.cut, self.rows - self.cut)]

    def send(self, k, ref, dev, src=None):
        cp = rcopy(ref if src is None else src, ref, self.ss.at[k], self.rs.at[k], dev)
        cp.start()
        self.sent.append(cp)

    def mid_send(self, k, ref, j, rk, src=None):
        cp = rcopy(ref if src is None else src, ref, self.ss.at[k], self.rs.at[rk], self.h.dev(z=self.h.near(j)))
        pl.when(self.h.middle)(lambda: cp.start())
        self.mids.append(cp)

    def wait(self, k, ref):
        rcopy(ref, ref, self.ss.at[0], self.rs.at[k], self.h.sib()).wait_recv()

    def start(self):
        h = self.h
        self.local = pltpu.make_async_copy(self.own, self.all.at[h.z, h.y, h.x, h.c], self.lsem)
        self.local.start()
        me = self.head(h.z, h.y, h.x)
        own = self.own.at[pl.ds(0, self.cut)]
        self.send(8, me, h.xdev(), own)
        self.send(4, me, h.ydev(), own)
        self.send(0, me, h.dev(z=h.near(1)), own)
        self.mid_send(34, me, 2, 1, own)
        if self.split:
            self.send(24, self.tail(h.z, h.y, h.x), h.xdev(), self.own.at[pl.ds(self.cut, self.rows - self.cut)])

    def along_z(self, j):
        h = self.h
        part = self.head(h.near(j), h.y, h.x)
        self.wait(j - 1, part)
        if j == 1:
            self.mid_send(35, part, 2, 2)
        else:
            self.mid_send(34 + j, part, 1, j - 1)
        self.send(8 + j, part, h.xdev())
        self.send(4 + j, part, h.ydev())

    def along_y(self, j):
        h = self.h
        z = h.near(j)
        part = self.head(z, 1 - h.y, h.x)
        self.wait(4 + j, part)
        self.send(12 + j, part, h.xdev())
        self.send(16 + j, self.pair(z, h.x, h.c), h.sib())

    def along_x(self, j):
        h = self.h
        z = h.near(j)
        self.wait(8 + j, self.head(z, h.y, 1 - h.x))
        self.wait(12 + j, self.head(z, 1 - h.y, 1 - h.x))
        self.send(20 + j, self.pair(z, 1 - h.x, h.c), h.sib())

    def tail_x(self):
        h = self.h
        self.wait(24, self.tail(h.z, h.y, 1 - h.x))
        self.send(25, self.all.at[h.z, h.y, :, h.c, pl.ds(self.cut, self.rows - self.cut)], h.ydev())

    def tail_y(self):
        h = self.h
        self.wait(25, self.all.at[h.z, 1 - h.y, :, h.c, pl.ds(self.cut, self.rows - self.cut)])
        part = self.plane(h.z, h.c)
        self.send(26, part, h.dev(z=h.near(1)))
        self.mid_send(38, part, 2, 27)
        self.send(30, part, h.sib())

    def tail_z(self, j):
        h = self.h
        part = self.plane(h.near(j), h.c)
        self.wait(25 + j, part)
        if j == 1:
            self.mid_send(39, part, 2, 28)
        else:
            self.mid_send(38 + j, part, 1, 25 + j)
        self.send(30 + j, part, h.sib())

    def steps(self):
        p = functools.partial
        x, y, z = self.along_x, self.along_y, self.along_z
        tx, ty, tz = ([p(f)] if self.split else [] for f in (self.tail_x, self.tail_y, self.tail_z))
        order = [self.local.wait, p(y, 0), p(z, 1)] + tx + [p(x, 0), p(z, 2), p(y, 1)] + ty
        order += [p(z, 3), p(x, 1), p(y, 2)] + [p(f, 1) for f in tz] + [p(x, 2), p(y, 3)]
        return order + [p(f, j) for f in tz for j in (2, 3)] + [p(x, 3)]

    def finish(self):
        h = self.h
        c = 1 - h.c
        for j in range(4):
            z = h.near(j)
            self.wait(16 + j, self.pair(z, h.x, c))
            self.wait(20 + j, self.pair(z, 1 - h.x, c))
            if self.split:
                self.wait(30 + j, self.plane(z, c))

    def drain(self):
        for cp in self.mids:
            pl.when(self.h.middle)(lambda cp=cp: cp.wait_send())


class Scatter:
    def __init__(self, h, dw, l1, lxa, lya, lza, lzb, lyb, lxb, ss, rs, out, sent):
        self.h, self.dw, self.l1, self.lxa, self.lya = h, dw, l1, lxa, lya
        self.lza, self.lzb, self.lyb, self.lxb, self.ss, self.rs = lza, lzb, lyb, lxb, ss, rs
        self.out, self.sent = out, sent
        self.all = dw.reshape(4, 2, 2, 2, SHARD, C)
        self.head, self.tail = pl.ds(0, SUM_CUT), pl.ds(SUM_CUT, SHARD - SUM_CUT)

    def at(self, i, lo=0, n=SHARD):
        return self.dw.at[pl.ds(pl.multiple_of(i * SHARD + lo, 16), n)]

    def send(self, k, src, dst, dev):
        cp = rcopy(src, dst, self.ss.at[k], self.rs.at[k], dev)
        cp.start()
        self.sent.append(cp)

    def wait(self, k, land):
        rcopy(land, land, self.ss.at[0], self.rs.at[k], self.h.sib()).wait_recv()

    def add(self, i, lo, n, *parts):
        d = self.at(i, lo, n)
        total = d[...].astype(F32)
        for part in parts:
            total = total + part.astype(F32)
        d[...] = total.astype(BF)

    def s1(self, q):
        self.send(q, self.all.at[q, :, :, 1 - self.h.c], self.l1.at[q], self.h.sib())

    def _far(self, q):
        h = self.h
        return rcopy(
            self.all.at[q, :, :, h.c, self.tail], self.lzb.at[h.z], self.ss.at[16 + q], self.rs.at[20 + h.z], h.dev(z=q)
        )

    def s2(self, q):
        h = self.h
        self.wait(q, self.l1.at[q])
        for j in range(4):
            self.add(h.idx(q, j // 2, j % 2), 0, SHARD, self.l1[q, j // 2, j % 2])
        self.send(4 + q, self.all.at[q, :, 1 - h.x, h.c, self.head], self.lxa.at[q], h.xdev())
        pl.when(h.z != q)(lambda: self._far(q).start())

    def s3(self, q):
        h = self.h
        self.wait(4 + q, self.lxa.at[q])
        for j in range(2):
            self.add(h.idx(q, j), 0, SUM_CUT, self.lxa[q, j])
        self.send(8 + q, self.all.at[q, 1 - h.y, h.x, h.c, self.head], self.lya.at[q], h.ydev())

    def _near(self, q):
        h = self.h
        return rcopy(
            self.all.at[q, h.y, h.x, h.c, self.head], self.lza.at[h.z], self.ss.at[12 + q], self.rs.at[24 + h.z], h.dev(z=q)
        )

    def s4(self, q):
        h = self.h
        self.wait(8 + q, self.lya.at[q])
        self.add(h.idx(q), 0, SUM_CUT, self.lya[q])
        pl.when(h.z != q)(lambda: self._near(q).start())

    def t1(self):
        h = self.h
        for j in (1, 2, 3):
            self.wait(20 + h.near(j), self.lzb.at[h.near(j)])
        for j in range(4):
            parts = [self.lzb[h.near(k), j // 2, j % 2] for k in (1, 2, 3)]
            self.add(h.idx(None, j // 2, j % 2), SUM_CUT, SHARD - SUM_CUT, *parts)
        self.send(28, self.all.at[h.z, 1 - h.y, :, h.c, self.tail], self.lyb, h.ydev())

    def t2(self):
        h = self.h
        self.wait(28, self.lyb)
        for j in range(2):
            self.add(h.idx(None, None, j), SUM_CUT, SHARD - SUM_CUT, self.lyb[j])
        self.send(29, self.all.at[h.z, h.y, 1 - h.x, h.c, self.tail], self.lxb, h.xdev())

    def finish(self, extra):
        h = self.h
        self.wait(29, self.lxb)
        self.out[SUM_CUT:] = (
            self.at(h.idx(), SUM_CUT, SHARD - SUM_CUT)[...].astype(F32) + self.lxb[...].astype(F32) + extra[SUM_CUT:]
        )
        total = self.at(h.idx(), 0, SUM_CUT)[...].astype(F32) + extra[:SUM_CUT]
        for j in (1, 2, 3):
            self.wait(24 + h.near(j), self.lza.at[h.near(j)])
            total = total + self.lza[h.near(j)].astype(F32)
        self.out[:SUM_CUT] = total

    def drain(self):
        for q in range(4):

            @pl.when(self.h.z != q)
            def _(q=q):
                self._near(q).wait_send()
                self._far(q).wait_send()


class Halo:
    def __init__(self, h, edges, land, ss, rs):
        self.h, self.edges, self.land, self.ss, self.rs = h, edges, land, ss, rs
        self.up = rcopy(edges.at[0], land.at[1], ss.at[0], rs.at[0], h.dev(z=h.z - 1))
        self.down = rcopy(edges.at[1], land.at[0], ss.at[1], rs.at[1], h.dev(z=h.z + 1))

    def start_one(self, k):
        to = self.h.z + 2 * k - 1
        cp = rcopy(self.edges.at[k], self.land.at[1 - k], self.ss.at[k], self.rs.at[k], self.h.dev(z=to))
        pl.when((to >= 0) & (to <= 3))(lambda: cp.start())

    def start(self):
        pl.when(self.h.z > 0)(lambda: self.up.start())
        pl.when(self.h.z < 3)(lambda: self.down.start())

    def wait(self):
        @pl.when(self.h.z > 0)
        def _():
            self.up.wait_send()
            self.down.wait_recv()

        @pl.when(self.h.z < 3)
        def _():
            self.down.wait_send()
            self.up.wait_recv()


class Sums:
    def __init__(self, h, buf, ss, rs, sent):
        self.h, self.buf, self.ss, self.rs, self.sent = h, buf, ss, rs, sent

    def start_plane(self, payload):
        h = self.h
        self.own = payload
        mine = self.buf.at[2, 0]
        mine[...] = payload
        for r in (1, 2, 3):
            _, x, c = h.other(0, r // 2, r % 2)
            cp = rcopy(mine, self.buf.at[0, h.gy], self.ss.at[r - 1], self.rs.at[r - 1], h.dev(x=x, c=c))
            cp.start()
            self.sent.append(cp)

    def plane(self):
        h = self.h
        for r in (1, 2, 3):
            _, x, c = h.other(0, r // 2, r % 2)
            land = self.buf.at[0, x * 2 + c]
            rcopy(land, land, self.ss.at[0], self.rs.at[r - 1], h.sib()).wait_recv()
        return [jnp.where(h.gy == g, self.own, self.buf[0, g]) for g in range(4)]

    def start_z(self, payload):
        h = self.h
        self.own = payload
        mine = self.buf.at[2, 1]
        mine[...] = payload
        for j in (1, 2, 3):
            cp = rcopy(mine, self.buf.at[1, h.z], self.ss.at[2 + j], self.rs.at[3 + h.z], h.dev(z=h.near(j)))
            cp.start()
            self.sent.append(cp)

    def along_z(self):
        h = self.h
        for j in (1, 2, 3):
            land = self.buf.at[1, h.near(j)]
            rcopy(land, land, self.ss.at[0], self.rs.at[3 + h.near(j)], h.sib()).wait_recv()
        return [jnp.where(h.z == g, self.own, self.buf[1, g]) for g in range(4)]


def fold(row):
    return [row[:, 128 * k : 128 * (k + 1)] for k in range(4)]


def pack_rows(*rows):
    rows = rows + (jnp.zeros((1, C), F32),) * (4 - len(rows))
    return jnp.concatenate([part for r in rows for part in fold(r)], axis=0)


def unpack_rows(p):
    return [jnp.concatenate([p[4 * n + k : 4 * n + k + 1] for k in range(4)], axis=1) for n in range(p.shape[0] // 4)]


def column(r):
    return jnp.broadcast_to(r, (128, C)).T


def merge(parts, counts):
    total = sum(counts)
    mass = sum(parts[g][0:4] for g in range(4))
    mean = mass / jnp.maximum(total, 1.0)
    spread = jnp.zeros_like(mass)
    for g in range(4):
        n = jnp.maximum(counts[g], 1.0)
        gap = parts[g][0:4] / n - mean
        spread = spread + parts[g][4:8] + counts[g] * gap * gap
    third = parts[0] + parts[1] + parts[2] + parts[3]
    return jnp.concatenate([mass, spread, third[8:16]], axis=0)


def nn(a, b):
    return lax.dot_general(a, b, (((1,), (0,)), ((), ())), preferred_element_type=F32)


def nt(a, b):
    return lax.dot_general(a, b, (((1,), (1,)), ((), ())), preferred_element_type=F32)


def tn(a, b):
    return lax.dot_general(a, b, (((0,), (0,)), ((), ())), preferred_element_type=F32)


def sigmoid(u):
    return 1.0 / (1.0 + jnp.exp(-u))


def body(
    feat, w1s, w2s, gain, bias, head, hbias, labels, heights, widths, picks,
    pooled_out, fg_out, c1_out, c2_out, gg_out, bg_out, hg_out, hbg_out,
    w1, w2, x3, first, second, slope, dh, base, hid, dw,
    al, edges, bland, hland, sland, fland, fgs, fgl,
    e32, exts, ext, gb, stat, pacc, pz, pg, res, cot, yb, ht, gsc, mc1, mc2,
    l1, lxa, lya, lza, lzb, lyb, lxb,
    sem_g, rem_g, sem_ge, rem_ge, sem_l, sem_h, rem_h, sem_s, rem_s, sem_a, rem_a, sem_p, rem_p, sem_r, rem_r,
):
    h = Here()
    sent = []
    z, y = h.z, h.y

    barrier = pltpu.get_barrier_semaphore()
    peers = [h.dev(z=h.near(j)) for j in (1, 2, 3)]
    for r in range(1, 8):
        yy, xx, cc = h.other(r // 4, (r // 2) % 2, r % 2)
        peers.append(h.dev(y=yy, x=xx, c=cc))
    for dev in peers:
        pl.semaphore_signal(barrier, inc=1, device_id=dev, device_id_type=MESH)
    pl.semaphore_wait(barrier, len(peers))

    def swap_rows(lo, n, r, k):
        src = feat.at[pl.ds(PER * (1 - y) + lo, n), r]
        return rcopy(src, al.at[pl.ds(lo, n), r], sem_a.at[4 + k], rem_a.at[4 + k], h.ydev())

    swap = [swap_rows(0, 3, y, 0), swap_rows(3, 3, y, 1)] + [swap_rows(2 * k, 2, 1 - y, 2 + k) for k in range(3)]
    g1 = Gather(h, w1s, w1, sem_g.at[0], rem_g.at[0], sem_l.at[0], SHARD, CUT, sent)
    sent2 = []
    g2 = Gather(h, w2s, w2, sem_g.at[1], rem_g.at[1], sem_l.at[1], SHARD, CUT, sent2)
    ge = Gather(h, exts, ext, sem_ge, rem_ge, sem_l.at[2], 16, 16, sent)
    g1.start()
    swap[0].start()
    swap[1].start()
    e32[...] = jnp.zeros_like(e32)
    place = lax.broadcasted_iota(jnp.int32, (4, 128), 1) // 16
    both = jnp.concatenate([gain[...].astype(F32), bias[...].astype(F32)], axis=0)
    both = jnp.concatenate([both] * 8, axis=1)
    e32[0:4, 0:128] = jnp.where(place == lax.rem(h.idx(), 8), both, 0.0)
    e32[:, 256 : 256 + TASKS] = head[...].astype(F32)
    e32[0:12, 384 : 384 + TASKS] = labels[...].astype(F32)
    exts[...] = e32[...].astype(BF)
    ge.start()

    image = lax.broadcasted_iota(jnp.int32, (1, 8 * PER), 1)
    high = broad = jnp.zeros((1, 8 * PER), jnp.int32)
    for k in range(8 * PER):
        high = jnp.where(image == k, heights[k], high)
        broad = jnp.where(image == k, widths[k], broad)

    def pixels(zz, lo, n):
        here = (image >= lo) & (image < lo + n)
        cells = jnp.where(here, jnp.clip(high - ROWS * zz, 0, ROWS) * broad, 0).astype(F32)
        return cells.sum(1, keepdims=True)

    n_plane = [pixels(z, 2 * PER * g + PER * y, PER) for g in range(4)]
    n_z = [sum(pixels(zz, 2 * PER * g + PER * y, PER) for g in range(4)) for zz in range(4)]
    total = sum(n_z)
    my_first = h.gy * 2 * PER + PER * y

    col = lax.broadcasted_iota(jnp.int32, (COLS, C), 0)

    def wide(i, r):
        return jnp.where(ROWS * z + r < heights[my_first + i], widths[my_first + i], 0)

    def keep(i, r, v):
        return jnp.where(col < wide(i, r), v, 0.0)

    zero8 = jnp.zeros((8, C), F32)

    def by8(v):
        return v.reshape(COLS // 8, 8, C).sum(0)

    def put3(i, row, v):
        x3[i, row, :, C : 2 * C] = v.astype(BF)
        x3[i, row, :, 0:C] = jnp.where(col == 0, 0.0, pltpu.roll(v, 1, 0)).astype(BF)
        x3[i, row, :, 2 * C : 3 * C] = jnp.where(col == COLS - 1, 0.0, pltpu.roll(v, COLS - 1, 0)).astype(BF)

    def put_halo(land):
        def one(i, _):
            @pl.when(z > 0)
            def _():
                put3(i, 0, land[0, i].astype(F32))

            @pl.when(z == 0)
            def _():
                x3[i, 0] = jnp.zeros((COLS, 3 * C), BF)

            @pl.when(z < 3)
            def _():
                put3(i, 5, land[1, i].astype(F32))

            @pl.when(z == 3)
            def _():
                x3[i, 5] = jnp.zeros((COLS, 3 * C), BF)

            return 0

        lax.fori_loop(0, PER, one, 0)

    def take_row(src, offset, r, row, i, acc):
        v = keep(i, row, src[offset + i, r].astype(F32))
        base[i, row] = v.astype(BF)
        put3(i, row + 1, v)
        return acc + by8(v)

    def take_edge(k, src, offset, r, i, acc):
        acc = take_row(src, offset, r, 3 * k, i, acc)
        edges[k, i] = base[i, 3 * k]
        return acc

    halo = Halo(h, edges, bland, sem_h.at[0], rem_h.at[0])
    base_sum = lax.fori_loop(0, PER, lambda i, acc: take_edge(y, feat, PER * y, y, i, acc), zero8)
    halo.start_one(y)
    base_sum = lax.fori_loop(0, PER, lambda i, acc: take_row(feat, PER * y, 1 - y, 1 + y, i, acc), base_sum)

    def edges_in(k, acc):
        swap[k].wait_recv()
        return lax.fori_loop(3 * k, 3 * k + 3, lambda i, acc: take_edge(1 - y, al, 0, 1 - y, i, acc), acc)

    def rows_in(k, acc):
        swap[2 + k].wait_recv()
        return lax.fori_loop(2 * k, 2 * k + 2, lambda i, acc: take_row(al, 0, y, 2 - y, i, acc), acc)

    todo1, late = g1.steps(), 9
    todo2, todoe = [], ge.steps()
    for t, step in enumerate(todo1):
        step()
        if t >= 1 and todoe:
            todoe.pop(0)()
        if t in (2, 4, 6):
            swap[1 + t // 2].start()
        if t == late - 1:
            g2.start()
            todo2 = g2.steps()
        elif t >= late:
            todo2.pop(0)()
        if t == 5:
            base_sum = edges_in(0, base_sum)
        if t == 8:
            base_sum = edges_in(1, base_sum)
            halo.start_one(1 - y)
        if t in (10, 12, 14):
            base_sum = rows_in((t - 10) // 2, base_sum)
    base_sum = base_sum.sum(0, keepdims=True)
    g1.finish()
    steps = todo2
    def go(todo, n):
        for _ in range(min(n, len(todo))):
            todo.pop(0)()

    def conv(w, out, land, halo, todo=()):
        for p in range(3):
            im = pl.ds(2 * p, 2)
            mid = nn(x3[im, 1:5].reshape(8 * COLS, 3 * C), w[3 * C : 6 * C]).reshape(2, 4, COLS, C)
            lo = nn(x3[im, 1:4].reshape(6 * COLS, 3 * C), w[0 : 3 * C]).reshape(2, 3, COLS, C)
            hi = nn(x3[im, 2:5].reshape(6 * COLS, 3 * C), w[6 * C : 9 * C]).reshape(2, 3, COLS, C)
            out[im, 0] = mid[:, 0] + hi[:, 0]
            out[im, 1] = mid[:, 1] + lo[:, 0] + hi[:, 1]
            out[im, 2] = mid[:, 2] + lo[:, 1] + hi[:, 2]
            out[im, 3] = mid[:, 3] + lo[:, 2]
            go(todo, 1)
        halo.wait()
        go(todo, 1)
        put_halo(land)
        out[:, 0] += nn(x3[:, 0].reshape(6 * COLS, 3 * C), w[0 : 3 * C]).reshape(PER, COLS, C)
        out[:, 3] += nn(x3[:, 5].reshape(6 * COLS, 3 * C), w[6 * C : 9 * C]).reshape(PER, COLS, C)

    def conv_back(w, out, land, halo, todo=()):

        def taps(lhs, a):
            acc = None
            for b in range(3):
                part = nt(lhs[:, (2 - b) * C : (3 - b) * C], w[(3 * a + b) * C : (3 * a + b + 1) * C])
                acc = part if acc is None else acc + part
            return acc

        for p in range(3):
            im = pl.ds(2 * p, 2)
            mid = taps(x3[im, 1:5].reshape(8 * COLS, 3 * C), 1).reshape(2, 4, COLS, C)
            lo = taps(x3[im, 1:4].reshape(6 * COLS, 3 * C), 2).reshape(2, 3, COLS, C)
            hi = taps(x3[im, 2:5].reshape(6 * COLS, 3 * C), 0).reshape(2, 3, COLS, C)
            out[im, 0] = mid[:, 0] + hi[:, 0]
            out[im, 1] = mid[:, 1] + lo[:, 0] + hi[:, 1]
            out[im, 2] = mid[:, 2] + lo[:, 1] + hi[:, 2]
            out[im, 3] = mid[:, 3] + lo[:, 2]
            if todo:
                todo[p]()
        halo.wait()
        put_halo(land)
        if todo:
            todo[3]()
        out[:, 0] += taps(x3[:, 0].reshape(6 * COLS, 3 * C), 2).reshape(PER, COLS, C)
        out[:, 3] += taps(x3[:, 5].reshape(6 * COLS, 3 * C), 0).reshape(PER, COLS, C)

    def spread(src):
        def one(i, carry):
            n, mean, dev = carry
            widths_i = [wide(i, r) for r in range(ROWS)]
            ni = sum(widths_i).astype(F32)
            mass = jnp.zeros((8, C), F32)
            for r in range(ROWS):
                v = jnp.where(col < widths_i[r], src[i, r], 0.0)
                mass = mass + v.reshape(COLS // 8, 8, C).sum(0)
            mi = mass.sum(0, keepdims=True) / jnp.maximum(ni, 1.0)
            sq = jnp.zeros((8, C), F32)
            for r in range(ROWS):
                v = jnp.where(col < widths_i[r], src[i, r] - mi, 0.0)
                sq = sq + (v * v).reshape(COLS // 8, 8, C).sum(0)
            both = jnp.maximum(n + ni, 1.0)
            gap = mi - mean
            return (
                n + ni,
                mean + gap * (ni / both),
                dev + sq.sum(0, keepdims=True) + gap * gap * (n * ni / both),
            )

        zero = jnp.zeros((1, C), F32)
        n, mean, dev = lax.fori_loop(0, PER, one, (jnp.float32(0.0), zero, zero))
        return mean * n, dev

    def statistics(src, k, todo, inputs):
        ex = Sums(h, stat.at[k], sem_s.at[k], rem_s.at[k], sent)
        ex.start_plane(pack_rows(*spread(src), inputs))
        go(todo, 2)
        ex.start_z(merge(ex.plane(), n_plane))
        go(todo, 2)
        both = merge(ex.along_z(), n_z)
        mass, dev, inputs, _ = unpack_rows(both)
        return mass / total, lax.rsqrt(dev / total + norm_eps), inputs / total

    def start_sums(k, *rows):
        ex = Sums(h, stat.at[k], sem_s.at[k], rem_s.at[k], sent)
        ex.start_plane(pack_rows(*rows))
        return ex

    def mid_sums(ex):
        parts = ex.plane()
        ex.start_z(parts[0] + parts[1] + parts[2] + parts[3])

    def end_sums(ex):
        parts = ex.along_z()
        return parts[0] + parts[1] + parts[2] + parts[3]

    def edges_first(one, start):
        def edge(i, acc):
            for k, r in enumerate((0, ROWS - 1)):
                v = one(i, r)
                edges[k, i] = v.astype(BF)
                acc = acc + by8(v)
            return acc

        def inner(i, acc):
            for r in range(1, ROWS - 1):
                acc = acc + by8(one(i, r))
            return acc

        acc = lax.fori_loop(0, PER, edge, zero8)
        start()
        return lax.fori_loop(0, PER, inner, acc).sum(0, keepdims=True)

    conv(w1, first, bland, halo, steps)
    center, rs1, base_mean = statistics(first, 0, steps, base_sum)
    ge.finish()

    for k in range(4):
        tile = sum(ext[16 * d : 16 * d + 16, 0:128].astype(F32) for d in range(8 * k, 8 * k + 8))
        gb[0:4, 128 * k : 128 * (k + 1)] = tile[0:4]
    ht[...] = ext[:, 256:384].astype(F32)
    gain1, bias1 = gb[0:1], gb[2:3]

    def hidden(i, r):
        xh = (first[i, r] - center) * rs1
        first[i, r] = xh
        u = gain1 * xh + bias1
        v = keep(i, r, u * sigmoid(u))
        hid[i, r] = v.astype(BF)
        put3(i, r + 1, v)
        return v

    halo = Halo(h, edges, hland, sem_h.at[1], rem_h.at[1])
    def after_hidden():
        halo.start()
        go(steps, 2)

    hid_sum = edges_first(hidden, after_hidden)
    go(steps, 99)
    g2.finish()
    conv(w2, second, hland, halo, [])
    center, rs2, hid_mean = statistics(second, 1, [], hid_sum)
    gain2, bias2 = gb[1:2], gb[3:4]

    pacc[...] = jnp.zeros_like(pacc)

    def finals(i, _):
        acc = [jnp.zeros((8, C), F32) for _ in range(3)]
        for r in range(ROWS):
            xh = (second[i, r] - center) * rs2
            second[i, r] = xh
            pre = gain2 * xh + bias2 + base[i, r].astype(F32)
            s = sigmoid(pre)
            act = keep(i, r, pre * s)
            sl = keep(i, r, s * (1.0 + pre * (1.0 - s)))
            slope[i, r] = sl
            for k, v in enumerate((act, sl, sl * xh)):
                acc[k] = acc[k] + v.reshape(COLS // 8, 8, C).sum(0)
        for k in range(3):
            pacc[k, pl.ds(i, 1)] = acc[k].sum(0, keepdims=True)
        return 0

    lax.fori_loop(0, PER, finals, 0)

    rows8 = lax.broadcasted_iota(jnp.int32, (8, 1), 0)
    inv_pix = jnp.zeros((8, 1), F32)
    for i in range(PER):
        inv_pix = jnp.where(rows8 == i, 1.0 / (heights[my_first + i] * widths[my_first + i]).astype(F32), inv_pix)
    me_z = pz.at[z]
    me_z[...] = pacc[0]
    for j in (1, 2, 3):
        cp = rcopy(me_z, me_z, sem_p.at[j - 1], rem_p.at[z], h.dev(z=h.near(j)))
        cp.start()
        sent.append(cp)
    head_gram = lax.dot_general(ht[...], ht[...], (((0,), (0,)), ((), ())), precision=HIGH, preferred_element_type=F32)
    for j in (1, 2, 3):
        land = pz.at[h.near(j)]
        rcopy(land, land, sem_p.at[0], rem_p.at[h.near(j)], h.sib()).wait_recv()
    slot = (y * 2 + h.x) * 2 + h.c
    me_p = pg.at[slot]
    me_p[...] = (pz[0] + pz[1] + pz[2] + pz[3]) * inv_pix
    for r in range(1, 8):
        yy, xx, cc = h.other(r // 4, (r // 2) % 2, r % 2)
        cp = rcopy(me_p, me_p, sem_p.at[2 + r], rem_p.at[3 + r], h.dev(y=yy, x=xx, c=cc))
        cp.start()
        sent.append(cp)
    lane = lax.broadcasted_iota(jnp.int32, (8, 128), 1)
    row = lax.broadcasted_iota(jnp.int32, (8, 128), 0)
    real = (row < PER) & (lane < TASKS)
    wanted = []
    for s in range(8):
        yy, gy = s // 4, s % 4
        lab = ext[16 * gy : 16 * gy + 16, 384:512].astype(F32)
        lab = lab[PER * yy : PER * yy + PER]
        wanted.append(jnp.concatenate([lab, jnp.zeros((2, 128), F32)], axis=0))
    for r in range(1, 8):
        yy, xx, cc = h.other(r // 4, (r // 2) % 2, r % 2)
        land = pg.at[(yy * 2 + xx) * 2 + cc]
        rcopy(land, land, sem_p.at[0], rem_p.at[3 + r], h.sib()).wait_recv()
    pooled = pg[...].reshape(64, C)
    offset = jnp.concatenate([hbias[...].astype(F32), jnp.zeros((1, 128 - TASKS), F32)], axis=1)
    logits = lax.dot_general(pooled, ht[...], (((1,), (0,)), ((), ())), precision=HIGH, preferred_element_type=F32)
    logits = logits.reshape(8, 8, 128) + offset
    images = 8 * PER
    for s in range(8):
        res[s] = jnp.where(real, (sigmoid(logits[s]) - wanted[s]) / images, 0.0)
    residual = res[...].reshape(64, 128)
    gram = head_gram * lax.dot_general(
        residual, residual, (((0,), (0,)), ((), ())), precision=HIGH, preferred_element_type=F32
    )
    gram = gram[0:TASKS]
    lane1 = lax.broadcasted_iota(jnp.int32, (1, 128), 1)
    sub = lax.broadcasted_iota(jnp.int32, (TASKS, 128), 0)

    def fw(k, carry):
        mix, q = carry
        t = picks[k]
        one = (lane1 == t).astype(F32)
        line = jnp.where(sub == t, gram, 0.0).sum(0, keepdims=True)
        self_dot = (mix * q).sum(1, keepdims=True)
        cross = (one * q).sum(1, keepdims=True)
        vertex = (one * line).sum(1, keepdims=True)
        d = jnp.maximum(self_dot + vertex - 2.0 * cross, 0.1 * vertex)
        step = jnp.clip((self_dot - cross) / d, 0.0, 1.0)
        return (1.0 - step) * mix + step * one, (1.0 - step) * q + step * line

    mix0 = jnp.where(lane1 < TASKS, 1.0 / TASKS, 0.0)
    mix, _ = lax.fori_loop(0, STEPS, fw, (mix0, gram.sum(0, keepdims=True) / TASKS))
    mine = res[slot] * mix
    cot[...] = inv_pix * lax.dot_general(
        mine, ht[...], (((1,), (1,)), ((), ())), precision=HIGH, preferred_element_type=F32
    )
    ex = start_sums(
        2, (cot[...] * pacc[1]).sum(0, keepdims=True), (cot[...] * pacc[2]).sum(0, keepdims=True)
    )

    for yy in range(2):
        pooled_out[PER * yy : PER * (yy + 1)] = pg[(yy * 2 + h.x) * 2 + h.c][0:PER]
    head_grad = lax.dot_general(
        pooled, residual, (((0,), (0,)), ((), ())), precision=HIGH, preferred_element_type=F32
    )
    mid_sums(ex)
    gsc[...] = head_grad
    hg_out[...] = gsc[pl.ds(pl.multiple_of(h.idx() * 16, 16), 16)][:, 0:TASKS]
    hbg_out[...] = residual.sum(0, keepdims=True)[:, 0:TASKS]
    sums2 = end_sums(ex)
    yb[0, 0:8] = sums2[0:8]
    mc1[0:C] = column(base_mean)
    mc1[C:] = mc1[0:256]
    mc2[0:C] = column(hid_mean)
    mc2[C:] = mc2[0:256]
    yb[0, 24:32] = pack_rows(hid_mean, base_mean)[0:8]

    sum_b, sum_g, _, _ = unpack_rows(sums2)
    mean_b, mean_g = sum_b / total, sum_g / total
    scale = gain2 * rs2

    def d_second(i, r):
        xh = second[i, r]
        dp = slope[i, r] * cot[pl.ds(i, 1)]
        v = keep(i, r, scale * (dp - mean_b - xh * mean_g))
        put3(i, r + 1, v)
        return v.astype(BF).astype(F32)

    halo = Halo(h, edges, sland, sem_h.at[2], rem_h.at[2])
    d2_sum = edges_first(d_second, halo.start)
    conv_back(w2, dh, sland, halo)

    def d_norm1(i, carry):
        a, b = carry
        for r in range(ROWS):
            xh = first[i, r]
            u = gain1 * xh + bias1
            s = sigmoid(u)
            v = keep(i, r, dh[i, r] * (s * (1.0 + u * (1.0 - s))))
            dh[i, r] = v
            a = a + v.reshape(COLS // 8, 8, C).sum(0)
            b = b + (v * xh).reshape(COLS // 8, 8, C).sum(0)
        return a, b

    a, b = lax.fori_loop(0, PER, d_norm1, (zero8, zero8))
    ex = start_sums(3, a.sum(0, keepdims=True), b.sum(0, keepdims=True), d2_sum)

    def weight_taps(x, out, mean, d_sum, lo, hi):
        for t in range(lo, hi):
            ta, tb = t // 3, t % 3
            d = x3[:, 2 - ta : 6 - ta, :, (2 - tb) * C : (3 - tb) * C].reshape(PER * ROWS * COLS, C)
            part = tn(x[...].reshape(PER * ROWS * COLS, C), d)
            off = jnp.concatenate([mean[0:C] * f for f in fold(d_sum)], axis=1)
            out[t * C : (t + 1) * C] = (part - off).astype(BF)

    def scatter(k, src, out):
        return Scatter(
            h, src, l1.at[k], lxa.at[k], lya.at[k], lza.at[k], lzb.at[k], lyb.at[k], lxb.at[k], sem_r.at[k], rem_r.at[k],
            out, sent,
        )

    r2 = scatter(0, dw, c2_out)
    weight_taps(hid, dw, mc2, d2_sum, 0, 3)
    r2.s1(0)
    mid_sums(ex)
    weight_taps(hid, dw, mc2, d2_sum, 3, 5)
    r2.s1(1)
    r2.s2(0)
    weight_taps(hid, dw, mc2, d2_sum, 5, 7)
    r2.s1(2)
    r2.s2(1)
    weight_taps(hid, dw, mc2, d2_sum, 7, 9)
    r2.s1(3)
    r2.s2(2)
    sums1 = end_sums(ex)
    yb[0, 8:20] = sums1[0:12]
    sum_b, sum_g, _, _ = unpack_rows(sums1)
    mean_b1, mean_g1 = sum_b / total, sum_g / total
    scale1 = gain1 * rs1

    def d_first(i, r):
        v = keep(i, r, scale1 * (dh[i, r] - mean_b1 - first[i, r] * mean_g1))
        put3(i, r + 1, v)
        return v.astype(BF).astype(F32)

    halo = Halo(h, edges, fland, sem_h.at[3], rem_h.at[3])
    d1_sum = edges_first(d_first, halo.start)
    r2.s2(3)
    ex = start_sums(4, d1_sum)
    for cp in sent2:
        cp.wait_send()
    g2.drain()
    r1 = scatter(1, w2, c1_out)
    weight_taps(base, w2, mc1, d1_sum, 3, 6)

    def other_taps():
        weight_taps(base, w2, mc1, d1_sum, 0, 3)
        r1.s1(0)
        r1.s1(1)
        weight_taps(base, w2, mc1, d1_sum, 6, 7)
        r1.s1(2)
        weight_taps(base, w2, mc1, d1_sum, 7, 8)
        r1.s2(0)
        weight_taps(base, w2, mc1, d1_sum, 8, 9)
        r1.s1(3)
        r1.s2(1)

    conv_back(w1, dh, fland, halo, [functools.partial(r2.s3, q) for q in range(3)] + [other_taps])
    r1.s2(2)
    mid_sums(ex)
    r2.s4(0)

    def result(i, r):
        return keep(i, r, dh[i, r] + slope[i, r] * cot[pl.ds(i, 1)])

    back = []
    for i in range(PER):
        for r in range(2):
            fgs[i, r] = result(i, 2 * (1 - y) + r).astype(BF)
        back.append(rcopy(fgs.at[i], fgl.at[i], sem_a.at[9 + i], rem_a.at[9 + i], h.ydev()))
        if i < 3:
            back[i].start()

    def stay(i, _):
        for r in range(2):
            fg_out[PER * y + i, r] = result(i, 2 * y + r).astype(BF)
        return 0

    lax.fori_loop(0, PER, stay, 0)
    r1.s2(3)
    r2.s3(3)
    r2.s4(1)
    yb[0, 20:24] = end_sums(ex)[0:4]
    ysum = rcopy(yb.at[0], yb.at[1], sem_a.at[0], rem_a.at[0], h.ydev())
    ysum.start()
    r2.s4(2)
    r1.s3(0)
    back[3].start()
    r2.s4(3)
    r2.t1()
    r1.s3(1)
    back[4].start()
    r1.s4(0)

    ysum.wait_recv()
    sb2, sg2, sb1, sg1 = unpack_rows(yb[0, 0:16] + yb[1, 0:16])
    tile = jnp.zeros((4, 128), F32)
    for k in range(4):
        rows = [v[:, 128 * k : 128 * (k + 1)] for v in (sg1, sg2, sb1, sb2)]
        tile = jnp.where(lax.div(h.idx(), 8) == k, jnp.concatenate(rows, axis=0), tile)
    own = jnp.zeros((4, 16), F32)
    for k in range(8):
        own = jnp.where(lax.rem(h.idx(), 8) == k, tile[:, 16 * k : 16 * (k + 1)], own)
    gg_out[...] = own[0:2]
    bg_out[...] = own[2:4]

    r2.t2()

    at = pl.ds(pl.multiple_of(lax.rem(h.idx() * SHARD, C), 16), SHARD)
    d2_all, d1_all, hid_other, base_other = unpack_rows(yb[1, 16:32])
    d2_mine, d1_mine, _, _ = unpack_rows(yb[0, 16:32])

    def taken_off(mean, other, all_mine, all_other):
        off = jnp.concatenate([mean[at] * f for f in fold(all_mine)], axis=1)
        mean[0:C] = column(other)
        mean[C:] = mean[0:256]
        return off + jnp.concatenate([mean[at] * f for f in fold(all_other)], axis=1)

    off2 = taken_off(mc2, hid_other, d2_mine, d2_all)
    off1 = taken_off(mc1, base_other, d1_mine, d1_all)
    r2.finish(off2)

    def land_rows(i):
        back[i].wait_recv()
        fg_out[PER * (1 - y) + i] = fgl[i]

    land_rows(0)
    r1.s3(2)
    r1.s4(1)
    r1.t1()
    land_rows(1)
    r1.s3(3)
    back[5].start()
    r1.s4(2)
    r1.t2()
    land_rows(2)
    land_rows(3)
    land_rows(4)
    r1.s4(3)
    land_rows(5)
    r1.finish(off1)

    ysum.wait_send()
    g1.drain()
    ge.drain()
    for cp in swap + back + sent:
        cp.wait_send()
    r1.drain()
    r2.drain()


def fused(features, w1s, w2s, gain, bias, head, head_bias, labels, heights, widths, picks):
    vm = pl.BlockSpec(memory_space=pltpu.VMEM)
    sm = pl.BlockSpec(memory_space=pltpu.SMEM)
    V = pltpu.VMEM
    dma = pltpu.SemaphoreType.DMA
    maps = (PER, ROWS, COLS, C)
    edge = (2, PER, COLS, C)
    half = (PER, 2, COLS, C)
    scratch = [
        V((9 * C, C), BF), V((9 * C, C), BF), V((PER, ROWS + 2, COLS, 3 * C), BF),
        V(maps, F32), V(maps, F32), V(maps, F32), V(maps, F32), V(maps, BF), V(maps, BF), V((9 * C, C), BF),
        V(half, BF), V(edge, BF), V(edge, BF), V(edge, BF), V(edge, BF), V(edge, BF), V(half, BF), V(half, BF),
        V((16, C), F32), V((16, C), BF), V((C, C), BF), V((8, C), F32),
        V((5, 3, 4, 16, 128), F32), V((3, 8, C), F32), V((4, 8, C), F32), V((8, 8, C), F32),
        V((8, 8, 128), F32), V((8, C), F32), V((2, 32, 128), F32), V((C, 128), F32), V((C, 128), F32),
        V((C + 256, 128), F32), V((C + 256, 128), F32),
        V((2, 4, 2, 2, SHARD, C), BF), V((2, 4, 2, SUM_CUT, C), BF), V((2, 4, SUM_CUT, C), BF), V((2, 4, SUM_CUT, C), BF),
        V((2, 4, 2, 2, SHARD - SUM_CUT, C), BF), V((2, 2, SHARD - SUM_CUT, C), BF), V((2, SHARD - SUM_CUT, C), BF),
        dma((2, 48)), dma((2, 48)), dma((48,)), dma((48,)), dma((3,)), dma((4, 2)), dma((4, 2)),
        dma((5, 8)), dma((5, 8)), dma((15,)), dma((15,)), dma((12,)), dma((12,)), dma((2, 48)), dma((2, 48)),
    ]
    f = jax.ShapeDtypeStruct
    outs = pl.pallas_call(
        body,
        out_shape=[
            f((2 * PER, C), F32), f((2 * PER, 2, COLS, C), BF), f((SHARD, C), F32), f((SHARD, C), F32),
            f((2, 16), F32), f((2, 16), F32), f((16, TASKS), F32), f((1, TASKS), F32),
        ],
        in_specs=[vm] * 8 + [sm] * 3,
        out_specs=[vm] * 8,
        scratch_shapes=scratch,
        compiler_params=pltpu.CompilerParams(
            collective_id=0, has_side_effects=True, vmem_limit_bytes=63 * 2**20
        ),
        name="block",
    )(
        features, w1s, w2s, gain.T, bias.T, head, head_bias.reshape(1, TASKS), labels, heights, widths, picks,
    )
    pooled, fg, c1, c2, gg, bg, hg, hbg = outs
    return pooled, fg.astype(F32), c1, c2, gg.T, bg.T, hg, hbg.reshape(TASKS)


def extended(cells, sides, width):
    for axis, dim in sides:
        count = lax.axis_size(axis)
        ends = count - 1
        head = lax.slice_in_dim(cells, 0, width, axis=dim)
        tail = lax.slice_in_dim(cells, cells.shape[dim] - width, cells.shape[dim], axis=dim)
        cells = jnp.concatenate(
            [
                lax.ppermute(tail, axis, [(i, (i + 1) % count) for i in range(ends)]),
                cells,
                lax.ppermute(head, axis, [((i + 1) % count, i) for i in range(ends)]),
            ],
            axis=dim,
        )
    return cells


def make_patches(padded, row_count, col_count):
    widened = jnp.pad(padded, ((0, 0), (0, 0), (1, 1), (0, 0)))
    pieces = [
        widened[:, row_off : row_off + row_count, col_off : col_off + col_count, :]
        for row_off in range(3)
        for col_off in range(3)
    ]
    joined = jnp.concatenate(pieces, axis=-1)
    return joined.reshape(-1, joined.shape[-1])


def conv_rows(act, weight):
    padded = extended(act, (("gx", 1),), 1)
    patches = make_patches(padded, act.shape[1], act.shape[2])
    output = jnp.dot(patches, weight, preferred_element_type=jnp.float32)
    return (output.reshape(act.shape[:3] + (weight.shape[1],)), padded)


def reversed_taps(weight):
    channels = weight.shape[1]
    taps = weight.reshape(9, channels, channels)[::-1]
    return jnp.transpose(taps, (0, 2, 1)).reshape(9 * channels, channels)


def weight_term(padded, grad_bf):
    patches = make_patches(padded, grad_bf.shape[1], grad_bf.shape[2])
    flat_grad = grad_bf.reshape(-1, grad_bf.shape[-1])
    return lax.dot_general(
        patches, flat_grad, (((0,), (0,)), ((), ())), preferred_element_type=jnp.float32
    )


def batch_statistics(values, inner_result, pixel_total):
    center_val = (
        lax.psum(jnp.sum(values * inner_result, axis=(0, 1, 2)), ("gx", "gy")) / pixel_total
    )
    centered = values - center_val
    spread_sq = (
        lax.psum(jnp.sum(inner_result * centered * centered, axis=(0, 1, 2)), ("gx", "gy"))
        / pixel_total
    )
    inverse_scale = lax.rsqrt(spread_sq + norm_eps)
    return (centered * inverse_scale, inverse_scale)


def norm_backward(
    output_gradient, normalized_input, inverse_scale, norm_scale_factor, inner_result, pixel_total
):
    bias_gradient_total, scale_gradient_total = lax.psum(
        (
            jnp.sum(output_gradient, axis=(0, 1, 2)),
            jnp.sum(output_gradient * normalized_input, axis=(0, 1, 2)),
        ),
        ("gx", "gy"),
    )
    backward_result = (
        norm_scale_factor
        * inverse_scale
        * (
            output_gradient
            - bias_gradient_total / pixel_total
            - normalized_input * scale_gradient_total / pixel_total
        )
        * inner_result
    )
    return (backward_result, scale_gradient_total, bias_gradient_total)


def silu_slope(values):
    sig_val = jax.nn.sigmoid(values)
    return sig_val * (1.0 + values * (1.0 - sig_val))


def frank_wolfe(gram, picks):
    task_ids = jnp.arange(TASKS)

    def fw_step(index, task_mix):
        onehot = (task_ids == picks[index]).astype(jnp.float32)
        mixed_vec = jnp.dot(gram, task_mix, precision=lax.Precision.HIGHEST)
        self_dot = jnp.sum(task_mix * mixed_vec)
        cross_dot = jnp.sum(onehot * mixed_vec)
        vertex_dot = jnp.sum(onehot * jnp.dot(gram, onehot, precision=lax.Precision.HIGHEST))
        distance = jnp.maximum(self_dot + vertex_dot - 2.0 * cross_dot, 0.1 * vertex_dot)
        step_size = jnp.clip((self_dot - cross_dot) / distance, 0.0, 1.0)
        return (1.0 - step_size) * task_mix + step_size * onehot

    start = jnp.full((TASKS,), 1.0 / TASKS, jnp.float32)
    return lax.fori_loop(0, STEPS, fw_step, start)


def on_device(
    features,
    conv1_weight,
    conv2_weight,
    norm_gain,
    norm_bias,
    head_weight,
    head_bias,
    labels,
    heights,
    widths,
    picks,
):
    image_count, row_count, col_count, channels = features.shape
    per_micro = image_count // MICRO
    total_images = image_count * lax.axis_size("gy")
    row_ids = lax.axis_index("gx") * row_count + jnp.arange(row_count)
    my_heights = lax.dynamic_slice_in_dim(heights, lax.axis_index("gy") * image_count, image_count)
    my_widths = lax.dynamic_slice_in_dim(widths, lax.axis_index("gy") * image_count, image_count)
    inside_all = (
        (row_ids[None, :, None] < my_heights[:, None, None])
        & (jnp.arange(col_count)[None, None, :] < my_widths[:, None, None])
    ).astype(jnp.float32)[..., None]
    pixel_count = (my_heights * my_widths).astype(jnp.float32)
    micro_pixels = jnp.sum((heights * widths).reshape(-1, MICRO, per_micro), axis=(0, 2)).astype(
        jnp.float32
    )

    def weights_now():
        return (
            lax.all_gather(conv1_weight, ("gx", "gy"), axis=0, tiled=True),
            lax.all_gather(conv2_weight, ("gx", "gy"), axis=0, tiled=True),
            lax.all_gather(norm_gain, ("gx", "gy"), axis=0, tiled=True),
            lax.all_gather(norm_bias, ("gx", "gy"), axis=0, tiled=True),
            lax.all_gather(head_weight, ("gx", "gy"), axis=0, tiled=True),
        )

    saved = []
    pooled_parts = []
    head_full = None
    for index in range(MICRO):
        conv_one, conv_two, gain_full, bias_full, head_full = weights_now()
        scale_factors = gain_full.astype(jnp.float32)
        bias_values = bias_full.astype(jnp.float32)
        inner_result = inside_all[index * per_micro : (index + 1) * per_micro]
        pixel_total = micro_pixels[index]
        base_input_bfloat = features[
            index * per_micro : (index + 1) * per_micro
        ] * inner_result.astype(jnp.bfloat16)
        first_convolution, padded_input = conv_rows(base_input_bfloat, conv_one)
        first_normalized, first_scale = batch_statistics(
            first_convolution, inner_result, pixel_total
        )
        first_norm_output = scale_factors[:, 0] * first_normalized + bias_values[:, 0]
        hidden_bf = (jax.nn.silu(first_norm_output) * inner_result).astype(jnp.bfloat16)
        second_convolution, padded_hidden_state = conv_rows(hidden_bf, conv_two)
        second_normalized, second_scale = batch_statistics(
            second_convolution, inner_result, pixel_total
        )
        before_activation = (
            scale_factors[:, 1] * second_normalized
            + bias_values[:, 1]
            + base_input_bfloat.astype(jnp.float32)
        )
        final_act = jax.nn.silu(before_activation) * inner_result
        pooled_parts.append(jnp.sum(final_act, axis=(1, 2)))
        saved.append(
            (
                padded_input,
                padded_hidden_state,
                first_normalized,
                first_scale,
                first_norm_output,
                second_normalized,
                second_scale,
                before_activation,
            )
        )
    pooled = lax.psum(jnp.concatenate(pooled_parts, axis=0), "gx") / pixel_count[:, None]
    head_mat = head_full.astype(jnp.float32)
    logits = jnp.dot(pooled, head_mat, precision=lax.Precision.HIGHEST) + head_bias.astype(
        jnp.float32
    )
    residual = (jax.nn.sigmoid(logits) - labels.astype(jnp.float32)) / total_images
    gram_part = jnp.dot(residual.T, residual, precision=lax.Precision.HIGHEST)
    head_part = jnp.dot(pooled.T, residual, precision=lax.Precision.HIGHEST)
    gram_sum, head_bias_grad, head_total = (
        lax.psum(gram_part.astype(jnp.bfloat16), "gy").astype(jnp.float32),
        lax.psum(jnp.sum(residual, axis=0).astype(jnp.bfloat16), "gy").astype(jnp.float32),
        lax.psum(head_part.astype(jnp.bfloat16), "gy").astype(jnp.float32),
    )
    gram = gram_sum * jnp.dot(head_mat.T, head_mat, precision=lax.Precision.HIGHEST)
    task_mix = frank_wolfe(gram, picks)
    pooled_cot = jnp.dot(residual * task_mix, head_mat.T, precision=lax.Precision.HIGHEST)
    shard_rows = 9 * channels // lax.axis_size(("gx", "gy"))
    conv1_grad = jnp.zeros((shard_rows, channels), jnp.float32)
    conv2_grad = jnp.zeros((shard_rows, channels), jnp.float32)
    gain_total = jnp.zeros((channels, 2), jnp.float32)
    bias_total = jnp.zeros((channels, 2), jnp.float32)
    feat_parts = []
    for index in range(MICRO):
        conv_one, conv_two, gain_full, bias_full, unused_heads = weights_now()
        scale_factors = gain_full.astype(jnp.float32)
        (
            padded_input,
            padded_hidden_state,
            first_normalized,
            first_scale,
            first_norm_output,
            second_normalized,
            second_scale,
            before_activation,
        ) = saved[index]
        inner_result = inside_all[index * per_micro : (index + 1) * per_micro]
        pixel_total = micro_pixels[index]
        cot_part = (
            pooled_cot[index * per_micro : (index + 1) * per_micro]
            / pixel_count[index * per_micro : (index + 1) * per_micro, None]
        )
        gradient_before_relu = (
            cot_part[:, None, None, :] * inner_result * silu_slope(before_activation)
        )
        d_second, gain_two, bias_two = norm_backward(
            gradient_before_relu,
            second_normalized,
            second_scale,
            scale_factors[:, 1],
            inner_result,
            pixel_total,
        )
        second_bf = d_second.astype(jnp.bfloat16)
        term_two = weight_term(padded_hidden_state, second_bf)
        d_hidden, unused_pad = conv_rows(second_bf, reversed_taps(conv_two))
        gradient_norm_first = d_hidden * inner_result * silu_slope(first_norm_output)
        d_first, gain_one, bias_one = norm_backward(
            gradient_norm_first,
            first_normalized,
            first_scale,
            scale_factors[:, 0],
            inner_result,
            pixel_total,
        )
        first_bf = d_first.astype(jnp.bfloat16)
        term_one = weight_term(padded_input, first_bf)
        d_base, unused_pad_two = conv_rows(first_bf, reversed_taps(conv_one))
        feat_parts.append((d_base + gradient_before_relu) * inner_result)
        gain_total = gain_total + jnp.stack([gain_one, gain_two], axis=1)
        bias_total = bias_total + jnp.stack([bias_one, bias_two], axis=1)
        shard_one, shard_two = (
            lax.psum_scatter(term_one, ("gx", "gy"), scatter_dimension=0, tiled=True),
            lax.psum_scatter(term_two, ("gx", "gy"), scatter_dimension=0, tiled=True),
        )
        conv1_grad = conv1_grad + shard_one
        conv2_grad = conv2_grad + shard_two
    flat_index = lax.axis_index(("gx", "gy"))
    chan_rows = channels // lax.axis_size(("gx", "gy"))
    gain_grad = lax.dynamic_slice_in_dim(gain_total, flat_index * chan_rows, chan_rows, 0)
    bias_grad = lax.dynamic_slice_in_dim(bias_total, flat_index * chan_rows, chan_rows, 0)
    head_grad = lax.dynamic_slice_in_dim(head_total, flat_index * chan_rows, chan_rows, 0)
    features_grad = jnp.concatenate(feat_parts, axis=0)
    return (
        pooled,
        features_grad,
        conv1_grad,
        conv2_grad,
        gain_grad,
        bias_grad,
        head_grad,
        head_bias_grad,
    )


def solution(mesh):
    in_specs = (
        P("gy", "gx", None, None),
        P(("gx", "gy"), None),
        P(("gx", "gy"), None),
        P(("gx", "gy"), None),
        P(("gx", "gy"), None),
        P(("gx", "gy"), None),
        P(),
        P("gy", None),
        P(),
        P(),
        P(),
    )
    out_specs = (
        P("gy", None),
        P("gy", "gx", None, None),
        P(("gx", "gy"), None),
        P(("gx", "gy"), None),
        P(("gx", "gy"), None),
        P(("gx", "gy"), None),
        P(("gx", "gy"), None),
        P(),
    )
    whole = dict(mesh.shape) != {"gx": 8, "gy": 4}
    return jax.shard_map(
        on_device if whole else fused, mesh=mesh, in_specs=in_specs, out_specs=out_specs, check_vma=False
    )
```

```python
import functools

import jax
import jax.numpy as jnp
from jax import lax
from jax.experimental import pallas as pl
from jax.experimental.pallas import tpu as pltpu
from jax.sharding import PartitionSpec as P

TASKS = 40
MICRO = 2
STEPS = 20
norm_eps = 1e-05
BF = jnp.bfloat16
F32 = jnp.float32
HIGH = lax.Precision.HIGHEST
MESH = pl.DeviceIdType.MESH

C = 512
COLS = 64
PER = 6
ROWS = 4
SHARD = 144
CUT = 112
SUM_CUT = 112


class Here:
    def __init__(self):
        gx = lax.axis_index("gx")
        gy = lax.axis_index("gy")
        self.z = lax.div(gx, 2)
        self.y = lax.rem(gx, 2)
        self.x = lax.div(gy, 2)
        self.c = lax.rem(gy, 2)
        self.gy = gy
        self.middle = lax.rem(self.z + 1, 4) >= 2

    def _fill(self, z, y, x, c):
        return (
            self.z if z is None else z,
            self.y if y is None else y,
            self.x if x is None else x,
            self.c if c is None else c,
        )

    def dev(self, z=None, y=None, x=None, c=None):
        z, y, x, c = self._fill(z, y, x, c)
        return {"gx": z * 2 + y, "gy": x * 2 + c}

    def idx(self, z=None, y=None, x=None, c=None):
        z, y, x, c = self._fill(z, y, x, c)
        return ((z * 2 + y) * 2 + x) * 2 + c

    def near(self, j):
        z = self.z
        if j == 0:
            return z
        if j == 1:
            return z + 1 - 2 * lax.rem(z, 2)
        if j == 2:
            return 2 - lax.div(z, 2)
        return 3 - 3 * lax.div(z, 2)

    def other(self, dy, dx, dc):
        return (
            1 - self.y if dy else self.y,
            1 - self.x if dx else self.x,
            1 - self.c if dc else self.c,
        )

    def ydev(self):
        return self.dev(y=1 - self.y)

    def xdev(self):
        return self.dev(x=1 - self.x)

    def sib(self):
        return self.dev(c=1 - self.c)


def rcopy(src, dst, ss, rs, dev):
    return pltpu.make_async_remote_copy(
        src_ref=src, dst_ref=dst, send_sem=ss, recv_sem=rs, device_id=dev, device_id_type=MESH
    )


class Gather:
    def __init__(self, h, own, out, ss, rs, lsem, rows, cut, sent):
        self.h, self.own, self.ss, self.rs = h, own, ss, rs
        self.lsem, self.rows, self.cut, self.sent = lsem, rows, cut, sent
        self.all = out.reshape(4, 2, 2, 2, rows, C)
        self.split = cut < rows
        self.mids = []

    def head(self, z, y, x):
        return self.all.at[z, y, x, self.h.c, pl.ds(0, self.cut)]

    def tail(self, z, y, x):
        return self.all.at[z, y, x, self.h.c, pl.ds(self.cut, self.rows - self.cut)]

    def pair(self, z, x, c):
        return self.all.at[z, :, x, c, pl.ds(0, self.cut)]

    def plane(self, z, c):
        return self.all.at[z, :, :, c, pl.ds(self.cut, self.rows - self.cut)]

    def send(self, k, ref, dev, src=None):
        cp = rcopy(ref if src is None else src, ref, self.ss.at[k], self.rs.at[k], dev)
        cp.start()
        self.sent.append(cp)

    def mid_send(self, k, ref, j, rk, src=None):
        cp = rcopy(ref if src is None else src, ref, self.ss.at[k], self.rs.at[rk], self.h.dev(z=self.h.near(j)))
        pl.when(self.h.middle)(lambda: cp.start())
        self.mids.append(cp)

    def wait(self, k, ref):
        rcopy(ref, ref, self.ss.at[0], self.rs.at[k], self.h.sib()).wait_recv()

    def start(self):
        h = self.h
        self.local = pltpu.make_async_copy(self.own, self.all.at[h.z, h.y, h.x, h.c], self.lsem)
        self.local.start()
        me = self.head(h.z, h.y, h.x)
        own = self.own.at[pl.ds(0, self.cut)]
        self.send(8, me, h.xdev(), own)
        self.send(4, me, h.ydev(), own)
        self.send(0, me, h.dev(z=h.near(1)), own)
        self.mid_send(34, me, 2, 1, own)
        if self.split:
            self.send(24, self.tail(h.z, h.y, h.x), h.xdev(), self.own.at[pl.ds(self.cut, self.rows - self.cut)])

    def along_z(self, j):
        h = self.h
        part = self.head(h.near(j), h.y, h.x)
        self.wait(j - 1, part)
        if j == 1:
            self.mid_send(35, part, 2, 2)
        else:
            self.mid_send(34 + j, part, 1, j - 1)
        self.send(8 + j, part, h.xdev())
        self.send(4 + j, part, h.ydev())

    def along_y(self, j):
        h = self.h
        z = h.near(j)
        part = self.head(z, 1 - h.y, h.x)
        self.wait(4 + j, part)
        self.send(12 + j, part, h.xdev())
        self.send(16 + j, self.pair(z, h.x, h.c), h.sib())

    def along_x(self, j):
        h = self.h
        z = h.near(j)
        self.wait(8 + j, self.head(z, h.y, 1 - h.x))
        self.wait(12 + j, self.head(z, 1 - h.y, 1 - h.x))
        self.send(20 + j, self.pair(z, 1 - h.x, h.c), h.sib())

    def tail_x(self):
        h = self.h
        self.wait(24, self.tail(h.z, h.y, 1 - h.x))
        self.send(25, self.all.at[h.z, h.y, :, h.c, pl.ds(self.cut, self.rows - self.cut)], h.ydev())

    def tail_y(self):
        h = self.h
        self.wait(25, self.all.at[h.z, 1 - h.y, :, h.c, pl.ds(self.cut, self.rows - self.cut)])
        part = self.plane(h.z, h.c)
        self.send(26, part, h.dev(z=h.near(1)))
        self.mid_send(38, part, 2, 27)
        self.send(30, part, h.sib())

    def tail_z(self, j):
        h = self.h
        part = self.plane(h.near(j), h.c)
        self.wait(25 + j, part)
        if j == 1:
            self.mid_send(39, part, 2, 28)
        else:
            self.mid_send(38 + j, part, 1, 25 + j)
        self.send(30 + j, part, h.sib())

    def steps(self):
        p = functools.partial
        x, y, z = self.along_x, self.along_y, self.along_z
        tx, ty, tz = ([p(f)] if self.split else [] for f in (self.tail_x, self.tail_y, self.tail_z))
        order = [self.local.wait, p(y, 0), p(z, 1)] + tx + [p(x, 0), p(z, 2), p(y, 1)] + ty
        order += [p(z, 3), p(x, 1), p(y, 2)] + [p(f, 1) for f in tz] + [p(x, 2), p(y, 3)]
        return order + [p(f, j) for f in tz for j in (2, 3)] + [p(x, 3)]

    def finish(self):
        h = self.h
        c = 1 - h.c
        for j in range(4):
            z = h.near(j)
            self.wait(16 + j, self.pair(z, h.x, c))
            self.wait(20 + j, self.pair(z, 1 - h.x, c))
            if self.split:
                self.wait(30 + j, self.plane(z, c))

    def drain(self):
        for cp in self.mids:
            pl.when(self.h.middle)(lambda cp=cp: cp.wait_send())


class Scatter:
    def __init__(self, h, dw, l1, lxa, lya, lza, lzb, lyb, lxb, ss, rs, out, sent):
        self.h, self.dw, self.l1, self.lxa, self.lya = h, dw, l1, lxa, lya
        self.lza, self.lzb, self.lyb, self.lxb, self.ss, self.rs = lza, lzb, lyb, lxb, ss, rs
        self.out, self.sent = out, sent
        self.all = dw.reshape(4, 2, 2, 2, SHARD, C)
        self.head, self.tail = pl.ds(0, SUM_CUT), pl.ds(SUM_CUT, SHARD - SUM_CUT)

    def at(self, i, lo=0, n=SHARD):
        return self.dw.at[pl.ds(pl.multiple_of(i * SHARD + lo, 16), n)]

    def send(self, k, src, dst, dev):
        cp = rcopy(src, dst, self.ss.at[k], self.rs.at[k], dev)
        cp.start()
        self.sent.append(cp)

    def wait(self, k, land):
        rcopy(land, land, self.ss.at[0], self.rs.at[k], self.h.sib()).wait_recv()

    def add(self, i, lo, n, *parts):
        d = self.at(i, lo, n)
        total = d[...].astype(F32)
        for part in parts:
            total = total + part.astype(F32)
        d[...] = total.astype(BF)

    def s1(self, q):
        self.send(q, self.all.at[q, :, :, 1 - self.h.c], self.l1.at[q], self.h.sib())

    def _far(self, q):
        h = self.h
        return rcopy(
            self.all.at[q, :, :, h.c, self.tail], self.lzb.at[h.z], self.ss.at[16 + q], self.rs.at[20 + h.z], h.dev(z=q)
        )

    def s2(self, q):
        h = self.h
        self.wait(q, self.l1.at[q])
        for j in range(4):
            self.add(h.idx(q, j // 2, j % 2), 0, SHARD, self.l1[q, j // 2, j % 2])
        self.send(4 + q, self.all.at[q, :, 1 - h.x, h.c, self.head], self.lxa.at[q], h.xdev())
        pl.when(h.z != q)(lambda: self._far(q).start())

    def s3(self, q):
        h = self.h
        self.wait(4 + q, self.lxa.at[q])
        for j in range(2):
            self.add(h.idx(q, j), 0, SUM_CUT, self.lxa[q, j])
        self.send(8 + q, self.all.at[q, 1 - h.y, h.x, h.c, self.head], self.lya.at[q], h.ydev())

    def _near(self, q):
        h = self.h
        return rcopy(
            self.all.at[q, h.y, h.x, h.c, self.head], self.lza.at[h.z], self.ss.at[12 + q], self.rs.at[24 + h.z], h.dev(z=q)
        )

    def s4(self, q):
        h = self.h
        self.wait(8 + q, self.lya.at[q])
        self.add(h.idx(q), 0, SUM_CUT, self.lya[q])
        pl.when(h.z != q)(lambda: self._near(q).start())

    def t1(self):
        h = self.h
        for j in (1, 2, 3):
            self.wait(20 + h.near(j), self.lzb.at[h.near(j)])
        for j in range(4):
            parts = [self.lzb[h.near(k), j // 2, j % 2] for k in (1, 2, 3)]
            self.add(h.idx(None, j // 2, j % 2), SUM_CUT, SHARD - SUM_CUT, *parts)
        self.send(28, self.all.at[h.z, 1 - h.y, :, h.c, self.tail], self.lyb, h.ydev())

    def t2(self):
        h = self.h
        self.wait(28, self.lyb)
        for j in range(2):
            self.add(h.idx(None, None, j), SUM_CUT, SHARD - SUM_CUT, self.lyb[j])
        self.send(29, self.all.at[h.z, h.y, 1 - h.x, h.c, self.tail], self.lxb, h.xdev())

    def finish(self, extra):
        h = self.h
        self.wait(29, self.lxb)
        self.out[SUM_CUT:] = (
            self.at(h.idx(), SUM_CUT, SHARD - SUM_CUT)[...].astype(F32) + self.lxb[...].astype(F32) + extra[SUM_CUT:]
        )
        total = self.at(h.idx(), 0, SUM_CUT)[...].astype(F32) + extra[:SUM_CUT]
        for j in (1, 2, 3):
            self.wait(24 + h.near(j), self.lza.at[h.near(j)])
            total = total + self.lza[h.near(j)].astype(F32)
        self.out[:SUM_CUT] = total

    def drain(self):
        for q in range(4):

            @pl.when(self.h.z != q)
            def _(q=q):
                self._near(q).wait_send()
                self._far(q).wait_send()


class Halo:
    def __init__(self, h, edges, land, ss, rs):
        self.h, self.edges, self.land, self.ss, self.rs = h, edges, land, ss, rs
        self.up = rcopy(edges.at[0], land.at[1], ss.at[0], rs.at[0], h.dev(z=h.z - 1))
        self.down = rcopy(edges.at[1], land.at[0], ss.at[1], rs.at[1], h.dev(z=h.z + 1))

    def start_one(self, k):
        to = self.h.z + 2 * k - 1
        cp = rcopy(self.edges.at[k], self.land.at[1 - k], self.ss.at[k], self.rs.at[k], self.h.dev(z=to))
        pl.when((to >= 0) & (to <= 3))(lambda: cp.start())

    def start(self):
        pl.when(self.h.z > 0)(lambda: self.up.start())
        pl.when(self.h.z < 3)(lambda: self.down.start())

    def wait(self):
        @pl.when(self.h.z > 0)
        def _():
            self.up.wait_send()
            self.down.wait_recv()

        @pl.when(self.h.z < 3)
        def _():
            self.down.wait_send()
            self.up.wait_recv()


class Sums:
    def __init__(self, h, buf, ss, rs, sent):
        self.h, self.buf, self.ss, self.rs, self.sent = h, buf, ss, rs, sent

    def start_plane(self, payload):
        h = self.h
        self.own = payload
        mine = self.buf.at[2, 0]
        mine[...] = payload
        for r in (1, 2, 3):
            _, x, c = h.other(0, r // 2, r % 2)
            cp = rcopy(mine, self.buf.at[0, h.gy], self.ss.at[r - 1], self.rs.at[r - 1], h.dev(x=x, c=c))
            cp.start()
            self.sent.append(cp)

    def plane(self):
        h = self.h
        for r in (1, 2, 3):
            _, x, c = h.other(0, r // 2, r % 2)
            land = self.buf.at[0, x * 2 + c]
            rcopy(land, land, self.ss.at[0], self.rs.at[r - 1], h.sib()).wait_recv()
        return [jnp.where(h.gy == g, self.own, self.buf[0, g]) for g in range(4)]

    def start_z(self, payload):
        h = self.h
        self.own = payload
        mine = self.buf.at[2, 1]
        mine[...] = payload
        for j in (1, 2, 3):
            cp = rcopy(mine, self.buf.at[1, h.z], self.ss.at[2 + j], self.rs.at[3 + h.z], h.dev(z=h.near(j)))
            cp.start()
            self.sent.append(cp)

    def along_z(self):
        h = self.h
        for j in (1, 2, 3):
            land = self.buf.at[1, h.near(j)]
            rcopy(land, land, self.ss.at[0], self.rs.at[3 + h.near(j)], h.sib()).wait_recv()
        return [jnp.where(h.z == g, self.own, self.buf[1, g]) for g in range(4)]


def fold(row):
    return [row[:, 128 * k : 128 * (k + 1)] for k in range(4)]


def pack_rows(*rows):
    rows = rows + (jnp.zeros((1, C), F32),) * (4 - len(rows))
    return jnp.concatenate([part for r in rows for part in fold(r)], axis=0)


def unpack_rows(p):
    return [jnp.concatenate([p[4 * n + k : 4 * n + k + 1] for k in range(4)], axis=1) for n in range(p.shape[0] // 4)]


def column(r):
    return jnp.broadcast_to(r, (128, C)).T


def merge(parts, counts):
    total = sum(counts)
    mass = sum(parts[g][0:4] for g in range(4))
    mean = mass / jnp.maximum(total, 1.0)
    spread = jnp.zeros_like(mass)
    for g in range(4):
        n = jnp.maximum(counts[g], 1.0)
        gap = parts[g][0:4] / n - mean
        spread = spread + parts[g][4:8] + counts[g] * gap * gap
    third = parts[0] + parts[1] + parts[2] + parts[3]
    return jnp.concatenate([mass, spread, third[8:16]], axis=0)


def nn(a, b):
    return lax.dot_general(a, b, (((1,), (0,)), ((), ())), preferred_element_type=F32)


def nt(a, b):
    return lax.dot_general(a, b, (((1,), (1,)), ((), ())), preferred_element_type=F32)


def tn(a, b):
    return lax.dot_general(a, b, (((0,), (0,)), ((), ())), preferred_element_type=F32)


def sigmoid(u):
    return 1.0 / (1.0 + jnp.exp(-u))


def body(
    feat, w1s, w2s, gain, bias, head, hbias, labels, heights, widths, picks,
    pooled_out, fg_out, c1_out, c2_out, gg_out, bg_out, hg_out, hbg_out,
    w1, w2, x3, first, second, slope, dh, base, hid, dw,
    al, edges, bland, hland, sland, fland, fgs, fgl,
    e32, exts, ext, gb, stat, pacc, pz, pg, res, cot, yb, ht, gsc, mc1, mc2,
    l1, lxa, lya, lza, lzb, lyb, lxb,
    sem_g, rem_g, sem_ge, rem_ge, sem_l, sem_h, rem_h, sem_s, rem_s, sem_a, rem_a, sem_p, rem_p, sem_r, rem_r,
):
    h = Here()
    sent = []
    z, y = h.z, h.y

    barrier = pltpu.get_barrier_semaphore()
    peers = [h.dev(z=h.near(j)) for j in (1, 2, 3)]
    for r in range(1, 8):
        yy, xx, cc = h.other(r // 4, (r // 2) % 2, r % 2)
        peers.append(h.dev(y=yy, x=xx, c=cc))
    for dev in peers:
        pl.semaphore_signal(barrier, inc=1, device_id=dev, device_id_type=MESH)
    pl.semaphore_wait(barrier, len(peers))

    def swap_rows(lo, n, r, k):
        src = feat.at[pl.ds(PER * (1 - y) + lo, n), r]
        return rcopy(src, al.at[pl.ds(lo, n), r], sem_a.at[4 + k], rem_a.at[4 + k], h.ydev())

    swap = [swap_rows(0, 3, y, 0), swap_rows(3, 3, y, 1)] + [swap_rows(2 * k, 2, 1 - y, 2 + k) for k in range(3)]
    g1 = Gather(h, w1s, w1, sem_g.at[0], rem_g.at[0], sem_l.at[0], SHARD, CUT, sent)
    sent2 = []
    g2 = Gather(h, w2s, w2, sem_g.at[1], rem_g.at[1], sem_l.at[1], SHARD, CUT, sent2)
    ge = Gather(h, exts, ext, sem_ge, rem_ge, sem_l.at[2], 16, 16, sent)
    g1.start()
    swap[0].start()
    swap[1].start()
    e32[...] = jnp.zeros_like(e32)
    place = lax.broadcasted_iota(jnp.int32, (4, 128), 1) // 16
    both = jnp.concatenate([gain[...].astype(F32), bias[...].astype(F32)], axis=0)
    both = jnp.concatenate([both] * 8, axis=1)
    e32[0:4, 0:128] = jnp.where(place == lax.rem(h.idx(), 8), both, 0.0)
    e32[:, 256 : 256 + TASKS] = head[...].astype(F32)
    e32[0:12, 384 : 384 + TASKS] = labels[...].astype(F32)
    exts[...] = e32[...].astype(BF)
    ge.start()

    image = lax.broadcasted_iota(jnp.int32, (1, 8 * PER), 1)
    high = broad = jnp.zeros((1, 8 * PER), jnp.int32)
    for k in range(8 * PER):
        high = jnp.where(image == k, heights[k], high)
        broad = jnp.where(image == k, widths[k], broad)

    def pixels(zz, lo, n):
        here = (image >= lo) & (image < lo + n)
        cells = jnp.where(here, jnp.clip(high - ROWS * zz, 0, ROWS) * broad, 0).astype(F32)
        return cells.sum(1, keepdims=True)

    n_plane = [pixels(z, 2 * PER * g + PER * y, PER) for g in range(4)]
    n_z = [sum(pixels(zz, 2 * PER * g + PER * y, PER) for g in range(4)) for zz in range(4)]
    total = sum(n_z)
    my_first = h.gy * 2 * PER + PER * y

    col = lax.broadcasted_iota(jnp.int32, (COLS, C), 0)

    def wide(i, r):
        return jnp.where(ROWS * z + r < heights[my_first + i], widths[my_first + i], 0)

    def keep(i, r, v):
        return jnp.where(col < wide(i, r), v, 0.0)

    zero8 = jnp.zeros((8, C), F32)

    def by8(v):
        return v.reshape(COLS // 8, 8, C).sum(0)

    def put3(i, row, v):
        x3[i, row, :, C : 2 * C] = v.astype(BF)
        x3[i, row, :, 0:C] = jnp.where(col == 0, 0.0, pltpu.roll(v, 1, 0)).astype(BF)
        x3[i, row, :, 2 * C : 3 * C] = jnp.where(col == COLS - 1, 0.0, pltpu.roll(v, COLS - 1, 0)).astype(BF)

    def put_halo(land):
        def one(i, _):
            @pl.when(z > 0)
            def _():
                put3(i, 0, land[0, i].astype(F32))

            @pl.when(z == 0)
            def _():
                x3[i, 0] = jnp.zeros((COLS, 3 * C), BF)

            @pl.when(z < 3)
            def _():
                put3(i, 5, land[1, i].astype(F32))

            @pl.when(z == 3)
            def _():
                x3[i, 5] = jnp.zeros((COLS, 3 * C), BF)

            return 0

        lax.fori_loop(0, PER, one, 0)

    def take_row(src, offset, r, row, i, acc):
        v = keep(i, row, src[offset + i, r].astype(F32))
        base[i, row] = v.astype(BF)
        put3(i, row + 1, v)
        return acc + by8(v)

    def take_edge(k, src, offset, r, i, acc):
        acc = take_row(src, offset, r, 3 * k, i, acc)
        edges[k, i] = base[i, 3 * k]
        return acc

    halo = Halo(h, edges, bland, sem_h.at[0], rem_h.at[0])
    base_sum = lax.fori_loop(0, PER, lambda i, acc: take_edge(y, feat, PER * y, y, i, acc), zero8)
    halo.start_one(y)
    base_sum = lax.fori_loop(0, PER, lambda i, acc: take_row(feat, PER * y, 1 - y, 1 + y, i, acc), base_sum)

    def edges_in(k, acc):
        swap[k].wait_recv()
        return lax.fori_loop(3 * k, 3 * k + 3, lambda i, acc: take_edge(1 - y, al, 0, 1 - y, i, acc), acc)

    def rows_in(k, acc):
        swap[2 + k].wait_recv()
        return lax.fori_loop(2 * k, 2 * k + 2, lambda i, acc: take_row(al, 0, y, 2 - y, i, acc), acc)

    todo1, late = g1.steps(), 9
    todo2, todoe = [], ge.steps()
    for t, step in enumerate(todo1):
        step()
        if t >= 1 and todoe:
            todoe.pop(0)()
        if t in (2, 4, 6):
            swap[1 + t // 2].start()
        if t == late - 1:
            g2.start()
            todo2 = g2.steps()
        elif t >= late:
            todo2.pop(0)()
        if t == 5:
            base_sum = edges_in(0, base_sum)
        if t == 8:
            base_sum = edges_in(1, base_sum)
            halo.start_one(1 - y)
        if t in (10, 12, 14):
            base_sum = rows_in((t - 10) // 2, base_sum)
    base_sum = base_sum.sum(0, keepdims=True)
    g1.finish()
    steps = todo2
    def go(todo, n):
        for _ in range(min(n, len(todo))):
            todo.pop(0)()

    def conv(w, out, land, halo, todo=()):
        for p in range(3):
            im = pl.ds(2 * p, 2)
            mid = nn(x3[im, 1:5].reshape(8 * COLS, 3 * C), w[3 * C : 6 * C]).reshape(2, 4, COLS, C)
            lo = nn(x3[im, 1:4].reshape(6 * COLS, 3 * C), w[0 : 3 * C]).reshape(2, 3, COLS, C)
            hi = nn(x3[im, 2:5].reshape(6 * COLS, 3 * C), w[6 * C : 9 * C]).reshape(2, 3, COLS, C)
            out[im, 0] = mid[:, 0] + hi[:, 0]
            out[im, 1] = mid[:, 1] + lo[:, 0] + hi[:, 1]
            out[im, 2] = mid[:, 2] + lo[:, 1] + hi[:, 2]
            out[im, 3] = mid[:, 3] + lo[:, 2]
            go(todo, 1)
        halo.wait()
        go(todo, 1)
        put_halo(land)
        out[:, 0] += nn(x3[:, 0].reshape(6 * COLS, 3 * C), w[0 : 3 * C]).reshape(PER, COLS, C)
        out[:, 3] += nn(x3[:, 5].reshape(6 * COLS, 3 * C), w[6 * C : 9 * C]).reshape(PER, COLS, C)

    def conv_back(w, out, land, halo, todo=()):

        def taps(lhs, a):
            acc = None
            for b in range(3):
                part = nt(lhs[:, (2 - b) * C : (3 - b) * C], w[(3 * a + b) * C : (3 * a + b + 1) * C])
                acc = part if acc is None else acc + part
            return acc

        for p in range(3):
            im = pl.ds(2 * p, 2)
            mid = taps(x3[im, 1:5].reshape(8 * COLS, 3 * C), 1).reshape(2, 4, COLS, C)
            lo = taps(x3[im, 1:4].reshape(6 * COLS, 3 * C), 2).reshape(2, 3, COLS, C)
            hi = taps(x3[im, 2:5].reshape(6 * COLS, 3 * C), 0).reshape(2, 3, COLS, C)
            out[im, 0] = mid[:, 0] + hi[:, 0]
            out[im, 1] = mid[:, 1] + lo[:, 0] + hi[:, 1]
            out[im, 2] = mid[:, 2] + lo[:, 1] + hi[:, 2]
            out[im, 3] = mid[:, 3] + lo[:, 2]
            if todo:
                todo[p]()
        halo.wait()
        put_halo(land)
        if todo:
            todo[3]()
        out[:, 0] += taps(x3[:, 0].reshape(6 * COLS, 3 * C), 2).reshape(PER, COLS, C)
        out[:, 3] += taps(x3[:, 5].reshape(6 * COLS, 3 * C), 0).reshape(PER, COLS, C)

    def spread(src):
        def one(i, carry):
            n, mean, dev = carry
            widths_i = [wide(i, r) for r in range(ROWS)]
            ni = sum(widths_i).astype(F32)
            mass = jnp.zeros((8, C), F32)
            for r in range(ROWS):
                v = jnp.where(col < widths_i[r], src[i, r], 0.0)
                mass = mass + v.reshape(COLS // 8, 8, C).sum(0)
            mi = mass.sum(0, keepdims=True) / jnp.maximum(ni, 1.0)
            sq = jnp.zeros((8, C), F32)
            for r in range(ROWS):
                v = jnp.where(col < widths_i[r], src[i, r] - mi, 0.0)
                sq = sq + (v * v).reshape(COLS // 8, 8, C).sum(0)
            both = jnp.maximum(n + ni, 1.0)
            gap = mi - mean
            return (
                n + ni,
                mean + gap * (ni / both),
                dev + sq.sum(0, keepdims=True) + gap * gap * (n * ni / both),
            )

        zero = jnp.zeros((1, C), F32)
        n, mean, dev = lax.fori_loop(0, PER, one, (jnp.float32(0.0), zero, zero))
        return mean * n, dev

    def statistics(src, k, todo, inputs):
        ex = Sums(h, stat.at[k], sem_s.at[k], rem_s.at[k], sent)
        ex.start_plane(pack_rows(*spread(src), inputs))
        go(todo, 2)
        ex.start_z(merge(ex.plane(), n_plane))
        go(todo, 2)
        both = merge(ex.along_z(), n_z)
        mass, dev, inputs, _ = unpack_rows(both)
        return mass / total, lax.rsqrt(dev / total + norm_eps), inputs / total

    def start_sums(k, *rows):
        ex = Sums(h, stat.at[k], sem_s.at[k], rem_s.at[k], sent)
        ex.start_plane(pack_rows(*rows))
        return ex

    def mid_sums(ex):
        parts = ex.plane()
        ex.start_z(parts[0] + parts[1] + parts[2] + parts[3])

    def end_sums(ex):
        parts = ex.along_z()
        return parts[0] + parts[1] + parts[2] + parts[3]

    def edges_first(one, start):
        def edge(i, acc):
            for k, r in enumerate((0, ROWS - 1)):
                v = one(i, r)
                edges[k, i] = v.astype(BF)
                acc = acc + by8(v)
            return acc

        def inner(i, acc):
            for r in range(1, ROWS - 1):
                acc = acc + by8(one(i, r))
            return acc

        acc = lax.fori_loop(0, PER, edge, zero8)
        start()
        return lax.fori_loop(0, PER, inner, acc).sum(0, keepdims=True)

    conv(w1, first, bland, halo, steps)
    center, rs1, base_mean = statistics(first, 0, steps, base_sum)
    ge.finish()

    for k in range(4):
        tile = sum(ext[16 * d : 16 * d + 16, 0:128].astype(F32) for d in range(8 * k, 8 * k + 8))
        gb[0:4, 128 * k : 128 * (k + 1)] = tile[0:4]
    ht[...] = ext[:, 256:384].astype(F32)
    gain1, bias1 = gb[0:1], gb[2:3]

    def hidden(i, r):
        xh = (first[i, r] - center) * rs1
        first[i, r] = xh
        u = gain1 * xh + bias1
        v = keep(i, r, u * sigmoid(u))
        hid[i, r] = v.astype(BF)
        put3(i, r + 1, v)
        return v

    halo = Halo(h, edges, hland, sem_h.at[1], rem_h.at[1])
    def after_hidden():
        halo.start()
        go(steps, 2)

    hid_sum = edges_first(hidden, after_hidden)
    go(steps, 99)
    g2.finish()
    conv(w2, second, hland, halo, [])
    center, rs2, hid_mean = statistics(second, 1, [], hid_sum)
    gain2, bias2 = gb[1:2], gb[3:4]

    pacc[...] = jnp.zeros_like(pacc)

    def finals(i, _):
        acc = [jnp.zeros((8, C), F32) for _ in range(3)]
        for r in range(ROWS):
            xh = (second[i, r] - center) * rs2
            second[i, r] = xh
            pre = gain2 * xh + bias2 + base[i, r].astype(F32)
            s = sigmoid(pre)
            act = keep(i, r, pre * s)
            sl = keep(i, r, s * (1.0 + pre * (1.0 - s)))
            slope[i, r] = sl
            for k, v in enumerate((act, sl, sl * xh)):
                acc[k] = acc[k] + v.reshape(COLS // 8, 8, C).sum(0)
        for k in range(3):
            pacc[k, pl.ds(i, 1)] = acc[k].sum(0, keepdims=True)
        return 0

    lax.fori_loop(0, PER, finals, 0)

    rows8 = lax.broadcasted_iota(jnp.int32, (8, 1), 0)
    inv_pix = jnp.zeros((8, 1), F32)
    for i in range(PER):
        inv_pix = jnp.where(rows8 == i, 1.0 / (heights[my_first + i] * widths[my_first + i]).astype(F32), inv_pix)
    me_z = pz.at[z]
    me_z[...] = pacc[0]
    for j in (1, 2, 3):
        cp = rcopy(me_z, me_z, sem_p.at[j - 1], rem_p.at[z], h.dev(z=h.near(j)))
        cp.start()
        sent.append(cp)
    head_gram = lax.dot_general(ht[...], ht[...], (((0,), (0,)), ((), ())), precision=HIGH, preferred_element_type=F32)
    for j in (1, 2, 3):
        land = pz.at[h.near(j)]
        rcopy(land, land, sem_p.at[0], rem_p.at[h.near(j)], h.sib()).wait_recv()
    slot = (y * 2 + h.x) * 2 + h.c
    me_p = pg.at[slot]
    me_p[...] = (pz[0] + pz[1] + pz[2] + pz[3]) * inv_pix
    for r in range(1, 8):
        yy, xx, cc = h.other(r // 4, (r // 2) % 2, r % 2)
        cp = rcopy(me_p, me_p, sem_p.at[2 + r], rem_p.at[3 + r], h.dev(y=yy, x=xx, c=cc))
        cp.start()
        sent.append(cp)
    lane = lax.broadcasted_iota(jnp.int32, (8, 128), 1)
    row = lax.broadcasted_iota(jnp.int32, (8, 128), 0)
    real = (row < PER) & (lane < TASKS)
    wanted = []
    for s in range(8):
        yy, gy = s // 4, s % 4
        lab = ext[16 * gy : 16 * gy + 16, 384:512].astype(F32)
        lab = lab[PER * yy : PER * yy + PER]
        wanted.append(jnp.concatenate([lab, jnp.zeros((2, 128), F32)], axis=0))
    for r in range(1, 8):
        yy, xx, cc = h.other(r // 4, (r // 2) % 2, r % 2)
        land = pg.at[(yy * 2 + xx) * 2 + cc]
        rcopy(land, land, sem_p.at[0], rem_p.at[3 + r], h.sib()).wait_recv()
    pooled = pg[...].reshape(64, C)
    offset = jnp.concatenate([hbias[...].astype(F32), jnp.zeros((1, 128 - TASKS), F32)], axis=1)
    logits = lax.dot_general(pooled, ht[...], (((1,), (0,)), ((), ())), precision=HIGH, preferred_element_type=F32)
    logits = logits.reshape(8, 8, 128) + offset
    images = 8 * PER
    for s in range(8):
        res[s] = jnp.where(real, (sigmoid(logits[s]) - wanted[s]) / images, 0.0)
    residual = res[...].reshape(64, 128)
    gram = head_gram * lax.dot_general(
        residual, residual, (((0,), (0,)), ((), ())), precision=HIGH, preferred_element_type=F32
    )
    gram = gram[0:TASKS]
    lane1 = lax.broadcasted_iota(jnp.int32, (1, 128), 1)
    sub = lax.broadcasted_iota(jnp.int32, (TASKS, 128), 0)

    def fw(k, carry):
        mix, q = carry
        t = picks[k]
        one = (lane1 == t).astype(F32)
        line = jnp.where(sub == t, gram, 0.0).sum(0, keepdims=True)
        self_dot = (mix * q).sum(1, keepdims=True)
        cross = (one * q).sum(1, keepdims=True)
        vertex = (one * line).sum(1, keepdims=True)
        d = jnp.maximum(self_dot + vertex - 2.0 * cross, 0.1 * vertex)
        step = jnp.clip((self_dot - cross) / d, 0.0, 1.0)
        return (1.0 - step) * mix + step * one, (1.0 - step) * q + step * line

    mix0 = jnp.where(lane1 < TASKS, 1.0 / TASKS, 0.0)
    mix, _ = lax.fori_loop(0, STEPS, fw, (mix0, gram.sum(0, keepdims=True) / TASKS))
    mine = res[slot] * mix
    cot[...] = inv_pix * lax.dot_general(
        mine, ht[...], (((1,), (1,)), ((), ())), precision=HIGH, preferred_element_type=F32
    )
    ex = start_sums(
        2, (cot[...] * pacc[1]).sum(0, keepdims=True), (cot[...] * pacc[2]).sum(0, keepdims=True)
    )

    for yy in range(2):
        pooled_out[PER * yy : PER * (yy + 1)] = pg[(yy * 2 + h.x) * 2 + h.c][0:PER]
    head_grad = lax.dot_general(
        pooled, residual, (((0,), (0,)), ((), ())), precision=HIGH, preferred_element_type=F32
    )
    mid_sums(ex)
    gsc[...] = head_grad
    hg_out[...] = gsc[pl.ds(pl.multiple_of(h.idx() * 16, 16), 16)][:, 0:TASKS]
    hbg_out[...] = residual.sum(0, keepdims=True)[:, 0:TASKS]
    sums2 = end_sums(ex)
    yb[0, 0:8] = sums2[0:8]
    mc1[0:C] = column(base_mean)
    mc1[C:] = mc1[0:256]
    mc2[0:C] = column(hid_mean)
    mc2[C:] = mc2[0:256]
    yb[0, 24:32] = pack_rows(hid_mean, base_mean)[0:8]

    sum_b, sum_g, _, _ = unpack_rows(sums2)
    mean_b, mean_g = sum_b / total, sum_g / total
    scale = gain2 * rs2

    def d_second(i, r):
        xh = second[i, r]
        dp = slope[i, r] * cot[pl.ds(i, 1)]
        v = keep(i, r, scale * (dp - mean_b - xh * mean_g))
        put3(i, r + 1, v)
        return v.astype(BF).astype(F32)

    halo = Halo(h, edges, sland, sem_h.at[2], rem_h.at[2])
    d2_sum = edges_first(d_second, halo.start)
    conv_back(w2, dh, sland, halo)

    def d_norm1(i, carry):
        a, b = carry
        for r in range(ROWS):
            xh = first[i, r]
            u = gain1 * xh + bias1
            s = sigmoid(u)
            v = keep(i, r, dh[i, r] * (s * (1.0 + u * (1.0 - s))))
            dh[i, r] = v
            a = a + v.reshape(COLS // 8, 8, C).sum(0)
            b = b + (v * xh).reshape(COLS // 8, 8, C).sum(0)
        return a, b

    a, b = lax.fori_loop(0, PER, d_norm1, (zero8, zero8))
    ex = start_sums(3, a.sum(0, keepdims=True), b.sum(0, keepdims=True), d2_sum)

    def weight_taps(x, out, mean, d_sum, lo, hi):
        for t in range(lo, hi):
            ta, tb = t // 3, t % 3
            d = x3[:, 2 - ta : 6 - ta, :, (2 - tb) * C : (3 - tb) * C].reshape(PER * ROWS * COLS, C)
            part = tn(x[...].reshape(PER * ROWS * COLS, C), d)
            off = jnp.concatenate([mean[0:C] * f for f in fold(d_sum)], axis=1)
            out[t * C : (t + 1) * C] = (part - off).astype(BF)

    def scatter(k, src, out):
        return Scatter(
            h, src, l1.at[k], lxa.at[k], lya.at[k], lza.at[k], lzb.at[k], lyb.at[k], lxb.at[k], sem_r.at[k], rem_r.at[k],
            out, sent,
        )

    r2 = scatter(0, dw, c2_out)
    weight_taps(hid, dw, mc2, d2_sum, 0, 3)
    r2.s1(0)
    mid_sums(ex)
    weight_taps(hid, dw, mc2, d2_sum, 3, 5)
    r2.s1(1)
    r2.s2(0)
    weight_taps(hid, dw, mc2, d2_sum, 5, 7)
    r2.s1(2)
    r2.s2(1)
    weight_taps(hid, dw, mc2, d2_sum, 7, 9)
    r2.s1(3)
    r2.s2(2)
    sums1 = end_sums(ex)
    yb[0, 8:20] = sums1[0:12]
    sum_b, sum_g, _, _ = unpack_rows(sums1)
    mean_b1, mean_g1 = sum_b / total, sum_g / total
    scale1 = gain1 * rs1

    def d_first(i, r):
        v = keep(i, r, scale1 * (dh[i, r] - mean_b1 - first[i, r] * mean_g1))
        put3(i, r + 1, v)
        return v.astype(BF).astype(F32)

    halo = Halo(h, edges, fland, sem_h.at[3], rem_h.at[3])
    d1_sum = edges_first(d_first, halo.start)
    r2.s2(3)
    ex = start_sums(4, d1_sum)
    for cp in sent2:
        cp.wait_send()
    g2.drain()
    r1 = scatter(1, w2, c1_out)
    weight_taps(base, w2, mc1, d1_sum, 3, 6)

    def other_taps():
        weight_taps(base, w2, mc1, d1_sum, 0, 3)
        r1.s1(0)
        r1.s1(1)
        weight_taps(base, w2, mc1, d1_sum, 6, 7)
        r1.s1(2)
        weight_taps(base, w2, mc1, d1_sum, 7, 8)
        r1.s2(0)
        weight_taps(base, w2, mc1, d1_sum, 8, 9)
        r1.s1(3)
        r1.s2(1)

    conv_back(w1, dh, fland, halo, [functools.partial(r2.s3, q) for q in range(3)] + [other_taps])
    r1.s2(2)
    mid_sums(ex)
    r2.s4(0)

    def result(i, r):
        return keep(i, r, dh[i, r] + slope[i, r] * cot[pl.ds(i, 1)])

    back = []
    for i in range(PER):
        for r in range(2):
            fgs[i, r] = result(i, 2 * (1 - y) + r).astype(BF)
        back.append(rcopy(fgs.at[i], fgl.at[i], sem_a.at[9 + i], rem_a.at[9 + i], h.ydev()))
        if i < 3:
            back[i].start()

    r1.s2(3)
    r2.s3(3)
    r2.s4(1)
    yb[0, 20:24] = end_sums(ex)[0:4]
    ysum = rcopy(yb.at[0], yb.at[1], sem_a.at[0], rem_a.at[0], h.ydev())
    ysum.start()
    def stay(i, _):
        for r in range(2):
            fg_out[PER * y + i, r] = result(i, 2 * y + r).astype(BF)
        return 0

    lax.fori_loop(0, PER, stay, 0)
    r2.s4(2)
    r1.s3(0)
    r2.s4(3)
    r2.t1()
    r1.s3(1)
    back[3].start()
    r1.s4(0)

    ysum.wait_recv()
    sb2, sg2, sb1, sg1 = unpack_rows(yb[0, 0:16] + yb[1, 0:16])
    tile = jnp.zeros((4, 128), F32)
    for k in range(4):
        rows = [v[:, 128 * k : 128 * (k + 1)] for v in (sg1, sg2, sb1, sb2)]
        tile = jnp.where(lax.div(h.idx(), 8) == k, jnp.concatenate(rows, axis=0), tile)
    own = jnp.zeros((4, 16), F32)
    for k in range(8):
        own = jnp.where(lax.rem(h.idx(), 8) == k, tile[:, 16 * k : 16 * (k + 1)], own)
    gg_out[...] = own[0:2]
    bg_out[...] = own[2:4]

    r2.t2()

    at = pl.ds(pl.multiple_of(lax.rem(h.idx() * SHARD, C), 16), SHARD)
    d2_all, d1_all, hid_other, base_other = unpack_rows(yb[1, 16:32])
    d2_mine, d1_mine, _, _ = unpack_rows(yb[0, 16:32])

    def taken_off(mean, other, all_mine, all_other):
        off = jnp.concatenate([mean[at] * f for f in fold(all_mine)], axis=1)
        mean[0:C] = column(other)
        mean[C:] = mean[0:256]
        return off + jnp.concatenate([mean[at] * f for f in fold(all_other)], axis=1)

    off2 = taken_off(mc2, hid_other, d2_mine, d2_all)
    off1 = taken_off(mc1, base_other, d1_mine, d1_all)
    r2.finish(off2)

    def land_rows(i):
        back[i].wait_recv()
        fg_out[PER * (1 - y) + i] = fgl[i]

    land_rows(0)
    r1.s3(2)
    back[4].start()
    r1.s4(1)
    r1.t1()
    land_rows(1)
    r1.s3(3)
    back[5].start()
    r1.s4(2)
    r1.t2()
    land_rows(2)
    land_rows(3)
    land_rows(4)
    r1.s4(3)
    land_rows(5)
    r1.finish(off1)

    ysum.wait_send()
    g1.drain()
    ge.drain()
    for cp in swap + back + sent:
        cp.wait_send()
    r1.drain()
    r2.drain()


def fused(features, w1s, w2s, gain, bias, head, head_bias, labels, heights, widths, picks):
    vm = pl.BlockSpec(memory_space=pltpu.VMEM)
    sm = pl.BlockSpec(memory_space=pltpu.SMEM)
    V = pltpu.VMEM
    dma = pltpu.SemaphoreType.DMA
    maps = (PER, ROWS, COLS, C)
    edge = (2, PER, COLS, C)
    half = (PER, 2, COLS, C)
    scratch = [
        V((9 * C, C), BF), V((9 * C, C), BF), V((PER, ROWS + 2, COLS, 3 * C), BF),
        V(maps, F32), V(maps, F32), V(maps, F32), V(maps, F32), V(maps, BF), V(maps, BF), V((9 * C, C), BF),
        V(half, BF), V(edge, BF), V(edge, BF), V(edge, BF), V(edge, BF), V(edge, BF), V(half, BF), V(half, BF),
        V((16, C), F32), V((16, C), BF), V((C, C), BF), V((8, C), F32),
        V((5, 3, 4, 16, 128), F32), V((3, 8, C), F32), V((4, 8, C), F32), V((8, 8, C), F32),
        V((8, 8, 128), F32), V((8, C), F32), V((2, 32, 128), F32), V((C, 128), F32), V((C, 128), F32),
        V((C + 256, 128), F32), V((C + 256, 128), F32),
        V((2, 4, 2, 2, SHARD, C), BF), V((2, 4, 2, SUM_CUT, C), BF), V((2, 4, SUM_CUT, C), BF), V((2, 4, SUM_CUT, C), BF),
        V((2, 4, 2, 2, SHARD - SUM_CUT, C), BF), V((2, 2, SHARD - SUM_CUT, C), BF), V((2, SHARD - SUM_CUT, C), BF),
        dma((2, 48)), dma((2, 48)), dma((48,)), dma((48,)), dma((3,)), dma((4, 2)), dma((4, 2)),
        dma((5, 8)), dma((5, 8)), dma((15,)), dma((15,)), dma((12,)), dma((12,)), dma((2, 48)), dma((2, 48)),
    ]
    f = jax.ShapeDtypeStruct
    outs = pl.pallas_call(
        body,
        out_shape=[
            f((2 * PER, C), F32), f((2 * PER, 2, COLS, C), BF), f((SHARD, C), F32), f((SHARD, C), F32),
            f((2, 16), F32), f((2, 16), F32), f((16, TASKS), F32), f((1, TASKS), F32),
        ],
        in_specs=[vm] * 8 + [sm] * 3,
        out_specs=[vm] * 8,
        scratch_shapes=scratch,
        compiler_params=pltpu.CompilerParams(
            collective_id=0, has_side_effects=True, vmem_limit_bytes=63 * 2**20
        ),
        name="block",
    )(
        features, w1s, w2s, gain.T, bias.T, head, head_bias.reshape(1, TASKS), labels, heights, widths, picks,
    )
    pooled, fg, c1, c2, gg, bg, hg, hbg = outs
    return pooled, fg.astype(F32), c1, c2, gg.T, bg.T, hg, hbg.reshape(TASKS)


def extended(cells, sides, width):
    for axis, dim in sides:
        count = lax.axis_size(axis)
        ends = count - 1
        head = lax.slice_in_dim(cells, 0, width, axis=dim)
        tail = lax.slice_in_dim(cells, cells.shape[dim] - width, cells.shape[dim], axis=dim)
        cells = jnp.concatenate(
            [
                lax.ppermute(tail, axis, [(i, (i + 1) % count) for i in range(ends)]),
                cells,
                lax.ppermute(head, axis, [((i + 1) % count, i) for i in range(ends)]),
            ],
            axis=dim,
        )
    return cells


def make_patches(padded, row_count, col_count):
    widened = jnp.pad(padded, ((0, 0), (0, 0), (1, 1), (0, 0)))
    pieces = [
        widened[:, row_off : row_off + row_count, col_off : col_off + col_count, :]
        for row_off in range(3)
        for col_off in range(3)
    ]
    joined = jnp.concatenate(pieces, axis=-1)
    return joined.reshape(-1, joined.shape[-1])


def conv_rows(act, weight):
    padded = extended(act, (("gx", 1),), 1)
    patches = make_patches(padded, act.shape[1], act.shape[2])
    output = jnp.dot(patches, weight, preferred_element_type=jnp.float32)
    return (output.reshape(act.shape[:3] + (weight.shape[1],)), padded)


def reversed_taps(weight):
    channels = weight.shape[1]
    taps = weight.reshape(9, channels, channels)[::-1]
    return jnp.transpose(taps, (0, 2, 1)).reshape(9 * channels, channels)


def weight_term(padded, grad_bf):
    patches = make_patches(padded, grad_bf.shape[1], grad_bf.shape[2])
    flat_grad = grad_bf.reshape(-1, grad_bf.shape[-1])
    return lax.dot_general(
        patches, flat_grad, (((0,), (0,)), ((), ())), preferred_element_type=jnp.float32
    )


def batch_statistics(values, inner_result, pixel_total):
    center_val = (
        lax.psum(jnp.sum(values * inner_result, axis=(0, 1, 2)), ("gx", "gy")) / pixel_total
    )
    centered = values - center_val
    spread_sq = (
        lax.psum(jnp.sum(inner_result * centered * centered, axis=(0, 1, 2)), ("gx", "gy"))
        / pixel_total
    )
    inverse_scale = lax.rsqrt(spread_sq + norm_eps)
    return (centered * inverse_scale, inverse_scale)


def norm_backward(
    output_gradient, normalized_input, inverse_scale, norm_scale_factor, inner_result, pixel_total
):
    bias_gradient_total, scale_gradient_total = lax.psum(
        (
            jnp.sum(output_gradient, axis=(0, 1, 2)),
            jnp.sum(output_gradient * normalized_input, axis=(0, 1, 2)),
        ),
        ("gx", "gy"),
    )
    backward_result = (
        norm_scale_factor
        * inverse_scale
        * (
            output_gradient
            - bias_gradient_total / pixel_total
            - normalized_input * scale_gradient_total / pixel_total
        )
        * inner_result
    )
    return (backward_result, scale_gradient_total, bias_gradient_total)


def silu_slope(values):
    sig_val = jax.nn.sigmoid(values)
    return sig_val * (1.0 + values * (1.0 - sig_val))


def frank_wolfe(gram, picks):
    task_ids = jnp.arange(TASKS)

    def fw_step(index, task_mix):
        onehot = (task_ids == picks[index]).astype(jnp.float32)
        mixed_vec = jnp.dot(gram, task_mix, precision=lax.Precision.HIGHEST)
        self_dot = jnp.sum(task_mix * mixed_vec)
        cross_dot = jnp.sum(onehot * mixed_vec)
        vertex_dot = jnp.sum(onehot * jnp.dot(gram, onehot, precision=lax.Precision.HIGHEST))
        distance = jnp.maximum(self_dot + vertex_dot - 2.0 * cross_dot, 0.1 * vertex_dot)
        step_size = jnp.clip((self_dot - cross_dot) / distance, 0.0, 1.0)
        return (1.0 - step_size) * task_mix + step_size * onehot

    start = jnp.full((TASKS,), 1.0 / TASKS, jnp.float32)
    return lax.fori_loop(0, STEPS, fw_step, start)


def on_device(
    features,
    conv1_weight,
    conv2_weight,
    norm_gain,
    norm_bias,
    head_weight,
    head_bias,
    labels,
    heights,
    widths,
    picks,
):
    image_count, row_count, col_count, channels = features.shape
    per_micro = image_count // MICRO
    total_images = image_count * lax.axis_size("gy")
    row_ids = lax.axis_index("gx") * row_count + jnp.arange(row_count)
    my_heights = lax.dynamic_slice_in_dim(heights, lax.axis_index("gy") * image_count, image_count)
    my_widths = lax.dynamic_slice_in_dim(widths, lax.axis_index("gy") * image_count, image_count)
    inside_all = (
        (row_ids[None, :, None] < my_heights[:, None, None])
        & (jnp.arange(col_count)[None, None, :] < my_widths[:, None, None])
    ).astype(jnp.float32)[..., None]
    pixel_count = (my_heights * my_widths).astype(jnp.float32)
    micro_pixels = jnp.sum((heights * widths).reshape(-1, MICRO, per_micro), axis=(0, 2)).astype(
        jnp.float32
    )

    def weights_now():
        return (
            lax.all_gather(conv1_weight, ("gx", "gy"), axis=0, tiled=True),
            lax.all_gather(conv2_weight, ("gx", "gy"), axis=0, tiled=True),
            lax.all_gather(norm_gain, ("gx", "gy"), axis=0, tiled=True),
            lax.all_gather(norm_bias, ("gx", "gy"), axis=0, tiled=True),
            lax.all_gather(head_weight, ("gx", "gy"), axis=0, tiled=True),
        )

    saved = []
    pooled_parts = []
    head_full = None
    for index in range(MICRO):
        conv_one, conv_two, gain_full, bias_full, head_full = weights_now()
        scale_factors = gain_full.astype(jnp.float32)
        bias_values = bias_full.astype(jnp.float32)
        inner_result = inside_all[index * per_micro : (index + 1) * per_micro]
        pixel_total = micro_pixels[index]
        base_input_bfloat = features[
            index * per_micro : (index + 1) * per_micro
        ] * inner_result.astype(jnp.bfloat16)
        first_convolution, padded_input = conv_rows(base_input_bfloat, conv_one)
        first_normalized, first_scale = batch_statistics(
            first_convolution, inner_result, pixel_total
        )
        first_norm_output = scale_factors[:, 0] * first_normalized + bias_values[:, 0]
        hidden_bf = (jax.nn.silu(first_norm_output) * inner_result).astype(jnp.bfloat16)
        second_convolution, padded_hidden_state = conv_rows(hidden_bf, conv_two)
        second_normalized, second_scale = batch_statistics(
            second_convolution, inner_result, pixel_total
        )
        before_activation = (
            scale_factors[:, 1] * second_normalized
            + bias_values[:, 1]
            + base_input_bfloat.astype(jnp.float32)
        )
        final_act = jax.nn.silu(before_activation) * inner_result
        pooled_parts.append(jnp.sum(final_act, axis=(1, 2)))
        saved.append(
            (
                padded_input,
                padded_hidden_state,
                first_normalized,
                first_scale,
                first_norm_output,
                second_normalized,
                second_scale,
                before_activation,
            )
        )
    pooled = lax.psum(jnp.concatenate(pooled_parts, axis=0), "gx") / pixel_count[:, None]
    head_mat = head_full.astype(jnp.float32)
    logits = jnp.dot(pooled, head_mat, precision=lax.Precision.HIGHEST) + head_bias.astype(
        jnp.float32
    )
    residual = (jax.nn.sigmoid(logits) - labels.astype(jnp.float32)) / total_images
    gram_part = jnp.dot(residual.T, residual, precision=lax.Precision.HIGHEST)
    head_part = jnp.dot(pooled.T, residual, precision=lax.Precision.HIGHEST)
    gram_sum, head_bias_grad, head_total = (
        lax.psum(gram_part.astype(jnp.bfloat16), "gy").astype(jnp.float32),
        lax.psum(jnp.sum(residual, axis=0).astype(jnp.bfloat16), "gy").astype(jnp.float32),
        lax.psum(head_part.astype(jnp.bfloat16), "gy").astype(jnp.float32),
    )
    gram = gram_sum * jnp.dot(head_mat.T, head_mat, precision=lax.Precision.HIGHEST)
    task_mix = frank_wolfe(gram, picks)
    pooled_cot = jnp.dot(residual * task_mix, head_mat.T, precision=lax.Precision.HIGHEST)
    shard_rows = 9 * channels // lax.axis_size(("gx", "gy"))
    conv1_grad = jnp.zeros((shard_rows, channels), jnp.float32)
    conv2_grad = jnp.zeros((shard_rows, channels), jnp.float32)
    gain_total = jnp.zeros((channels, 2), jnp.float32)
    bias_total = jnp.zeros((channels, 2), jnp.float32)
    feat_parts = []
    for index in range(MICRO):
        conv_one, conv_two, gain_full, bias_full, unused_heads = weights_now()
        scale_factors = gain_full.astype(jnp.float32)
        (
            padded_input,
            padded_hidden_state,
            first_normalized,
            first_scale,
            first_norm_output,
            second_normalized,
            second_scale,
            before_activation,
        ) = saved[index]
        inner_result = inside_all[index * per_micro : (index + 1) * per_micro]
        pixel_total = micro_pixels[index]
        cot_part = (
            pooled_cot[index * per_micro : (index + 1) * per_micro]
            / pixel_count[index * per_micro : (index + 1) * per_micro, None]
        )
        gradient_before_relu = (
            cot_part[:, None, None, :] * inner_result * silu_slope(before_activation)
        )
        d_second, gain_two, bias_two = norm_backward(
            gradient_before_relu,
            second_normalized,
            second_scale,
            scale_factors[:, 1],
            inner_result,
            pixel_total,
        )
        second_bf = d_second.astype(jnp.bfloat16)
        term_two = weight_term(padded_hidden_state, second_bf)
        d_hidden, unused_pad = conv_rows(second_bf, reversed_taps(conv_two))
        gradient_norm_first = d_hidden * inner_result * silu_slope(first_norm_output)
        d_first, gain_one, bias_one = norm_backward(
            gradient_norm_first,
            first_normalized,
            first_scale,
            scale_factors[:, 0],
            inner_result,
            pixel_total,
        )
        first_bf = d_first.astype(jnp.bfloat16)
        term_one = weight_term(padded_input, first_bf)
        d_base, unused_pad_two = conv_rows(first_bf, reversed_taps(conv_one))
        feat_parts.append((d_base + gradient_before_relu) * inner_result)
        gain_total = gain_total + jnp.stack([gain_one, gain_two], axis=1)
        bias_total = bias_total + jnp.stack([bias_one, bias_two], axis=1)
        shard_one, shard_two = (
            lax.psum_scatter(term_one, ("gx", "gy"), scatter_dimension=0, tiled=True),
            lax.psum_scatter(term_two, ("gx", "gy"), scatter_dimension=0, tiled=True),
        )
        conv1_grad = conv1_grad + shard_one
        conv2_grad = conv2_grad + shard_two
    flat_index = lax.axis_index(("gx", "gy"))
    chan_rows = channels // lax.axis_size(("gx", "gy"))
    gain_grad = lax.dynamic_slice_in_dim(gain_total, flat_index * chan_rows, chan_rows, 0)
    bias_grad = lax.dynamic_slice_in_dim(bias_total, flat_index * chan_rows, chan_rows, 0)
    head_grad = lax.dynamic_slice_in_dim(head_total, flat_index * chan_rows, chan_rows, 0)
    features_grad = jnp.concatenate(feat_parts, axis=0)
    return (
        pooled,
        features_grad,
        conv1_grad,
        conv2_grad,
        gain_grad,
        bias_grad,
        head_grad,
        head_bias_grad,
    )


def solution(mesh):
    in_specs = (
        P("gy", "gx", None, None),
        P(("gx", "gy"), None),
        P(("gx", "gy"), None),
        P(("gx", "gy"), None),
        P(("gx", "gy"), None),
        P(("gx", "gy"), None),
        P(),
        P("gy", None),
        P(),
        P(),
        P(),
    )
    out_specs = (
        P("gy", None),
        P("gy", "gx", None, None),
        P(("gx", "gy"), None),
        P(("gx", "gy"), None),
        P(("gx", "gy"), None),
        P(("gx", "gy"), None),
        P(("gx", "gy"), None),
        P(),
    )
    whole = dict(mesh.shape) != {"gx": 8, "gy": 4}
    return jax.shard_map(
        on_device if whole else fused, mesh=mesh, in_specs=in_specs, out_specs=out_specs, check_vma=False
    )
```
